256 devices in a mesh: gx: 8 (over z), gy: 4 (over x), gz: 8 (over y, core).
Axes of the slice: x: 4, y: 4, z: 8, core: 2. Of those that a mesh axis runs over, the one named last changes fastest.
Arguments:
- pressure: float32 [16384, 512], P(('gx', 'gy', 'gz')), may hold values from -6 to 6
- rhs: float32 [16384, 512], P(('gx', 'gy', 'gz')), may hold values from -6 to 6
- jacobi: float32 [16384, 512], P(('gx', 'gy', 'gz')), may hold values from 0.05 to 0.5
- geom: float32 [3, 16384, 512], P(None, ('gx', 'gy', 'gz')), may hold values from 0.005 to 0.05
- velocity: float32 [3, 16384, 512], P(None, ('gx', 'gy', 'gz')), may hold values from -6 to 6
- force: float32 [3, 16384, 512], P(None, ('gx', 'gy', 'gz')), may hold values from -6 to 6
- mass: float32 [16384, 512], P(('gx', 'gy', 'gz')), may hold values from 0.2 to 2
- metric: float32 [3, 16384], P(None, ('gx', 'gy', 'gz')), may hold values from 0.05 to 0.5
- conn: int32 [16384, 512], P(('gx', 'gy', 'gz')), may hold values from 0 to 25991, as said below
- ent_peer: int32 [256, 8192], P(('gx', 'gy', 'gz')), may hold values from 0 to 31, as said below
- ent_slot: int32 [256, 8192], P(('gx', 'gy', 'gz')), may hold values from 0 to 255
- ent_node: int32 [256, 8192], P(('gx', 'gy', 'gz')), may hold values from 0 to 25991, as said below
- counts: int32 [256, 32], P(('gx', 'gy', 'gz')), may hold values from 0 to 256, as said below
- axial_nodes: int32 [256, 2, 2048], P(('gx', 'gy', 'gz')), may hold values from 0 to 25991, as said below
Outputs:
- new_pressure: float32 [16384, 512], P(('gx', 'gy', 'gz'))
- momentum_residual: float32 [3, 16384, 512], P(None, ('gx', 'gy', 'gz'))
The draws below stay inside these ranges and needn't reach their ends.
Inputs may be any that keep to these rules, and one draw needn't show every extreme that they name: `conn`: each device's elements form a brick of 8 x 8 x 1 elements in some order, with nodes 0 to 25991 numbered in some order; every element point has one node. The pairs (ent_peer, ent_slot) of one device are all different. `ent_node`: each entry's node lies on the side of the device's brick (first or last node along its first or second direction); several entries may name the same node. counts is symmetric between two ranks of one slab and 0 towards a device's own rank; a nonzero count is 128 or more; each slab has a pair with 256. `axial_nodes`: the lower list (0) holds different nodes of the brick's first node layer along its third direction, the upper list (1) different nodes of its last layer; slot k of a device's upper list pairs with slot k of the lower list of the same rank in the next slab.
All inputs are finite; a program needn't handle non-finite values.
Results may differ from the reference program's by a relative error of at most 0.0001.
Values sent between devices are 32-bit elements; how exact they have to be, the bound alone decides.
No kernel may reach another device: no remote copies, remote signals or barrier semaphores. Data moves between devices by JAX's collectives and lax.ppermute only.
A program may use at most 128 MiB of HBM per device.

```python
import math
import jax
import jax.numpy as jnp
import numpy as np
from jax import lax

BX = 8
BY = 8
BZ = 1
AXIAL = 2048
E_DEV = 64
NODES = 25992
SLOTS = 256
RANKS = 32
SLABS = 8
DEVS = 256
ENTRIES = 8192
ELEMS = 16384


def entry_order(key):
    key = jax.random.fold_in(key, 101)
    keys = jax.random.split(key, DEVS)
    return jax.vmap(lambda single: jax.random.permutation(single, ENTRIES))(keys).astype(jnp.int32)


def node_layout(key):
    key = jax.random.fold_in(key, 303)
    keys = jax.random.split(key, DEVS)
    return jax.vmap(lambda single: jax.random.permutation(single, NODES))(keys).astype(jnp.int32)


def side_positions():
    extent_x = 7 * BX + 1
    extent_y = 7 * BY + 1
    extent_z = 7 * BZ + 1
    grid_x, grid_y, grid_z = np.meshgrid(np.arange(extent_x), np.arange(extent_y), np.arange(extent_z), indexing='ij')
    linear = (grid_x * extent_y + grid_y) * extent_z + grid_z
    onside = (grid_x == 0) | (grid_x == extent_x - 1) | (grid_y == 0) | (grid_y == extent_y - 1)
    return jnp.asarray(linear[onside].reshape(-1), jnp.int32)


def draw_conn(key, part):
    order = node_layout(key)
    key = jax.random.fold_in(key, 11)
    keys = jax.random.split(key, DEVS)

    def per_device(single, node_order):
        elem_order = jax.random.permutation(single, E_DEV).astype(jnp.int32)
        brick = elem_order[:, None]
        point = jnp.arange(512, dtype=jnp.int32)[None, :]
        coord_x = 7 * (brick // (BY * BZ)) + point // 64
        coord_y = 7 * (brick // BZ % BY) + point // 8 % 8
        coord_z = 7 * (brick % BZ) + point % 8
        linear = (coord_x * (7 * BY + 1) + coord_y) * (7 * BZ + 1) + coord_z
        return node_order[linear]
    return jax.vmap(per_device)(keys, order).reshape(ELEMS, 512).astype(jnp.int32)


def draw_ent_peer(key, part):
    base = entry_order(key)
    return (base // SLOTS).astype(jnp.int32)


def draw_ent_slot(key, part):
    base = entry_order(key)
    return (base % SLOTS).astype(jnp.int32)


def draw_ent_node(key, part):
    order = node_layout(key)
    key = jax.random.fold_in(key, 21)
    sides = side_positions()
    picks = jax.random.randint(key, (DEVS, ENTRIES), 0, sides.shape[0])
    positions = sides[picks]
    return jnp.take_along_axis(order, positions, axis=1).astype(jnp.int32)


def draw_axial_nodes(key, part):
    order = node_layout(key)
    key = jax.random.fold_in(key, 31)
    keys = jax.random.split(key, DEVS)
    face_count = (7 * BX + 1) * (7 * BY + 1)
    extent_z = 7 * BZ + 1

    def per_device(single, node_order):
        key_low, key_high = jax.random.split(single)
        low_face = jax.random.permutation(key_low, face_count)[:AXIAL].astype(jnp.int32)
        high_face = jax.random.permutation(key_high, face_count)[:AXIAL].astype(jnp.int32)
        low_pos = low_face * extent_z
        high_pos = high_face * extent_z + (extent_z - 1)
        return jnp.stack([node_order[low_pos], node_order[high_pos]], axis=0)
    return jax.vmap(per_device)(keys, order).astype(jnp.int32)


def draw_counts(key, part):
    key = jax.random.fold_in(key, 15)
    key_adj, key_amount, key_first, key_second = jax.random.split(key, 4)
    adjacent = jax.random.randint(key_adj, (SLABS, RANKS, RANKS), 0, 2)
    amount = jax.random.randint(key_amount, (SLABS, RANKS, RANKS), SLOTS // 2, SLOTS + 1)
    upper_part = adjacent * amount
    row_index = jnp.arange(RANKS, dtype=jnp.int32)[:, None]
    col_index = jnp.arange(RANKS, dtype=jnp.int32)[None, :]
    mirrored = jnp.swapaxes(upper_part, 1, 2)
    table = jnp.where(row_index < col_index, upper_part, jnp.where(row_index > col_index, mirrored, 0))
    first = jax.random.randint(key_first, (SLABS,), 0, RANKS)
    second = (first + jax.random.randint(key_second, (SLABS,), 1, RANKS)) % RANKS
    hit = (row_index == first[:, None, None]) & (col_index == second[:, None, None]) | (row_index == second[:, None, None]) & (col_index == first[:, None, None])
    table = jnp.where(hit, SLOTS, table)
    return table.reshape(DEVS, RANKS).astype(jnp.int32)


def block_scale(rng, extent, cuts, least, high):
    gain = 1.0
    for axis_at, parts in cuts:
        draws = jax.random.uniform(jax.random.fold_in(jax.random.fold_in(rng, 6), axis_at), (parts,), jnp.float32, least / len(cuts), high / len(cuts))
        gain = gain * jnp.repeat(jnp.exp(draws), extent[axis_at] // parts).reshape((-1,) + (1,) * (len(extent) - 1 - axis_at))
    return gain


def noise(own_key, extent, scale, reach, pieces=(), held_as=jnp.bfloat16):
    values = scale * jax.random.normal(own_key, extent, jnp.float32)
    if pieces:
        values = values * block_scale(own_key, extent, pieces, -0.22, 0.18)
    return jnp.clip(values, -reach, reach).astype(held_as)


def setup_inputs(seed: int = 0) -> dict:
    splits = jax.random.split(jax.random.key(seed), 15)
    return {
        "pressure": noise(splits[0], (ELEMS, 512), 1.0, 6.0, ((0, 256),), jnp.float32),
        "rhs": noise(splits[1], (ELEMS, 512), 1.0, 6.0, ((0, 256),), jnp.float32),
        "jacobi": jnp.clip(jnp.exp(math.log(0.5) - 2.3025851 * jax.random.uniform(splits[2], (ELEMS, 512), jnp.float32) ** block_scale(splits[2], (ELEMS, 512), ((0, 256),), -0.2, 0.2)), 0.05, 0.5),
        "geom": jnp.clip(jnp.exp(math.log(0.05) - 2.3025851 * jax.random.uniform(splits[3], (3, ELEMS, 512), jnp.float32) ** block_scale(splits[3], (3, ELEMS, 512), ((1, 256),), -0.2, 0.2)), 0.005, 0.05),
        "velocity": noise(splits[4], (3, ELEMS, 512), 1.0, 6.0, ((1, 256),), jnp.float32),
        "force": noise(splits[5], (3, ELEMS, 512), 1.0, 6.0, ((1, 256),), jnp.float32),
        "mass": jnp.clip(jnp.exp(math.log(2.0) - 2.3025851 * jax.random.uniform(splits[6], (ELEMS, 512), jnp.float32) ** block_scale(splits[6], (ELEMS, 512), ((0, 256),), -0.2, 0.2)), 0.2, 2.0),
        "metric": jnp.clip(jnp.exp(math.log(0.5) - 2.3025851 * jax.random.uniform(splits[7], (3, ELEMS), jnp.float32) ** block_scale(splits[7], (3, ELEMS), ((1, 256),), -0.2, 0.2)), 0.05, 0.5),
        "conn": draw_conn(jax.random.fold_in(splits[14], 71), 0),
        "ent_peer": draw_ent_peer(jax.random.fold_in(splits[14], 71), 0),
        "ent_slot": draw_ent_slot(jax.random.fold_in(splits[14], 71), 0),
        "ent_node": draw_ent_node(jax.random.fold_in(splits[14], 71), 0),
        "counts": draw_counts(jax.random.fold_in(splits[14], 71), 0),
        "axial_nodes": draw_axial_nodes(jax.random.fold_in(splits[14], 71), 0),
    }


VISCOSITY = 0.2
CHEB_THETA = 1.1
CHEB_DELTA = 0.9
RHO_FIRST = 9.0 / 11.0
RHO_NEXT = 99.0 / 161.0


def deriv_table():
    points = np.array([-1.0, -0.8717401485096066, -0.5917001814331423, -0.2092992179024789,
                       0.2092992179024789, 0.5917001814331423, 0.8717401485096066, 1.0])
    before = np.ones(8)
    legendre = points.copy()
    for degree in range(1, 7):
        after = ((2 * degree + 1) * points * legendre - degree * before) / (degree + 1)
        before = legendre
        legendre = after
    spread = points[:, None] - points[None, :]
    safe = np.where(spread == 0.0, 1.0, spread)
    deriv = legendre[:, None] / (legendre[None, :] * safe)
    deriv = np.where(spread == 0.0, 0.0, deriv)
    deriv[0, 0] = -14.0
    deriv[7, 7] = 14.0
    return deriv


def kron_tables():
    deriv = deriv_table()
    eye_one = np.eye(8)
    eye_two = np.eye(64)
    first_dir = np.kron(deriv, eye_two)
    second_dir = np.kron(eye_one, np.kron(deriv, eye_one))
    third_dir = np.kron(eye_two, deriv)
    return [jnp.asarray(table, jnp.float32) for table in (first_dir, second_dir, third_dir)]


def forward(field, table):
    return jnp.matmul(field, table.T, precision=lax.Precision.HIGHEST)


def backward(field, table):
    return jnp.matmul(field, table, precision=lax.Precision.HIGHEST)


def laplace(field, geom, tables):
    result = jnp.zeros_like(field)
    for axis in range(3):
        result = result + backward(geom[axis] * forward(field, tables[axis]), tables[axis])
    return result


def momentum_terms(velocity, force, mass, metric, geom, tables):
    convect = jnp.zeros_like(velocity)
    diffuse = jnp.zeros_like(velocity)
    for axis in range(3):
        grad = forward(velocity, tables[axis])
        convect = convect + (metric[axis][:, None] * velocity[axis]) * grad
        diffuse = diffuse + backward(geom[axis] * grad, tables[axis])
    return mass * (force - convect) - VISCOSITY * diffuse


def reference(pressure, rhs, jacobi, geom, velocity, force, mass, metric, conn, ent_peer, ent_slot, ent_node, counts, axial_nodes):
    tables = kron_tables()
    device_ids = jnp.arange(DEVS, dtype=jnp.int32)
    global_ids = (conn.reshape(DEVS, E_DEV * 512) + device_ids[:, None] * NODES).reshape(-1).astype(jnp.int32)
    limit = jnp.take_along_axis(counts, ent_peer, axis=1)
    valid = (ent_slot < limit).astype(jnp.float32)
    rows = jnp.broadcast_to(device_ids[:, None], ent_peer.shape)
    source = (device_ids // RANKS)[:, None] * RANKS + ent_peer
    own_rank = jnp.broadcast_to((device_ids % RANKS)[:, None], ent_peer.shape)
    slab = device_ids // RANKS
    rank = device_ids % RANKS
    lower = ((slab - 1) % SLABS) * RANKS + rank
    upper = ((slab + 1) % SLABS) * RANKS + rank

    def assemble(stack):
        width = stack.shape[0]
        local = jax.vmap(lambda row: jax.ops.segment_sum(row, global_ids, num_segments=DEVS * NODES))(stack.reshape(width, -1))
        local = local.reshape(width, DEVS, NODES)
        sent = local[:, rows, ent_node] * valid
        message = jnp.zeros((width, DEVS, RANKS, SLOTS), jnp.float32).at[:, rows, ent_peer, ent_slot].set(sent)
        received = message[:, source, own_rank, ent_slot] * valid
        rims = local[:, device_ids[:, None, None], axial_nodes]
        from_lower = rims[:, lower, 1]
        from_upper = rims[:, upper, 0]
        total = local.at[:, rows, ent_node].add(received)
        total = total.at[:, device_ids[:, None], axial_nodes[:, 0]].add(from_lower)
        total = total.at[:, device_ids[:, None], axial_nodes[:, 1]].add(from_upper)
        return total.reshape(width, -1)[:, global_ids].reshape(stack.shape)

    start_res = rhs - assemble(laplace(pressure, geom, tables)[None])[0]
    step_first = jacobi * start_res / CHEB_THETA
    first = pressure + step_first
    next_res = start_res - assemble(laplace(step_first, geom, tables)[None])[0]
    step_next = (RHO_NEXT * RHO_FIRST) * step_first + (2.0 * RHO_NEXT / CHEB_DELTA) * jacobi * next_res
    new_pressure = first + step_next
    momentum_residual = assemble(momentum_terms(velocity, force, mass, metric, geom, tables))
    return new_pressure, momentum_residual
```

```python
import jax
import jax.numpy as jnp
import ml_dtypes
import numpy as np
from jax import lax
from jax.experimental import pallas as pl
from jax.experimental.pallas import tpu as pltpu
from jax.sharding import PartitionSpec as P

F32 = jnp.float32
BF16 = jnp.bfloat16
I32 = jnp.int32

VISCOSITY = 0.2
CHEB_THETA = 1.1
CHEB_DELTA = 0.9
RHO_FIRST = 9.0 / 11.0
RHO_NEXT = 99.0 / 161.0

HI = 208
VMEM_LIMIT = 48 * 1024 * 1024


def deriv_table():
    points = np.array(
        [
            -1.0,
            -0.8717401485096066,
            -0.5917001814331423,
            -0.2092992179024789,
            0.2092992179024789,
            0.5917001814331423,
            0.8717401485096066,
            1.0,
        ]
    )
    before = np.ones(8)
    legendre = points.copy()
    for degree in range(1, 7):
        after = ((2 * degree + 1) * points * legendre - degree * before) / (degree + 1)
        before = legendre
        legendre = after
    spread = points[:, None] - points[None, :]
    safe = np.where(spread == 0.0, 1.0, spread)
    deriv = legendre[:, None] / (legendre[None, :] * safe)
    deriv = np.where(spread == 0.0, 0.0, deriv)
    deriv[0, 0] = -14.0
    deriv[7, 7] = 14.0
    return deriv


def np_split(table):
    rest = table.astype(np.float32)
    parts = []
    for _ in range(3):
        part = rest.astype(ml_dtypes.bfloat16)
        parts.append(part)
        rest = rest - part.astype(np.float32)
    return parts


def const_tables():
    d32 = deriv_table().astype(np.float32)
    along_j = np.kron(np.eye(2), np.kron(d32, np.eye(8))).astype(np.float32)
    along_k = np.kron(np.eye(16), d32).astype(np.float32)
    fwd = np.concatenate([along_j.T, along_k.T], axis=1)
    bwd = np.concatenate([along_j, along_k], axis=0)
    fh, fm, fl = np_split(fwd)
    bh, bm, bl = np_split(bwd)
    tab_f = np.concatenate([fh, fh, fm, fm, fl, fh], axis=0)
    tab_b = np.concatenate([bh, bm, bl], axis=0)
    coef = np.zeros((64, 128), np.float32)
    for way, mat in enumerate((d32, d32.T)):
        for to in range(4):
            for src in range(4):
                for half in range(2):
                    lanes = slice(64 * half, 64 * half + 64)
                    row = way * 32 + (to * 4 + src) * 2
                    coef[row, lanes] = mat[2 * to + half, 2 * src + half]
                    coef[row + 1, lanes] = mat[2 * to + half, 2 * src + 1 - half]
    return tab_f, tab_b, coef


def iota(shape, dim):
    return lax.broadcasted_iota(I32, shape, dim)


def split(x, count):
    parts = []
    for at in range(count):
        part = x.astype(BF16)
        parts.append(part)
        if at + 1 < count:
            x = x - part.astype(F32)
    return parts


def dot(a, b):
    return lax.dot_general(a, b, (((1,), (0,)), ((), ())), preferred_element_type=F32)


def dot_nt(a, b):
    return lax.dot_general(a, b, (((1,), (1,)), ((), ())), preferred_element_type=F32)


def one_hot(row, count):
    return (iota((count, row.shape[1]), 0) == row).astype(F32).astype(BF16)


def chunks_of(x):
    return [x[:, 128 * c : 128 * c + 128] for c in range(4)]


def along_i(chunks, coef_ref, way):
    turned = [pltpu.roll(x, 64, 1) for x in chunks]
    out = []
    for to in range(4):
        total = None
        for src in range(4):
            row = way * 32 + (to * 4 + src) * 2
            term = coef_ref[row : row + 1, :] * chunks[src] + coef_ref[row + 1 : row + 2, :] * turned[src]
            total = term if total is None else total + term
        out.append(total)
    return out


def grads(chunks, tab_f_ref, coef_ref):
    rows = chunks[0].shape[0]
    g_i = along_i(chunks, coef_ref, 0)
    h, m, l = split(jnp.concatenate(chunks, axis=0), 3)
    hm = jnp.concatenate([h, m], axis=1)
    hl = jnp.concatenate([h, l], axis=1)
    g_jk = dot(hm, tab_f_ref[0:256, :]) + (dot(hm, tab_f_ref[256:512, :]) + dot(hl, tab_f_ref[512:768, :]))
    g_j = [g_jk[rows * c : rows * c + rows, 0:128] for c in range(4)]
    g_k = [g_jk[rows * c : rows * c + rows, 128:256] for c in range(4)]
    return g_i, g_j, g_k


def divergence(u_i, u_j, u_k, tab_b_ref, coef_ref):
    rows = u_i[0].shape[0]
    out_i = along_i(u_i, coef_ref, 1)
    u = jnp.concatenate([jnp.concatenate(u_j, axis=0), jnp.concatenate(u_k, axis=0)], axis=1)
    h, m, l = split(u, 3)
    b_h = tab_b_ref[0:256, :]
    b_m = tab_b_ref[256:512, :]
    b_l = tab_b_ref[512:768, :]
    wide = jnp.concatenate([b_h, b_m], axis=1)
    both = dot(h, wide) + dot(m, wide)
    small = dot(h, b_l) + dot(l, b_h)
    total = both[:, 0:128] + (both[:, 128:256] + small)
    return [out_i[c] + total[rows * c : rows * c + rows] for c in range(4)]


def tiled(x, times):
    return x if times == 1 else jnp.concatenate([x] * times, axis=0)


def laplace(chunks, geom_ref, tab_f_ref, tab_b_ref, coef_ref):
    g_i, g_j, g_k = grads(chunks, tab_f_ref, coef_ref)
    geom = [chunks_of(geom_ref[a]) for a in range(3)]
    return divergence(
        [geom[0][c] * g_i[c] for c in range(4)],
        [geom[1][c] * g_j[c] for c in range(4)],
        [geom[2][c] * g_k[c] for c in range(4)],
        tab_b_ref,
        coef_ref,
    )


def permute(perm, chunks):
    parts = split(jnp.concatenate(chunks, axis=1), 3)
    return chunks_of(dot(perm, jnp.concatenate(parts, axis=0)))


def assemble_local(w):
    lane = iota((64, 128), 1)
    row = iota((64, 128), 0)
    bx = row & 7
    jj = (lane >> 3) & 7
    w = list(w)
    low = pltpu.roll(pltpu.roll(w[0], 64, 1), 63, 0)
    high = pltpu.roll(pltpu.roll(w[3], 64, 1), 1, 0)
    w[3] = w[3] + jnp.where((lane >= 64) & (bx < 7), low, 0.0)
    w[0] = w[0] + jnp.where((lane < 64) & (bx > 0), high, 0.0)
    out = []
    zero = jnp.zeros((8, 128), F32)
    for x in w:
        nxt = jnp.concatenate([pltpu.roll(x[8:64], 56, 1), zero], axis=0)
        prv = jnp.concatenate([zero, pltpu.roll(x[0:56], 72, 1)], axis=0)
        out.append(x + jnp.where(jj == 7, nxt, 0.0) + jnp.where(jj == 0, prv, 0.0))
    return out


def pack_sides(w):
    lane1 = iota((1, 128), 1)
    rows = [
        jnp.where(lane1 < 64, w[0][8 * by : 8 * by + 1], w[3][8 * by + 7 : 8 * by + 8]) for by in range(8)
    ]
    x_side = jnp.concatenate(rows, axis=0)
    jj = (iota((8, 128), 1) >> 3) & 7
    y_side = jnp.zeros((8, 128), F32)
    for c in range(4):
        y_side = jnp.where(jj == 2 * c, pltpu.roll(w[c][0:8], 16 * c, 1), y_side)
        y_side = jnp.where(jj == 2 * c + 1, pltpu.roll(w[c][56:64], (16 * c - 48) % 128, 1), y_side)
    return jnp.concatenate([x_side, y_side], axis=0)


def pack_faces(w):
    kk = iota((64, 128), 1) & 7
    face = jnp.zeros((64, 128), F32)
    for c in range(4):
        face = jnp.where(kk == 2 * c, pltpu.roll(w[c], 2 * c, 1), face)
        face = jnp.where(kk == 2 * c + 1, pltpu.roll(w[c], (2 * c - 6) % 128, 1), face)
    return face


def add_back(w, side, face):
    lane = iota((64, 128), 1)
    sub = iota((64, 128), 0) & 7
    kk = lane & 7
    jj = (iota((8, 128), 1) >> 3) & 7
    x_rows = jnp.concatenate(
        [jnp.broadcast_to(side[by : by + 1], (8, 128)) for by in range(8)], axis=0
    )
    y_side = side[8:16]
    out = []
    for c in range(4):
        x = w[c]
        if c == 0:
            x = x + jnp.where((sub == 0) & (lane < 64), x_rows, 0.0)
        if c == 3:
            x = x + jnp.where((sub == 7) & (lane >= 64), x_rows, 0.0)
        x = x + jnp.where(kk == 0, pltpu.roll(face, (-2 * c) % 128, 1), 0.0)
        x = x + jnp.where(kk == 7, pltpu.roll(face, (6 - 2 * c) % 128, 1), 0.0)
        first = x[0:8] + jnp.where(jj == 0, pltpu.roll(y_side, (-16 * c) % 128, 1), 0.0)
        last = x[56:64] + jnp.where(jj == 7, pltpu.roll(y_side, (48 - 16 * c) % 128, 1), 0.0)
        out.append(jnp.concatenate([first, x[8:56], last], axis=0))
    return out


def block_row(block):
    return jnp.concatenate([block[t : t + 1] for t in range(8)], axis=1)


def gather_tables(tables, idx_block, hi_count):
    row = block_row(idx_block)
    lows = one_hot(row & 127, 128)
    parts = []
    for table in tables:
        parts += split(table, 2)
    got = dot(jnp.concatenate(parts, axis=0), lows)
    mask = iota((hi_count, 1024), 0) == (row >> 7)
    out = []
    for at in range(len(tables)):
        both = got[2 * at * hi_count : (2 * at + 1) * hi_count] + got[(2 * at + 1) * hi_count : (2 * at + 2) * hi_count]
        out.append(jnp.sum(jnp.where(mask, both, 0.0), axis=0, keepdims=True))
    return out


def scatter_tables(rows, idx_block, hi_count):
    row = block_row(idx_block)
    lows = one_hot(row & 127, 128)
    mask = iota((hi_count, 1024), 0) == (row >> 7)
    parts = []
    for values in rows:
        for part in split(values, 2):
            spread = jnp.broadcast_to(part.astype(F32), (hi_count, 1024))
            parts.append(jnp.where(mask, spread, 0.0).astype(BF16))
    return dot_nt(jnp.concatenate(parts, axis=0), lows)


def send_values(local_fields, sidx_ref, fidx_ref, msg_ref, up_ref, down_ref, base, stride, face_base):
    sides = [pack_sides(w) for w in local_fields]
    faces = [pack_faces(w) for w in local_fields]
    for g in range(8):
        got = gather_tables(sides, sidx_ref[8 * g : 8 * g + 8, :], 16)
        for f, values in enumerate(got):
            for t in range(8):
                peer, half = (8 * g + t) // 2, t % 2
                at = peer * stride + base + 2 * f + half
                msg_ref[at : at + 1, :] = values[:, 128 * t : 128 * t + 128]
    for g in range(4):
        got = gather_tables(faces, fidx_ref[8 * g : 8 * g + 8, :], 64)
        out_ref = down_ref if g < 2 else up_ref
        for f, values in enumerate(got):
            for t in range(8):
                at = face_base + 16 * f + 8 * (g % 2) + t
                out_ref[at : at + 1, :] = values[:, 128 * t : 128 * t + 128]


def take_values(count, sidx_ref, fidx_ref, msg_ref, low_refs, upp_refs, stride):
    side = None
    for g in range(8):
        rows = []
        for f in range(count):
            cells = []
            for t in range(8):
                at = (8 * g + t) // 2 * stride + 2 * f + t % 2
                cells.append(msg_ref[at : at + 1, :])
            rows.append(jnp.concatenate(cells, axis=1))
        part = scatter_tables(rows, sidx_ref[8 * g : 8 * g + 8, :], 16)
        side = part if side is None else side + part
    face = None
    for g in range(4):
        refs = low_refs if g < 2 else upp_refs
        rows = [block_row(refs[f][0][refs[f][1] + 8 * (g % 2) : refs[f][1] + 8 * (g % 2) + 8, :]) for f in range(count)]
        part = scatter_tables(rows, fidx_ref[8 * g : 8 * g + 8, :], 64)
        face = part if face is None else face + part
    sides = [side[32 * f : 32 * f + 16] + side[32 * f + 16 : 32 * f + 32] for f in range(count)]
    faces = [face[128 * f : 128 * f + 64] + face[128 * f + 64 : 128 * f + 128] for f in range(count)]
    return sides, faces


def chain_place(left):
    eye = (iota((64, 64), 0) == iota((64, 64), 1)).astype(F32)
    l1 = left.astype(BF16)
    l2 = dot(l1, l1)
    m1 = eye + left
    l2b = l2.astype(BF16)
    l4 = dot(l2b, l2b)
    m2 = m1 + dot(l2b, m1.astype(BF16))
    m4 = m2 + dot(l4.astype(BF16), m2.astype(BF16))
    return jnp.sum(m4, axis=1, keepdims=True) - 1.0


def brick_places(conn):
    same = iota((64, 64), 0) == iota((64, 64), 1)

    def as_row(col):
        return jnp.sum(jnp.where(same, col, 0), axis=0, keepdims=True)

    end_x = as_row(conn[:, 475:476])
    end_y = as_row(conn[:, 251:252])
    left_x = (conn[:, 27:28] == end_x).astype(F32)
    left_y = (conn[:, 195:196] == end_y).astype(F32)
    return (chain_place(left_y) * 8.0 + chain_place(left_x)).astype(I32)


def place_table(hi_ref, lo_ref, acc_ref, blocks, hi_count):
    lane = (iota((1, 128), 1)).astype(F32)
    acc_ref[...] = jnp.zeros((HI, 256), F32)

    def step(g, carry):
        hi_block = hi_ref[pl.ds(pl.multiple_of(8 * g, 8), 8), :]
        lo_block = lo_ref[pl.ds(pl.multiple_of(8 * g, 8), 8), :]
        top = one_hot(block_row(hi_block), HI)
        low, high = [], []
        for t in range(8):
            hit = iota((128, 128), 0) == lo_block[t : t + 1]
            base = ((8 * g + t) * 128).astype(F32)
            low.append(jnp.where(hit, jnp.broadcast_to(lane, (128, 128)), 0.0).astype(BF16))
            high.append(jnp.where(hit, base, 0.0).astype(BF16))
        both = jnp.concatenate([jnp.concatenate(low, axis=1), jnp.concatenate(high, axis=1)], axis=0)
        acc_ref[...] += dot_nt(top, both)
        return carry

    lax.fori_loop(0, blocks, step, 0)


def look_up(table, row):
    low = one_hot(row & 127, 128)
    got = dot(table, jnp.concatenate([low, low], axis=0))
    mask = iota((HI, row.shape[1]), 0) == (row >> 7)
    return jnp.sum(jnp.where(mask, got, 0.0), axis=0, keepdims=True)


def tables_body(conn_ref, peer_ref, slot_ref, node_ref, counts_ref, axial_ref, sidx_ref, fidx_ref, perm_ref, back_ref, scratch):
    acc_s, acc_f, s_hi, s_lo, f_hi, f_lo, nodes = scratch
    conn = conn_ref[...]
    place = brick_places(conn)
    lane3 = iota((64, 192), 1) & 63
    place_row = jnp.sum(jnp.where(lane3 == iota((64, 192), 0), place, 0), axis=0, keepdims=True)
    perm_ref[...] = (iota((64, 192), 0) == place_row).astype(F32).astype(BF16)
    back_ref[...] = (lane3 == place).astype(F32).astype(BF16)
    perm = perm_ref[:, 0:64]

    ids = jnp.concatenate([(conn >> 7).astype(F32), (conn & 127).astype(F32)], axis=1).astype(BF16)
    ids = dot(perm, ids)
    hi_c = chunks_of(ids[:, 0:512])
    lo_c = chunks_of(ids[:, 512:1024])
    lane8 = iota((8, 128), 1)
    row8 = iota((8, 128), 0)
    keep_x = (((lane8 >> 3) & 7) < 7) | (row8 == 7)
    i_y = 2 * (((lane8 >> 3) & 7) >> 1) + (lane8 >> 6)
    keep_y = (i_y < 7) & ((row8 > 0) | (i_y > 0))
    lane = iota((64, 128), 1)
    row = iota((64, 128), 0)
    i_f = 2 * ((lane & 7) >> 1) + (lane >> 6)
    keep_f = ((i_f < 7) | ((row & 7) == 7)) & ((((lane >> 3) & 7) < 7) | ((row >> 3) == 7))
    side_hi = pack_sides(hi_c)
    s_hi[0:8, :] = jnp.where(keep_x, side_hi[0:8], -1.0).astype(I32)
    s_hi[8:16, :] = jnp.where(keep_y, side_hi[8:16], -1.0).astype(I32)
    s_lo[...] = pack_sides(lo_c).astype(I32)
    f_hi[...] = jnp.where(keep_f, pack_faces(hi_c), -1.0).astype(I32)
    f_lo[...] = pack_faces(lo_c).astype(I32)
    place_table(s_hi, s_lo, acc_s, 2, 16)
    place_table(f_hi, f_lo, acc_f, 8, 64)

    nodes[...] = jnp.zeros((128, 128), F32)

    def invert(g, carry):
        at = pl.ds(pl.multiple_of(1024 * g, 1024), 1024)
        peer = peer_ref[:, at]
        slot = slot_ref[:, at]
        node = node_ref[:, at]
        hit = iota((64, 1024), 0) == (peer * 2 + (slot >> 7))
        first = jnp.where(hit, (node >> 7).astype(F32), 0.0).astype(BF16)
        second = jnp.where(hit, (node & 127).astype(F32), 0.0).astype(BF16)
        nodes[...] += dot_nt(jnp.concatenate([first, second], axis=0), one_hot(slot & 127, 128))
        return carry

    lax.fori_loop(0, 8, invert, 0)
    ordered = (nodes[0:64, :] * 128.0 + nodes[64:128, :]).astype(I32)
    table_s = acc_s[...].astype(BF16)
    for g in range(8):
        places = look_up(table_s, block_row(ordered[8 * g : 8 * g + 8]))
        for t in range(8):
            sidx_ref[8 * g + t : 8 * g + t + 1, :] = places[:, 128 * t : 128 * t + 128].astype(I32)
    table_f = acc_f[...].astype(BF16)
    for g in range(4):
        cells = axial_ref[g // 2 : g // 2 + 1, 1024 * (g % 2) : 1024 * (g % 2) + 1024]
        places = look_up(table_f, cells)
        for t in range(8):
            fidx_ref[8 * g + t : 8 * g + t + 1, :] = places[:, 128 * t : 128 * t + 128].astype(I32)
    limit = jnp.sum(
        jnp.where(iota((64, 32), 1) == (iota((64, 32), 0) >> 1), counts_ref[...], 0), axis=1, keepdims=True
    )
    slots = (iota((64, 128), 0) & 1) * 128 + iota((64, 128), 1)
    sidx_ref[...] = jnp.where(slots < limit, sidx_ref[...], -1)


def first_kernel(
    conn_ref, peer_ref, slot_ref, node_ref, counts_ref, axial_ref, pressure_ref, geom_ref, tab_f_ref, tab_b_ref, coef_ref,
    msg_ref, up_ref, down_ref, w_ref, sidx_ref, fidx_ref, perm_ref, back_ref, *scratch,
):
    tables_body(
        conn_ref, peer_ref, slot_ref, node_ref, counts_ref, axial_ref, sidx_ref, fidx_ref, perm_ref, back_ref, scratch
    )
    out = laplace(chunks_of(pressure_ref[...]), geom_ref, tab_f_ref, tab_b_ref, coef_ref)
    w = permute(perm_ref[...], out)
    for c in range(4):
        w_ref[:, 128 * c : 128 * c + 128] = w[c]
    send_values([assemble_local(w)], sidx_ref, fidx_ref, msg_ref, up_ref, down_ref, 0, 2, 0)


def momentum_kernel(
    velocity_ref, force_ref, mass_ref, metric_ref, geom_ref, tab_f_ref, tab_b_ref, coef_ref, perm_ref, sidx_ref, fidx_ref,
    msg_ref, up_ref, down_ref, w_ref,
):
    parts = [chunks_of(velocity_ref[a]) for a in range(3)]
    stacked = [jnp.concatenate([parts[a][c] for a in range(3)], axis=0) for c in range(4)]
    grad = grads(stacked, tab_f_ref, coef_ref)
    same = iota((64, 64), 0) == iota((64, 64), 1)
    scale = [jnp.sum(jnp.where(same, metric_ref[a : a + 1, :], 0.0), axis=1, keepdims=True) for a in range(3)]
    convect = []
    flux = [[], [], []]
    for c in range(4):
        total = None
        for a in range(3):
            speed = tiled(scale[a] * parts[a][c], 3)
            term = speed * grad[a][c]
            total = term if total is None else total + term
            flux[a].append(tiled(geom_ref[a, :, 128 * c : 128 * c + 128], 3) * grad[a][c])
        convect.append(total)
    diffuse = divergence(flux[0], flux[1], flux[2], tab_b_ref, coef_ref)
    fields = []
    for f in range(3):
        rows = slice(64 * f, 64 * f + 64)
        out = []
        for c in range(4):
            lanes = slice(128 * c, 128 * c + 128)
            out.append(
                mass_ref[:, lanes] * (force_ref[f, :, lanes] - convect[c][rows]) - VISCOSITY * diffuse[c][rows]
            )
        w = permute(perm_ref[...], out)
        for c in range(4):
            w_ref[f, :, 128 * c : 128 * c + 128] = w[c]
        fields.append(assemble_local(w))
    send_values(fields, sidx_ref, fidx_ref, msg_ref, up_ref, down_ref, 0, 6, 0)


def second_kernel(
    msg_in_ref, low_ref, upp_ref, w_in_ref, pressure_ref, rhs_ref, jacobi_ref, geom_ref, tab_f_ref, tab_b_ref, coef_ref,
    perm_ref, back_ref, sidx_ref, fidx_ref, msg_m_ref, up_m_ref, down_m_ref,
    msg_ref, up_ref, down_ref, w_ref, base_ref, res_ref,
):
    sides, faces = take_values(1, sidx_ref, fidx_ref, msg_in_ref, [(low_ref, 0)], [(upp_ref, 0)], 2)
    w = add_back(chunks_of(w_in_ref[...]), sides[0], faces[0])
    applied = permute(back_ref[...], assemble_local(w))
    step = []
    for c in range(4):
        lanes = slice(128 * c, 128 * c + 128)
        jac = jacobi_ref[:, lanes]
        res = rhs_ref[:, lanes] - applied[c]
        step.append(jac * res / CHEB_THETA)
        first = pressure_ref[:, lanes] + step[c]
        base_ref[:, lanes] = first + RHO_NEXT * RHO_FIRST * step[c]
        res_ref[:, lanes] = res
    out = laplace(step, geom_ref, tab_f_ref, tab_b_ref, coef_ref)
    w = permute(perm_ref[...], out)
    for c in range(4):
        w_ref[:, 128 * c : 128 * c + 128] = w[c]
    send_values([assemble_local(w)], sidx_ref, fidx_ref, msg_ref, up_ref, down_ref, 0, 8, 0)
    for peer in range(32):
        msg_ref[8 * peer + 2 : 8 * peer + 8, :] = msg_m_ref[6 * peer : 6 * peer + 6, :]
    up_ref[16:64, :] = up_m_ref[...]
    down_ref[16:64, :] = down_m_ref[...]


def last_kernel(
    msg_in_ref, low_ref, upp_ref, w_in_ref, w_m_ref, jacobi_ref, base_ref, res_ref, back_ref, sidx_ref, fidx_ref,
    pressure_ref, momentum_ref,
):
    low = [(low_ref, 16 * f) for f in range(4)]
    upp = [(upp_ref, 16 * f) for f in range(4)]
    sides, faces = take_values(4, sidx_ref, fidx_ref, msg_in_ref, low, upp, 8)
    for f in range(4):
        held = w_in_ref[...] if f == 0 else w_m_ref[f - 1]
        w = add_back(chunks_of(held), sides[f], faces[f])
        applied = permute(back_ref[...], assemble_local(w))
        for c in range(4):
            lanes = slice(128 * c, 128 * c + 128)
            if f == 0:
                pressure_ref[:, lanes] = base_ref[:, lanes] + 2.0 * RHO_NEXT / CHEB_DELTA * jacobi_ref[:, lanes] * (
                    res_ref[:, lanes] - applied[c]
                )
            else:
                momentum_ref[f - 1, :, lanes] = applied[c]


def shape(*dims, dtype=F32):
    return jax.ShapeDtypeStruct(dims, dtype)


def call(kernel, outs, args, scratch=(), name=None):
    vmem = pl.BlockSpec(memory_space=pltpu.VMEM)
    return pl.pallas_call(
        kernel,
        out_shape=outs,
        in_specs=[vmem] * len(args),
        out_specs=[vmem] * len(outs),
        scratch_shapes=list(scratch),
        compiler_params=pltpu.CompilerParams(vmem_limit_bytes=VMEM_LIMIT),
        name=name,
    )(*args)


def consts():
    return [jnp.asarray(t) for t in const_tables()]


def run_first(conn, peer, slot, node, counts, axial, pressure, geom):
    return call(
        first_kernel,
        [shape(64, 128), shape(16, 128), shape(16, 128), shape(64, 512), shape(64, 128, dtype=I32),
         shape(32, 128, dtype=I32), shape(64, 192, dtype=BF16), shape(64, 192, dtype=BF16)],
        [conn, peer, slot, node, counts, axial, pressure, geom, *consts()],
        [pltpu.VMEM((HI, 256), F32), pltpu.VMEM((HI, 256), F32), pltpu.VMEM((16, 128), I32), pltpu.VMEM((16, 128), I32),
         pltpu.VMEM((64, 128), I32), pltpu.VMEM((64, 128), I32), pltpu.VMEM((128, 128), F32)],
        "first",
    )


def run_momentum(velocity, force, mass, metric, geom, perm, sidx, fidx):
    return call(
        momentum_kernel,
        [shape(192, 128), shape(48, 128), shape(48, 128), shape(3, 64, 512)],
        [velocity, force, mass, metric, geom, *consts(), perm, sidx, fidx],
        name="momentum",
    )


def run_second(msg, low, upp, w, pressure, rhs, jacobi, geom, perm, back, sidx, fidx, msg_m, up_m, down_m):
    return call(
        second_kernel,
        [shape(256, 128), shape(64, 128), shape(64, 128), shape(64, 512), shape(64, 512), shape(64, 512)],
        [msg, low, upp, w, pressure, rhs, jacobi, geom, *consts(), perm, back, sidx, fidx, msg_m, up_m, down_m],
        name="second",
    )


def run_last(msg, low, upp, w, w_m, jacobi, base, res, back, sidx, fidx):
    return call(
        last_kernel,
        [shape(64, 512), shape(3, 64, 512)],
        [msg, low, upp, w, w_m, jacobi, base, res, back, sidx, fidx],
        name="last",
    )


def exchange(msg, up, down):
    rows = msg.shape[0] // 32
    arrived = lax.all_to_all(msg.reshape(32, rows, 128), ("gy", "gz"), split_axis=0, concat_axis=0, tiled=True)
    count = lax.axis_size("gx")
    from_low = lax.ppermute(up, "gx", [(i, (i + 1) % count) for i in range(count)])
    from_upp = lax.ppermute(down, "gx", [((i + 1) % count, i) for i in range(count)])
    return arrived.reshape(32 * rows, 128), from_low, from_upp


def on_device(
    pressure, rhs, jacobi, geom, velocity, force, mass, metric, conn, ent_peer, ent_slot, ent_node, counts, axial_nodes
):
    msg, up, down, w, sidx, fidx, perm, back = run_first(
        conn, ent_peer, ent_slot, ent_node, counts, axial_nodes[0], pressure, geom
    )
    got = exchange(msg, up, down)
    msg_m, up_m, down_m, w_m = run_momentum(velocity, force, mass, metric, geom, perm, sidx, fidx)
    msg, up, down, w, base, res = run_second(
        *got, w, pressure, rhs, jacobi, geom, perm, back, sidx, fidx, msg_m, up_m, down_m
    )
    got = exchange(msg, up, down)
    return tuple(run_last(*got, w, w_m, jacobi, base, res, back, sidx, fidx))


def solution(mesh):
    both = P(("gx", "gy", "gz"), None)
    three = P(None, ("gx", "gy", "gz"), None)
    return jax.shard_map(
        on_device,
        mesh=mesh,
        in_specs=(
            both, both, both, three, three, three, both, P(None, ("gx", "gy", "gz")), both, both, both, both, both,
            P(("gx", "gy", "gz"), None, None),
        ),
        out_specs=(both, three),
        check_vma=False,
    )
```

```python
import jax
import jax.numpy as jnp
import numpy as np
from jax import lax
from jax.experimental import pallas as pl
from jax.experimental.pallas import tpu as pltpu
from jax.sharding import PartitionSpec as P

F32 = jnp.float32
BF16 = jnp.bfloat16
I32 = jnp.int32

VISCOSITY = 0.2
CHEB_THETA = 1.1
CHEB_DELTA = 0.9
RHO_FIRST = 9.0 / 11.0
RHO_NEXT = 99.0 / 161.0

HI = 208
VMEM_LIMIT = 48 * 1024 * 1024


def deriv_table():
    points = np.array(
        [
            -1.0,
            -0.8717401485096066,
            -0.5917001814331423,
            -0.2092992179024789,
            0.2092992179024789,
            0.5917001814331423,
            0.8717401485096066,
            1.0,
        ]
    )
    before = np.ones(8)
    legendre = points.copy()
    for degree in range(1, 7):
        after = ((2 * degree + 1) * points * legendre - degree * before) / (degree + 1)
        before = legendre
        legendre = after
    spread = points[:, None] - points[None, :]
    safe = np.where(spread == 0.0, 1.0, spread)
    deriv = legendre[:, None] / (legendre[None, :] * safe)
    deriv = np.where(spread == 0.0, 0.0, deriv)
    deriv[0, 0] = -14.0
    deriv[7, 7] = 14.0
    return deriv


def const_tables():
    d32 = deriv_table().astype(np.float32)
    along_j = np.kron(np.eye(2), np.kron(d32, np.eye(8))).astype(np.float32)
    along_k = np.kron(np.eye(16), d32).astype(np.float32)
    fwd = np.concatenate([along_j.T, along_k.T], axis=1)
    bwd = np.concatenate([along_j, along_k], axis=0)
    coef = np.zeros((64, 128), np.float32)
    for way, mat in enumerate((d32, d32.T)):
        for to in range(4):
            for src in range(4):
                for half in range(2):
                    lanes = slice(64 * half, 64 * half + 64)
                    row = way * 32 + (to * 4 + src) * 2
                    coef[row, lanes] = mat[2 * to + half, 2 * src + half]
                    coef[row + 1, lanes] = mat[2 * to + half, 2 * src + 1 - half]
    return fwd, bwd, coef


def iota(shape, dim):
    return lax.broadcasted_iota(I32, shape, dim)


def split(x, count):
    parts = []
    for at in range(count):
        part = x.astype(BF16)
        parts.append(part)
        if at + 1 < count:
            x = x - part.astype(F32)
    return parts


def dot(a, b):
    return lax.dot_general(a, b, (((1,), (0,)), ((), ())), preferred_element_type=F32)


def dot_nt(a, b):
    return lax.dot_general(a, b, (((1,), (1,)), ((), ())), preferred_element_type=F32)


def one_hot(row, count):
    return (iota((count, row.shape[1]), 0) == row).astype(F32).astype(BF16)


def chunks_of(x):
    return [x[:, 128 * c : 128 * c + 128] for c in range(4)]


def along_i(chunks, coef_ref, way):
    turned = [pltpu.roll(x, 64, 1) for x in chunks]
    out = []
    for to in range(4):
        total = None
        for src in range(4):
            row = way * 32 + (to * 4 + src) * 2
            term = coef_ref[row : row + 1, :] * chunks[src] + coef_ref[row + 1 : row + 2, :] * turned[src]
            total = term if total is None else total + term
        out.append(total)
    return out


def grads(chunks, tab_f_ref, coef_ref):
    rows = chunks[0].shape[0]
    g_i = along_i(chunks, coef_ref, 0)
    h, m, l = split(jnp.concatenate(chunks, axis=0), 3)
    hm = jnp.concatenate([h, m], axis=1)
    hl = jnp.concatenate([h, l], axis=1)
    g_jk = dot(hm, tab_f_ref[0:256, :]) + (dot(hm, tab_f_ref[256:512, :]) + dot(hl, tab_f_ref[512:768, :]))
    g_j = [g_jk[rows * c : rows * c + rows, 0:128] for c in range(4)]
    g_k = [g_jk[rows * c : rows * c + rows, 128:256] for c in range(4)]
    return g_i, g_j, g_k


def divergence(u_i, u_j, u_k, tab_b_ref, coef_ref):
    rows = u_i[0].shape[0]
    out_i = along_i(u_i, coef_ref, 1)
    u = jnp.concatenate([jnp.concatenate(u_j, axis=0), jnp.concatenate(u_k, axis=0)], axis=1)
    h, m, l = split(u, 3)
    b_h = tab_b_ref[0:256, :]
    b_m = tab_b_ref[256:512, :]
    b_l = tab_b_ref[512:768, :]
    wide = jnp.concatenate([b_h, b_m], axis=1)
    both = dot(h, wide) + dot(m, wide)
    small = dot(h, b_l) + dot(l, b_h)
    total = both[:, 0:128] + (both[:, 128:256] + small)
    return [out_i[c] + total[rows * c : rows * c + rows] for c in range(4)]


def tiled(x, times):
    return x if times == 1 else jnp.concatenate([x] * times, axis=0)


def laplace(chunks, geom_ref, tab_f_ref, tab_b_ref, coef_ref):
    g_i, g_j, g_k = grads(chunks, tab_f_ref, coef_ref)
    geom = [chunks_of(geom_ref[a]) for a in range(3)]
    return divergence(
        [geom[0][c] * g_i[c] for c in range(4)],
        [geom[1][c] * g_j[c] for c in range(4)],
        [geom[2][c] * g_k[c] for c in range(4)],
        tab_b_ref,
        coef_ref,
    )


def permute(perm, chunks):
    parts = split(jnp.concatenate(chunks, axis=1), 3)
    return chunks_of(dot(perm, jnp.concatenate(parts, axis=0)))


def assemble_local(w):
    lane = iota((64, 128), 1)
    row = iota((64, 128), 0)
    bx = row & 7
    jj = (lane >> 3) & 7
    w = list(w)
    low = pltpu.roll(pltpu.roll(w[0], 64, 1), 63, 0)
    high = pltpu.roll(pltpu.roll(w[3], 64, 1), 1, 0)
    w[3] = w[3] + jnp.where((lane >= 64) & (bx < 7), low, 0.0)
    w[0] = w[0] + jnp.where((lane < 64) & (bx > 0), high, 0.0)
    out = []
    zero = jnp.zeros((8, 128), F32)
    for x in w:
        nxt = jnp.concatenate([pltpu.roll(x[8:64], 56, 1), zero], axis=0)
        prv = jnp.concatenate([zero, pltpu.roll(x[0:56], 72, 1)], axis=0)
        out.append(x + jnp.where(jj == 7, nxt, 0.0) + jnp.where(jj == 0, prv, 0.0))
    return out


def pack_sides(w):
    lane1 = iota((1, 128), 1)
    rows = [
        jnp.where(lane1 < 64, w[0][8 * by : 8 * by + 1], w[3][8 * by + 7 : 8 * by + 8]) for by in range(8)
    ]
    x_side = jnp.concatenate(rows, axis=0)
    jj = (iota((8, 128), 1) >> 3) & 7
    y_side = jnp.zeros((8, 128), F32)
    for c in range(4):
        y_side = jnp.where(jj == 2 * c, pltpu.roll(w[c][0:8], 16 * c, 1), y_side)
        y_side = jnp.where(jj == 2 * c + 1, pltpu.roll(w[c][56:64], (16 * c - 48) % 128, 1), y_side)
    return jnp.concatenate([x_side, y_side], axis=0)


def pack_faces(w):
    kk = iota((64, 128), 1) & 7
    face = jnp.zeros((64, 128), F32)
    for c in range(4):
        face = jnp.where(kk == 2 * c, pltpu.roll(w[c], 2 * c, 1), face)
        face = jnp.where(kk == 2 * c + 1, pltpu.roll(w[c], (2 * c - 6) % 128, 1), face)
    return face


def add_back(w, side, face):
    lane = iota((64, 128), 1)
    sub = iota((64, 128), 0) & 7
    kk = lane & 7
    jj = (iota((8, 128), 1) >> 3) & 7
    x_rows = jnp.concatenate(
        [jnp.broadcast_to(side[by : by + 1], (8, 128)) for by in range(8)], axis=0
    )
    y_side = side[8:16]
    out = []
    for c in range(4):
        x = w[c]
        if c == 0:
            x = x + jnp.where((sub == 0) & (lane < 64), x_rows, 0.0)
        if c == 3:
            x = x + jnp.where((sub == 7) & (lane >= 64), x_rows, 0.0)
        x = x + jnp.where(kk == 0, pltpu.roll(face, (-2 * c) % 128, 1), 0.0)
        x = x + jnp.where(kk == 7, pltpu.roll(face, (6 - 2 * c) % 128, 1), 0.0)
        first = x[0:8] + jnp.where(jj == 0, pltpu.roll(y_side, (-16 * c) % 128, 1), 0.0)
        last = x[56:64] + jnp.where(jj == 7, pltpu.roll(y_side, (48 - 16 * c) % 128, 1), 0.0)
        out.append(jnp.concatenate([first, x[8:56], last], axis=0))
    return out


def block_row(block):
    return jnp.concatenate([block[t : t + 1] for t in range(8)], axis=1)


def gather_tables(tables, hi_block, lows, hi_count):
    parts = []
    for table in tables:
        parts += split(table, 2)
    got = dot(jnp.concatenate(parts, axis=0), lows)
    mask = iota((hi_count, 1024), 0) == block_row(hi_block)
    out = []
    for at in range(len(tables)):
        both = got[2 * at * hi_count : (2 * at + 1) * hi_count] + got[(2 * at + 1) * hi_count : (2 * at + 2) * hi_count]
        out.append(jnp.sum(jnp.where(mask, both, 0.0), axis=0, keepdims=True))
    return out


def scatter_tables(rows, hi_block, lows, hi_count):
    mask = iota((hi_count, 1024), 0) == block_row(hi_block)
    parts = []
    for values in rows:
        for part in split(values, 2):
            spread = jnp.broadcast_to(part.astype(F32), (hi_count, 1024))
            parts.append(jnp.where(mask, spread, 0.0).astype(BF16))
    return dot_nt(jnp.concatenate(parts, axis=0), lows)


def lanes_of(g):
    return slice(1024 * g, 1024 * g + 1024)


def rows_of(g):
    return slice(8 * g, 8 * g + 8)


def send_values(local_fields, shi_ref, fhi_ref, slow_ref, flow_ref, msg_ref, up_ref, down_ref, stride):
    sides = [pack_sides(w) for w in local_fields]
    faces = [pack_faces(w) for w in local_fields]
    for g in range(8):
        got = gather_tables(sides, shi_ref[rows_of(g), :], slow_ref[:, lanes_of(g)], 16)
        for f, values in enumerate(got):
            for t in range(8):
                at = (8 * g + t) // 2 * stride + 2 * f + t % 2
                msg_ref[at : at + 1, :] = values[:, 128 * t : 128 * t + 128]
    for g in range(4):
        got = gather_tables(faces, fhi_ref[rows_of(g), :], flow_ref[:, lanes_of(g)], 64)
        out_ref = down_ref if g < 2 else up_ref
        for f, values in enumerate(got):
            for t in range(8):
                at = 16 * f + 8 * (g % 2) + t
                out_ref[at : at + 1, :] = values[:, 128 * t : 128 * t + 128]


def take_values(count, shi_ref, fhi_ref, slow_ref, flow_ref, msg_ref, low_ref, upp_ref, stride):
    side = None
    for g in range(8):
        rows = []
        for f in range(count):
            cells = []
            for t in range(8):
                at = (8 * g + t) // 2 * stride + 2 * f + t % 2
                cells.append(msg_ref[at : at + 1, :])
            rows.append(jnp.concatenate(cells, axis=1))
        part = scatter_tables(rows, shi_ref[rows_of(g), :], slow_ref[:, lanes_of(g)], 16)
        side = part if side is None else side + part
    face = None
    for g in range(4):
        ref = low_ref if g < 2 else upp_ref
        rows = [block_row(ref[16 * f + 8 * (g % 2) : 16 * f + 8 * (g % 2) + 8, :]) for f in range(count)]
        part = scatter_tables(rows, fhi_ref[rows_of(g), :], flow_ref[:, lanes_of(g)], 64)
        face = part if face is None else face + part
    sides = [side[32 * f : 32 * f + 16] + side[32 * f + 16 : 32 * f + 32] for f in range(count)]
    faces = [face[128 * f : 128 * f + 64] + face[128 * f + 64 : 128 * f + 128] for f in range(count)]
    return sides, faces


def chain_place(left):
    eye = (iota((64, 64), 0) == iota((64, 64), 1)).astype(F32)
    l1 = left.astype(BF16)
    l2 = dot(l1, l1)
    m1 = eye + left
    l2b = l2.astype(BF16)
    l4 = dot(l2b, l2b)
    m2 = m1 + dot(l2b, m1.astype(BF16))
    m4 = m2 + dot(l4.astype(BF16), m2.astype(BF16))
    return jnp.sum(m4, axis=1, keepdims=True) - 1.0


def brick_places(conn):
    same = iota((64, 64), 0) == iota((64, 64), 1)

    def as_row(col):
        return jnp.sum(jnp.where(same, col, 0), axis=0, keepdims=True)

    end_x = as_row(conn[:, 475:476])
    end_y = as_row(conn[:, 251:252])
    left_x = (conn[:, 27:28] == end_x).astype(F32)
    left_y = (conn[:, 195:196] == end_y).astype(F32)
    return (chain_place(left_y) * 8.0 + chain_place(left_x)).astype(I32)


def place_table(hi, lo, count):
    lane = 1.0 + iota((128, 128), 1).astype(F32) * (1.0 / 128.0)
    total = None
    for g in range(count // 8):
        top = one_hot(block_row(hi[rows_of(g)]), HI)
        low = []
        for t in range(8):
            hit = iota((128, 128), 0) == lo[8 * g + t : 8 * g + t + 1]
            low.append(jnp.where(hit, lane * (2.0 ** (8 * g + t - count // 2)), 0.0).astype(BF16))
        part = dot_nt(jnp.concatenate(low, axis=1), top)
        total = part if total is None else total + part
    return total.astype(BF16)


def look_up(table, row):
    got = dot(table, one_hot(row >> 7, HI))
    mask = iota((128, row.shape[1]), 0) == (row & 127)
    return jnp.sum(jnp.where(mask, got, 0.0), axis=0, keepdims=True)


def decode(x, count):
    x = x * (2.0 ** (count // 2))
    row = jnp.zeros(x.shape, I32)
    jump = count // 2
    while jump:
        big = x >= 2.0**jump
        row = row + jnp.where(big, jump, 0)
        x = jnp.where(big, x * (2.0**-jump), x)
        jump //= 2
    return row, (x * 128.0).astype(I32) - 128


def put_rows(ref, at, values):
    for t in range(8):
        ref[at + t : at + t + 1, :] = values[:, 128 * t : 128 * t + 128]


def build_perm(conn, perm_ref, back_ref):
    place = brick_places(conn)
    lane3 = iota((64, 192), 1) & 63
    place_row = jnp.sum(jnp.where(lane3 == iota((64, 192), 0), place, 0), axis=0, keepdims=True)
    perm_ref[...] = (iota((64, 192), 0) == place_row).astype(F32).astype(BF16)
    back_ref[...] = (lane3 == place).astype(F32).astype(BF16)


def node_places(conn, perm):
    ids = jnp.concatenate([(conn >> 7).astype(F32), (conn & 127).astype(F32)], axis=1).astype(BF16)
    ids = dot(perm, ids)
    hi_c = chunks_of(ids[:, 0:512])
    lo_c = chunks_of(ids[:, 512:1024])
    lane8 = iota((16, 128), 1)
    row8 = iota((16, 128), 0)
    in_x = (((lane8 >> 3) & 7) < 7) | (row8 == 7)
    i_y = 2 * (((lane8 >> 3) & 7) >> 1) + (lane8 >> 6)
    in_y = (i_y < 7) & ((row8 > 8) | (i_y > 0))
    keep_s = ((row8 < 8) & in_x) | ((row8 >= 8) & in_y)
    lane = iota((64, 128), 1)
    row = iota((64, 128), 0)
    i_f = 2 * ((lane & 7) >> 1) + (lane >> 6)
    keep_f = ((i_f < 7) | ((row & 7) == 7)) & ((((lane >> 3) & 7) < 7) | ((row >> 3) == 7))
    table_s = place_table(
        jnp.where(keep_s, pack_sides(hi_c), -1.0).astype(I32), pack_sides(lo_c).astype(I32), 16
    )
    table_f = place_table(
        jnp.where(keep_f, pack_faces(hi_c), -1.0).astype(I32), pack_faces(lo_c).astype(I32), 64
    )
    return table_s, table_f


def side_lists(table_s, peer_ref, slot_ref, node_ref, counts, shi_ref, slow_ref):
    total = None
    for g in range(8):
        at = lanes_of(g)
        slot = slot_ref[:, at]
        places = look_up(table_s, node_ref[:, at])
        hit = iota((64, 1024), 0) == (peer_ref[:, at] * 2 + (slot >> 7))
        part = dot_nt(jnp.where(hit, places, 0.0).astype(BF16), one_hot(slot & 127, 128))
        total = part if total is None else total + part
    row, lane = decode(total, 16)
    limit = jnp.sum(jnp.where(iota((64, 32), 1) == (iota((64, 32), 0) >> 1), counts, 0), axis=1, keepdims=True)
    slots = (iota((64, 128), 0) & 1) * 128 + iota((64, 128), 1)
    shi_ref[...] = jnp.where(slots < limit, row, -1)
    for g in range(8):
        slow_ref[:, lanes_of(g)] = one_hot(block_row(lane[rows_of(g)]), 128)


def face_lists(table_f, axial_ref, coded_ref, fhi_ref, flow_ref):
    for g in range(4):
        put_rows(coded_ref, 8 * g, look_up(table_f, axial_ref[0, g // 2 : g // 2 + 1, lanes_of(g % 2)]))
    row, lane = decode(coded_ref[...], 64)
    fhi_ref[...] = row
    for g in range(4):
        flow_ref[:, lanes_of(g)] = one_hot(block_row(lane[rows_of(g)]), 128)


def first_kernel(*refs):
    (conn_h, peer_h, slot_h, node_h, counts_h, axial_h, pressure_h, geom_h, fwd_h, bwd_h, coef_h) = refs[:11]
    later_h = refs[11:17]
    (msg_ref, up_ref, down_ref, w_ref, shi_ref, fhi_ref, slow_ref, flow_ref, perm_ref, back_ref) = refs[17:27]
    (tab_f_ref, tab_b_ref, coef_ref, pressure_ref, geom_ref) = refs[27:32]
    later = refs[32:38]
    (conn_ref, peer_ref, slot_ref, node_ref, counts_ref, axial_ref, fwd_ref, bwd_ref, coded_ref, sems) = refs[38:]
    pairs = [
        (conn_h, conn_ref), (pressure_h, pressure_ref), (fwd_h, fwd_ref), (bwd_h, bwd_ref), (coef_h, coef_ref),
        (geom_h, geom_ref), (node_h, node_ref), (peer_h, peer_ref), (slot_h, slot_ref), (counts_h, counts_ref),
        (axial_h, axial_ref), *zip(later_h, later),
    ]
    copies = [pltpu.make_async_copy(src, dst, sems.at[at]) for at, (src, dst) in enumerate(pairs)]
    for copy in copies:
        copy.start()
    copies[0].wait()
    conn = conn_ref[...]
    build_perm(conn, perm_ref, back_ref)
    for copy in copies[1:11]:
        copy.wait()
    fh, fm, fl = split(fwd_ref[...], 3)
    for at, part in enumerate([fh, fh, fm, fm, fl, fh]):
        tab_f_ref[128 * at : 128 * at + 128, :] = part
    for at, part in enumerate(split(bwd_ref[...], 3)):
        tab_b_ref[256 * at : 256 * at + 256, :] = part
    table_s, table_f = node_places(conn, perm_ref[:, 0:64])
    out = laplace(chunks_of(pressure_ref[...]), geom_ref, tab_f_ref, tab_b_ref, coef_ref)
    w = permute(perm_ref[...], out)
    for c in range(4):
        w_ref[:, 128 * c : 128 * c + 128] = w[c]
    side_lists(table_s, peer_ref, slot_ref, node_ref, counts_ref[...], shi_ref, slow_ref)
    face_lists(table_f, axial_ref, coded_ref, fhi_ref, flow_ref)
    send_values([assemble_local(w)], shi_ref, fhi_ref, slow_ref, flow_ref, msg_ref, up_ref, down_ref, 2)
    for copy in copies[11:]:
        copy.wait()


def momentum_kernel(
    velocity_ref, force_ref, mass_ref, metric_ref, geom_ref, tab_f_ref, tab_b_ref, coef_ref, perm_ref, shi_ref, fhi_ref,
    slow_ref, flow_ref,
    msg_ref, up_ref, down_ref, w_ref,
):
    parts = [chunks_of(velocity_ref[a]) for a in range(3)]
    stacked = [jnp.concatenate([parts[a][c] for a in range(3)], axis=0) for c in range(4)]
    grad = grads(stacked, tab_f_ref, coef_ref)
    same = iota((64, 64), 0) == iota((64, 64), 1)
    scale = [jnp.sum(jnp.where(same, metric_ref[a : a + 1, :], 0.0), axis=1, keepdims=True) for a in range(3)]
    convect = []
    flux = [[], [], []]
    for c in range(4):
        total = None
        for a in range(3):
            speed = tiled(scale[a] * parts[a][c], 3)
            term = speed * grad[a][c]
            total = term if total is None else total + term
            flux[a].append(tiled(geom_ref[a, :, 128 * c : 128 * c + 128], 3) * grad[a][c])
        convect.append(total)
    diffuse = divergence(flux[0], flux[1], flux[2], tab_b_ref, coef_ref)
    fields = []
    for f in range(3):
        rows = slice(64 * f, 64 * f + 64)
        out = []
        for c in range(4):
            lanes = slice(128 * c, 128 * c + 128)
            out.append(
                mass_ref[:, lanes] * (force_ref[f, :, lanes] - convect[c][rows]) - VISCOSITY * diffuse[c][rows]
            )
        w = permute(perm_ref[...], out)
        for c in range(4):
            w_ref[f, :, 128 * c : 128 * c + 128] = w[c]
        fields.append(assemble_local(w))
    send_values(fields, shi_ref, fhi_ref, slow_ref, flow_ref, msg_ref, up_ref, down_ref, 6)


def second_kernel(
    msg_in_ref, low_ref, upp_ref, w_in_ref, pressure_ref, rhs_ref, jacobi_ref, geom_ref, tab_f_ref, tab_b_ref, coef_ref,
    perm_ref, back_ref, shi_ref, fhi_ref, slow_ref, flow_ref, msg_m_ref, up_m_ref, down_m_ref,
    msg_ref, up_ref, down_ref, w_ref, base_ref, res_ref,
):
    sides, faces = take_values(1, shi_ref, fhi_ref, slow_ref, flow_ref, msg_in_ref, low_ref, upp_ref, 2)
    w = add_back(chunks_of(w_in_ref[...]), sides[0], faces[0])
    applied = permute(back_ref[...], assemble_local(w))
    step = []
    for c in range(4):
        lanes = slice(128 * c, 128 * c + 128)
        jac = jacobi_ref[:, lanes]
        res = rhs_ref[:, lanes] - applied[c]
        step.append(jac * res / CHEB_THETA)
        first = pressure_ref[:, lanes] + step[c]
        base_ref[:, lanes] = first + RHO_NEXT * RHO_FIRST * step[c]
        res_ref[:, lanes] = res
    out = laplace(step, geom_ref, tab_f_ref, tab_b_ref, coef_ref)
    w = permute(perm_ref[...], out)
    for c in range(4):
        w_ref[:, 128 * c : 128 * c + 128] = w[c]
    send_values([assemble_local(w)], shi_ref, fhi_ref, slow_ref, flow_ref, msg_ref, up_ref, down_ref, 8)
    for peer in range(32):
        msg_ref[8 * peer + 2 : 8 * peer + 8, :] = msg_m_ref[6 * peer : 6 * peer + 6, :]
    up_ref[16:64, :] = up_m_ref[...]
    down_ref[16:64, :] = down_m_ref[...]


def last_kernel(
    msg_in_ref, low_ref, upp_ref, w_in_ref, w_m_ref, jacobi_ref, base_ref, res_ref, back_ref, shi_ref, fhi_ref, slow_ref,
    flow_ref,
    pressure_h, momentum_h,
    out_ref, sems,
):
    sides, faces = take_values(4, shi_ref, fhi_ref, slow_ref, flow_ref, msg_in_ref, low_ref, upp_ref, 8)
    copies = []
    for f in range(4):
        held = w_in_ref[...] if f == 0 else w_m_ref[f - 1]
        w = add_back(chunks_of(held), sides[f], faces[f])
        applied = permute(back_ref[...], assemble_local(w))
        for c in range(4):
            lanes = slice(128 * c, 128 * c + 128)
            value = applied[c]
            if f == 0:
                value = base_ref[:, lanes] + 2.0 * RHO_NEXT / CHEB_DELTA * jacobi_ref[:, lanes] * (
                    res_ref[:, lanes] - value
                )
            out_ref[f, :, lanes] = value
        copy = pltpu.make_async_copy(out_ref.at[f], pressure_h if f == 0 else momentum_h.at[f - 1], sems.at[f])
        copy.start()
        copies.append(copy)
    for copy in copies:
        copy.wait()


def shape(*dims, dtype=F32):
    return jax.ShapeDtypeStruct(dims, dtype)


def in_vmem():
    return pl.BlockSpec(memory_space=pltpu.VMEM)


def in_hbm():
    return pl.BlockSpec(memory_space=pltpu.HBM)


def call(kernel, outs, args, scratch=(), name=None, args_hbm=False, outs_hbm=False):
    if args_hbm:
        args = [pltpu.with_memory_space_constraint(x, pltpu.HBM) for x in args]
    return pl.pallas_call(
        kernel,
        out_shape=outs,
        in_specs=[in_hbm() if args_hbm else in_vmem() for _ in args],
        out_specs=[in_hbm() if outs_hbm else in_vmem() for _ in outs],
        scratch_shapes=list(scratch),
        compiler_params=pltpu.CompilerParams(vmem_limit_bytes=VMEM_LIMIT),
        name=name,
    )(*args)


def like(x):
    return jax.ShapeDtypeStruct(x.shape, x.dtype)


def run_first(conn, peer, slot, node, counts, axial, pressure, geom, later):
    fwd, bwd, coef = [jnp.asarray(t) for t in const_tables()]
    held = [conn, peer, slot, node, counts, axial, fwd, bwd]
    outs = call(
        first_kernel,
        [shape(64, 128), shape(16, 128), shape(16, 128), shape(64, 512), shape(64, 128, dtype=I32),
         shape(32, 128, dtype=I32), shape(128, 8192, dtype=BF16), shape(128, 4096, dtype=BF16),
         shape(64, 192, dtype=BF16), shape(64, 192, dtype=BF16), shape(768, 256, dtype=BF16), shape(768, 128, dtype=BF16),
         like(coef), like(pressure), like(geom), *[like(x) for x in later]],
        [conn, peer, slot, node, counts, axial, pressure, geom, fwd, bwd, coef, *later],
        [*[pltpu.VMEM(x.shape, x.dtype) for x in held], pltpu.VMEM((32, 128), F32),
         pltpu.SemaphoreType.DMA((11 + len(later),))],
        "first",
        args_hbm=True,
    )
    return outs[:4], outs[4:8], outs[8:10], outs[10:13], outs[13:15], outs[15:]


def run_momentum(velocity, force, mass, metric, geom, tables, perm, lists):
    return call(
        momentum_kernel,
        [shape(192, 128), shape(48, 128), shape(48, 128), shape(3, 64, 512)],
        [velocity, force, mass, metric, geom, *tables, perm, *lists],
        name="momentum",
    )


def run_second(msg, low, upp, w, pressure, rhs, jacobi, geom, tables, perm, back, lists, msg_m, up_m, down_m):
    return call(
        second_kernel,
        [shape(256, 128), shape(64, 128), shape(64, 128), shape(64, 512), shape(64, 512), shape(64, 512)],
        [msg, low, upp, w, pressure, rhs, jacobi, geom, *tables, perm, back, *lists, msg_m, up_m, down_m],
        name="second",
    )


def run_last(msg, low, upp, w, w_m, jacobi, base, res, back, lists):
    return call(
        last_kernel,
        [shape(64, 512), shape(3, 64, 512)],
        [msg, low, upp, w, w_m, jacobi, base, res, back, *lists],
        [pltpu.VMEM((4, 64, 512), F32), pltpu.SemaphoreType.DMA((4,))],
        name="last",
        outs_hbm=True,
    )


def exchange(msg, up, down):
    rows = msg.shape[0] // 32
    arrived = lax.all_to_all(msg.reshape(32, rows, 128), ("gy", "gz"), split_axis=0, concat_axis=0, tiled=True)
    count = lax.axis_size("gx")
    from_low = lax.ppermute(up, "gx", [(i, (i + 1) % count) for i in range(count)])
    from_upp = lax.ppermute(down, "gx", [((i + 1) % count, i) for i in range(count)])
    return arrived.reshape(32 * rows, 128), from_low, from_upp


def on_device(
    pressure, rhs, jacobi, geom, velocity, force, mass, metric, conn, ent_peer, ent_slot, ent_node, counts, axial_nodes
):
    sent, lists, (perm, back), tables, (pressure, geom), later = run_first(
        conn, ent_peer, ent_slot, ent_node, counts, axial_nodes, pressure, geom,
        [velocity, force, mass, metric, rhs, jacobi],
    )
    velocity, force, mass, metric, rhs, jacobi = later
    msg, up, down, w = sent
    got = exchange(msg, up, down)
    msg_m, up_m, down_m, w_m = run_momentum(velocity, force, mass, metric, geom, tables, perm, lists)
    msg, up, down, w, base, res = run_second(
        *got, w, pressure, rhs, jacobi, geom, tables, perm, back, lists, msg_m, up_m, down_m
    )
    got = exchange(msg, up, down)
    return tuple(run_last(*got, w, w_m, jacobi, base, res, back, lists))


def solution(mesh):
    both = P(("gx", "gy", "gz"), None)
    three = P(None, ("gx", "gy", "gz"), None)
    return jax.shard_map(
        on_device,
        mesh=mesh,
        in_specs=(
            both, both, both, three, three, three, both, P(None, ("gx", "gy", "gz")), both, both, both, both, both,
            P(("gx", "gy", "gz"), None, None),
        ),
        out_specs=(both, three),
        check_vma=False,
    )
```

```python
import jax
import jax.numpy as jnp
import numpy as np
from jax import lax
from jax.experimental import pallas as pl
from jax.experimental.pallas import tpu as pltpu
from jax.sharding import PartitionSpec as P

F32 = jnp.float32
BF16 = jnp.bfloat16
I32 = jnp.int32

VISCOSITY = 0.2
CHEB_THETA = 1.1
CHEB_DELTA = 0.9
RHO_FIRST = 9.0 / 11.0
RHO_NEXT = 99.0 / 161.0

HI = 208
VMEM_LIMIT = 48 * 1024 * 1024


def deriv_table():
    points = np.array(
        [
            -1.0,
            -0.8717401485096066,
            -0.5917001814331423,
            -0.2092992179024789,
            0.2092992179024789,
            0.5917001814331423,
            0.8717401485096066,
            1.0,
        ]
    )
    before = np.ones(8)
    legendre = points.copy()
    for degree in range(1, 7):
        after = ((2 * degree + 1) * points * legendre - degree * before) / (degree + 1)
        before = legendre
        legendre = after
    spread = points[:, None] - points[None, :]
    safe = np.where(spread == 0.0, 1.0, spread)
    deriv = legendre[:, None] / (legendre[None, :] * safe)
    deriv = np.where(spread == 0.0, 0.0, deriv)
    deriv[0, 0] = -14.0
    deriv[7, 7] = 14.0
    return deriv


def const_tables():
    d32 = deriv_table().astype(np.float32)
    along_j = np.kron(np.eye(2), np.kron(d32, np.eye(8))).astype(np.float32)
    along_k = np.kron(np.eye(16), d32).astype(np.float32)
    fwd = np.concatenate([along_j.T, along_k.T], axis=1)
    bwd = np.concatenate([along_j, along_k], axis=0)
    coef = np.zeros((64, 128), np.float32)
    for way, mat in enumerate((d32, d32.T)):
        for to in range(4):
            for src in range(4):
                for half in range(2):
                    lanes = slice(64 * half, 64 * half + 64)
                    row = way * 32 + (to * 4 + src) * 2
                    coef[row, lanes] = mat[2 * to + half, 2 * src + half]
                    coef[row + 1, lanes] = mat[2 * to + half, 2 * src + 1 - half]
    return fwd, bwd, coef


def iota(shape, dim):
    return lax.broadcasted_iota(I32, shape, dim)


def split(x, count):
    parts = []
    for at in range(count):
        part = x.astype(BF16)
        parts.append(part)
        if at + 1 < count:
            x = x - part.astype(F32)
    return parts


def dot(a, b):
    return lax.dot_general(a, b, (((1,), (0,)), ((), ())), preferred_element_type=F32)


def dot_nt(a, b):
    return lax.dot_general(a, b, (((1,), (1,)), ((), ())), preferred_element_type=F32)


def one_hot(row, count):
    return (iota((count, row.shape[1]), 0) == row).astype(F32).astype(BF16)


def chunks_of(x):
    return [x[:, 128 * c : 128 * c + 128] for c in range(4)]


def along_i(chunks, coef_ref, way):
    turned = [pltpu.roll(x, 64, 1) for x in chunks]
    out = []
    for to in range(4):
        total = None
        for src in range(4):
            row = way * 32 + (to * 4 + src) * 2
            term = coef_ref[row : row + 1, :] * chunks[src] + coef_ref[row + 1 : row + 2, :] * turned[src]
            total = term if total is None else total + term
        out.append(total)
    return out


def grads(chunks, tab_f_ref, coef_ref):
    rows = chunks[0].shape[0]
    g_i = along_i(chunks, coef_ref, 0)
    h, m, l = split(jnp.concatenate(chunks, axis=0), 3)
    hm = jnp.concatenate([h, m], axis=1)
    hl = jnp.concatenate([h, l], axis=1)
    g_jk = dot(hm, tab_f_ref[0:256, :]) + (dot(hm, tab_f_ref[256:512, :]) + dot(hl, tab_f_ref[512:768, :]))
    g_j = [g_jk[rows * c : rows * c + rows, 0:128] for c in range(4)]
    g_k = [g_jk[rows * c : rows * c + rows, 128:256] for c in range(4)]
    return g_i, g_j, g_k


def divergence(u_i, u_j, u_k, tab_b_ref, coef_ref):
    rows = u_i[0].shape[0]
    out_i = along_i(u_i, coef_ref, 1)
    u = jnp.concatenate([jnp.concatenate(u_j, axis=0), jnp.concatenate(u_k, axis=0)], axis=1)
    h, m, l = split(u, 3)
    b_h = tab_b_ref[0:256, :]
    b_m = tab_b_ref[256:512, :]
    b_l = tab_b_ref[512:768, :]
    wide = jnp.concatenate([b_h, b_m], axis=1)
    both = dot(h, wide) + dot(m, wide)
    small = dot(h, b_l) + dot(l, b_h)
    total = both[:, 0:128] + (both[:, 128:256] + small)
    return [out_i[c] + total[rows * c : rows * c + rows] for c in range(4)]


def tiled(x, times):
    return x if times == 1 else jnp.concatenate([x] * times, axis=0)


def laplace(chunks, geom_ref, tab_f_ref, tab_b_ref, coef_ref):
    g_i, g_j, g_k = grads(chunks, tab_f_ref, coef_ref)
    geom = [chunks_of(geom_ref[a]) for a in range(3)]
    return divergence(
        [geom[0][c] * g_i[c] for c in range(4)],
        [geom[1][c] * g_j[c] for c in range(4)],
        [geom[2][c] * g_k[c] for c in range(4)],
        tab_b_ref,
        coef_ref,
    )


def permute(perm, chunks):
    parts = split(jnp.concatenate(chunks, axis=1), 3)
    return chunks_of(dot(perm, jnp.concatenate(parts, axis=0)))


def assemble_local(w):
    lane = iota((64, 128), 1)
    row = iota((64, 128), 0)
    bx = row & 7
    jj = (lane >> 3) & 7
    w = list(w)
    low = pltpu.roll(pltpu.roll(w[0], 64, 1), 63, 0)
    high = pltpu.roll(pltpu.roll(w[3], 64, 1), 1, 0)
    w[3] = w[3] + jnp.where((lane >= 64) & (bx < 7), low, 0.0)
    w[0] = w[0] + jnp.where((lane < 64) & (bx > 0), high, 0.0)
    out = []
    zero = jnp.zeros((8, 128), F32)
    for x in w:
        nxt = jnp.concatenate([pltpu.roll(x[8:64], 56, 1), zero], axis=0)
        prv = jnp.concatenate([zero, pltpu.roll(x[0:56], 72, 1)], axis=0)
        out.append(x + jnp.where(jj == 7, nxt, 0.0) + jnp.where(jj == 0, prv, 0.0))
    return out


def pack_sides(w):
    lane1 = iota((1, 128), 1)
    rows = [
        jnp.where(lane1 < 64, w[0][8 * by : 8 * by + 1], w[3][8 * by + 7 : 8 * by + 8]) for by in range(8)
    ]
    x_side = jnp.concatenate(rows, axis=0)
    jj = (iota((8, 128), 1) >> 3) & 7
    y_side = jnp.zeros((8, 128), F32)
    for c in range(4):
        y_side = jnp.where(jj == 2 * c, pltpu.roll(w[c][0:8], 16 * c, 1), y_side)
        y_side = jnp.where(jj == 2 * c + 1, pltpu.roll(w[c][56:64], (16 * c - 48) % 128, 1), y_side)
    return jnp.concatenate([x_side, y_side], axis=0)


def pack_faces(w):
    kk = iota((64, 128), 1) & 7
    face = jnp.zeros((64, 128), F32)
    for c in range(4):
        face = jnp.where(kk == 2 * c, pltpu.roll(w[c], 2 * c, 1), face)
        face = jnp.where(kk == 2 * c + 1, pltpu.roll(w[c], (2 * c - 6) % 128, 1), face)
    return face


def add_back(w, side, face):
    lane = iota((64, 128), 1)
    sub = iota((64, 128), 0) & 7
    kk = lane & 7
    jj = (iota((8, 128), 1) >> 3) & 7
    x_rows = jnp.concatenate(
        [jnp.broadcast_to(side[by : by + 1], (8, 128)) for by in range(8)], axis=0
    )
    y_side = side[8:16]
    out = []
    for c in range(4):
        x = w[c]
        if c == 0:
            x = x + jnp.where((sub == 0) & (lane < 64), x_rows, 0.0)
        if c == 3:
            x = x + jnp.where((sub == 7) & (lane >= 64), x_rows, 0.0)
        x = x + jnp.where(kk == 0, pltpu.roll(face, (-2 * c) % 128, 1), 0.0)
        x = x + jnp.where(kk == 7, pltpu.roll(face, (6 - 2 * c) % 128, 1), 0.0)
        first = x[0:8] + jnp.where(jj == 0, pltpu.roll(y_side, (-16 * c) % 128, 1), 0.0)
        last = x[56:64] + jnp.where(jj == 7, pltpu.roll(y_side, (48 - 16 * c) % 128, 1), 0.0)
        out.append(jnp.concatenate([first, x[8:56], last], axis=0))
    return out


def block_row(block):
    return jnp.concatenate([block[t : t + 1] for t in range(8)], axis=1)


def gather_tables(tables, hi_block, lows, hi_count):
    parts = []
    for table in tables:
        parts += split(table, 2)
    got = dot(jnp.concatenate(parts, axis=0), lows)
    mask = iota((hi_count, 1024), 0) == block_row(hi_block)
    out = []
    for at in range(len(tables)):
        both = got[2 * at * hi_count : (2 * at + 1) * hi_count] + got[(2 * at + 1) * hi_count : (2 * at + 2) * hi_count]
        out.append(jnp.sum(jnp.where(mask, both, 0.0), axis=0, keepdims=True))
    return out


def scatter_tables(rows, hi_block, lows, hi_count):
    mask = iota((hi_count, 1024), 0) == block_row(hi_block)
    parts = []
    for values in rows:
        for part in split(values, 2):
            spread = jnp.broadcast_to(part.astype(F32), (hi_count, 1024))
            parts.append(jnp.where(mask, spread, 0.0).astype(BF16))
    return dot_nt(jnp.concatenate(parts, axis=0), lows)


def build_lows(slo_ref, flo_ref, slow_ref, flow_ref):
    for g in range(8):
        slow_ref[:, lanes_of(g)] = one_hot(block_row(slo_ref[rows_of(g), :]), 128)
    for g in range(4):
        flow_ref[:, lanes_of(g)] = one_hot(block_row(flo_ref[rows_of(g), :]), 128)


def lanes_of(g):
    return slice(1024 * g, 1024 * g + 1024)


def rows_of(g):
    return slice(8 * g, 8 * g + 8)


def send_values(local_fields, shi_ref, fhi_ref, slow_ref, flow_ref, msg_ref, up_ref, down_ref, stride):
    sides = [pack_sides(w) for w in local_fields]
    faces = [pack_faces(w) for w in local_fields]
    for g in range(8):
        got = gather_tables(sides, shi_ref[rows_of(g), :], slow_ref[:, lanes_of(g)], 16)
        for f, values in enumerate(got):
            for t in range(8):
                at = (8 * g + t) // 2 * stride + 2 * f + t % 2
                msg_ref[at : at + 1, :] = values[:, 128 * t : 128 * t + 128]
    for g in range(4):
        got = gather_tables(faces, fhi_ref[rows_of(g), :], flow_ref[:, lanes_of(g)], 64)
        out_ref = down_ref if g < 2 else up_ref
        for f, values in enumerate(got):
            for t in range(8):
                at = 16 * f + 8 * (g % 2) + t
                out_ref[at : at + 1, :] = values[:, 128 * t : 128 * t + 128]


def take_values(count, shi_ref, fhi_ref, slow_ref, flow_ref, msg_ref, low_ref, upp_ref, stride):
    side = None
    for g in range(8):
        rows = []
        for f in range(count):
            cells = []
            for t in range(8):
                at = (8 * g + t) // 2 * stride + 2 * f + t % 2
                cells.append(msg_ref[at : at + 1, :])
            rows.append(jnp.concatenate(cells, axis=1))
        part = scatter_tables(rows, shi_ref[rows_of(g), :], slow_ref[:, lanes_of(g)], 16)
        side = part if side is None else side + part
    face = None
    for g in range(4):
        ref = low_ref if g < 2 else upp_ref
        rows = [block_row(ref[16 * f + 8 * (g % 2) : 16 * f + 8 * (g % 2) + 8, :]) for f in range(count)]
        part = scatter_tables(rows, fhi_ref[rows_of(g), :], flow_ref[:, lanes_of(g)], 64)
        face = part if face is None else face + part
    sides = [side[32 * f : 32 * f + 16] + side[32 * f + 16 : 32 * f + 32] for f in range(count)]
    faces = [face[128 * f : 128 * f + 64] + face[128 * f + 64 : 128 * f + 128] for f in range(count)]
    return sides, faces


def chain_place(left):
    eye = (iota((64, 64), 0) == iota((64, 64), 1)).astype(F32)
    l1 = left.astype(BF16)
    l2 = dot(l1, l1)
    m1 = eye + left
    l2b = l2.astype(BF16)
    l4 = dot(l2b, l2b)
    m2 = m1 + dot(l2b, m1.astype(BF16))
    m4 = m2 + dot(l4.astype(BF16), m2.astype(BF16))
    return jnp.sum(m4, axis=1, keepdims=True) - 1.0


def brick_places(conn):
    same = iota((64, 64), 0) == iota((64, 64), 1)

    def as_row(col):
        return jnp.sum(jnp.where(same, col, 0), axis=0, keepdims=True)

    end_x = as_row(conn[:, 475:476])
    end_y = as_row(conn[:, 251:252])
    left_x = (conn[:, 27:28] == end_x).astype(F32)
    left_y = (conn[:, 195:196] == end_y).astype(F32)
    return (chain_place(left_y) * 8.0 + chain_place(left_x)).astype(I32)


def place_table(hi, lo, count):
    lane = 1.0 + iota((128, 128), 1).astype(F32) * (1.0 / 128.0)
    total = None
    for g in range(count // 8):
        top = one_hot(block_row(hi[rows_of(g)]), HI)
        low = []
        for t in range(8):
            hit = iota((128, 128), 0) == lo[8 * g + t : 8 * g + t + 1]
            low.append(jnp.where(hit, lane * (2.0 ** (8 * g + t - count // 2)), 0.0).astype(BF16))
        part = dot_nt(jnp.concatenate(low, axis=1), top)
        total = part if total is None else total + part
    return total.astype(BF16)


def look_up(table, row):
    got = dot(table, one_hot(row >> 7, HI))
    mask = iota((128, row.shape[1]), 0) == (row & 127)
    return jnp.sum(jnp.where(mask, got, 0.0), axis=0, keepdims=True)


def decode(x, count):
    x = x * (2.0 ** (count // 2))
    row = jnp.zeros(x.shape, I32)
    jump = count // 2
    while jump:
        big = x >= 2.0**jump
        row = row + jnp.where(big, jump, 0)
        x = jnp.where(big, x * (2.0**-jump), x)
        jump //= 2
    return row, (x * 128.0).astype(I32) - 128


def put_rows(ref, at, values):
    for t in range(8):
        ref[at + t : at + t + 1, :] = values[:, 128 * t : 128 * t + 128]


def build_perm(conn, perm_ref, back_ref):
    place = brick_places(conn)
    lane3 = iota((64, 192), 1) & 63
    place_row = jnp.sum(jnp.where(lane3 == iota((64, 192), 0), place, 0), axis=0, keepdims=True)
    perm_ref[...] = (iota((64, 192), 0) == place_row).astype(F32).astype(BF16)
    back_ref[...] = (lane3 == place).astype(F32).astype(BF16)


def node_places(conn, perm):
    ids = jnp.concatenate([(conn >> 7).astype(F32), (conn & 127).astype(F32)], axis=1).astype(BF16)
    ids = dot(perm, ids)
    hi_c = chunks_of(ids[:, 0:512])
    lo_c = chunks_of(ids[:, 512:1024])
    lane8 = iota((16, 128), 1)
    row8 = iota((16, 128), 0)
    in_x = (((lane8 >> 3) & 7) < 7) | (row8 == 7)
    i_y = 2 * (((lane8 >> 3) & 7) >> 1) + (lane8 >> 6)
    in_y = (i_y < 7) & ((row8 > 8) | (i_y > 0))
    keep_s = ((row8 < 8) & in_x) | ((row8 >= 8) & in_y)
    lane = iota((64, 128), 1)
    row = iota((64, 128), 0)
    i_f = 2 * ((lane & 7) >> 1) + (lane >> 6)
    keep_f = ((i_f < 7) | ((row & 7) == 7)) & ((((lane >> 3) & 7) < 7) | ((row >> 3) == 7))
    table_s = place_table(
        jnp.where(keep_s, pack_sides(hi_c), -1.0).astype(I32), pack_sides(lo_c).astype(I32), 16
    )
    table_f = place_table(
        jnp.where(keep_f, pack_faces(hi_c), -1.0).astype(I32), pack_faces(lo_c).astype(I32), 64
    )
    return table_s, table_f


def side_lists(table_s, peer_ref, slot_ref, node_ref, counts, shi_ref, slo_ref):
    total = None
    for g in range(8):
        at = lanes_of(g)
        slot = slot_ref[:, at]
        places = look_up(table_s, node_ref[:, at])
        hit = iota((64, 1024), 0) == (peer_ref[:, at] * 2 + (slot >> 7))
        part = dot_nt(jnp.where(hit, places, 0.0).astype(BF16), one_hot(slot & 127, 128))
        total = part if total is None else total + part
    row, lane = decode(total, 16)
    limit = jnp.sum(jnp.where(iota((64, 32), 1) == (iota((64, 32), 0) >> 1), counts, 0), axis=1, keepdims=True)
    slots = (iota((64, 128), 0) & 1) * 128 + iota((64, 128), 1)
    shi_ref[...] = jnp.where(slots < limit, row, -1)
    slo_ref[...] = lane


def face_lists(table_f, axial_ref, coded_ref, fhi_ref, flo_ref):
    for g in range(4):
        put_rows(coded_ref, 8 * g, look_up(table_f, axial_ref[0, g // 2 : g // 2 + 1, lanes_of(g % 2)]))
    row, lane = decode(coded_ref[...], 64)
    fhi_ref[...] = row
    flo_ref[...] = lane


def first_kernel(*refs):
    (conn_h, peer_h, slot_h, node_h, counts_h, axial_h, pressure_h, geom_h, fwd_h, bwd_h, coef_h) = refs[:11]
    later_h = refs[11:17]
    (msg_ref, up_ref, down_ref, w_ref, shi_ref, fhi_ref, slo_ref, flo_ref, perm_ref, back_ref) = refs[17:27]
    (tab_f_ref, tab_b_ref, coef_ref, pressure_ref, geom_ref) = refs[27:32]
    later = refs[32:38]
    (conn_ref, peer_ref, slot_ref, node_ref, counts_ref, axial_ref, fwd_ref, bwd_ref, coded_ref, slow_ref, flow_ref, sems) = (
        refs[38:]
    )
    pairs = [
        (conn_h, conn_ref), (pressure_h, pressure_ref), (fwd_h, fwd_ref), (bwd_h, bwd_ref), (coef_h, coef_ref),
        (geom_h, geom_ref), (node_h, node_ref), (peer_h, peer_ref), (slot_h, slot_ref), (counts_h, counts_ref),
        (axial_h, axial_ref), *zip(later_h, later),
    ]
    copies = [pltpu.make_async_copy(src, dst, sems.at[at]) for at, (src, dst) in enumerate(pairs)]
    for copy in copies:
        copy.start()
    copies[0].wait()
    conn = conn_ref[...]
    build_perm(conn, perm_ref, back_ref)
    for copy in copies[1:11]:
        copy.wait()
    fh, fm, fl = split(fwd_ref[...], 3)
    for at, part in enumerate([fh, fh, fm, fm, fl, fh]):
        tab_f_ref[128 * at : 128 * at + 128, :] = part
    for at, part in enumerate(split(bwd_ref[...], 3)):
        tab_b_ref[256 * at : 256 * at + 256, :] = part
    table_s, table_f = node_places(conn, perm_ref[:, 0:64])
    out = laplace(chunks_of(pressure_ref[...]), geom_ref, tab_f_ref, tab_b_ref, coef_ref)
    w = permute(perm_ref[...], out)
    for c in range(4):
        w_ref[:, 128 * c : 128 * c + 128] = w[c]
    side_lists(table_s, peer_ref, slot_ref, node_ref, counts_ref[...], shi_ref, slo_ref)
    face_lists(table_f, axial_ref, coded_ref, fhi_ref, flo_ref)
    build_lows(slo_ref, flo_ref, slow_ref, flow_ref)
    send_values([assemble_local(w)], shi_ref, fhi_ref, slow_ref, flow_ref, msg_ref, up_ref, down_ref, 2)
    for copy in copies[11:]:
        copy.wait()


def momentum_kernel(
    velocity_ref, force_ref, mass_ref, metric_ref, geom_ref, tab_f_ref, tab_b_ref, coef_ref, perm_ref, shi_ref, fhi_ref,
    slo_ref, flo_ref,
    msg_ref, up_ref, down_ref, w_ref,
    slow_ref, flow_ref,
):
    build_lows(slo_ref, flo_ref, slow_ref, flow_ref)
    parts = [chunks_of(velocity_ref[a]) for a in range(3)]
    stacked = [jnp.concatenate([parts[a][c] for a in range(3)], axis=0) for c in range(4)]
    grad = grads(stacked, tab_f_ref, coef_ref)
    same = iota((64, 64), 0) == iota((64, 64), 1)
    scale = [jnp.sum(jnp.where(same, metric_ref[a : a + 1, :], 0.0), axis=1, keepdims=True) for a in range(3)]
    convect = []
    flux = [[], [], []]
    for c in range(4):
        total = None
        for a in range(3):
            speed = tiled(scale[a] * parts[a][c], 3)
            term = speed * grad[a][c]
            total = term if total is None else total + term
            flux[a].append(tiled(geom_ref[a, :, 128 * c : 128 * c + 128], 3) * grad[a][c])
        convect.append(total)
    diffuse = divergence(flux[0], flux[1], flux[2], tab_b_ref, coef_ref)
    fields = []
    for f in range(3):
        rows = slice(64 * f, 64 * f + 64)
        out = []
        for c in range(4):
            lanes = slice(128 * c, 128 * c + 128)
            out.append(
                mass_ref[:, lanes] * (force_ref[f, :, lanes] - convect[c][rows]) - VISCOSITY * diffuse[c][rows]
            )
        w = permute(perm_ref[...], out)
        for c in range(4):
            w_ref[f, :, 128 * c : 128 * c + 128] = w[c]
        fields.append(assemble_local(w))
    send_values(fields, shi_ref, fhi_ref, slow_ref, flow_ref, msg_ref, up_ref, down_ref, 6)


def second_kernel(
    msg_in_ref, low_ref, upp_ref, w_in_ref, pressure_ref, rhs_ref, jacobi_ref, geom_ref, tab_f_ref, tab_b_ref, coef_ref,
    perm_ref, back_ref, shi_ref, fhi_ref, slo_ref, flo_ref, msg_m_ref, up_m_ref, down_m_ref,
    msg_ref, up_ref, down_ref, w_ref, base_ref, res_ref,
    slow_ref, flow_ref,
):
    build_lows(slo_ref, flo_ref, slow_ref, flow_ref)
    sides, faces = take_values(1, shi_ref, fhi_ref, slow_ref, flow_ref, msg_in_ref, low_ref, upp_ref, 2)
    w = add_back(chunks_of(w_in_ref[...]), sides[0], faces[0])
    applied = permute(back_ref[...], assemble_local(w))
    step = []
    for c in range(4):
        lanes = slice(128 * c, 128 * c + 128)
        jac = jacobi_ref[:, lanes]
        res = rhs_ref[:, lanes] - applied[c]
        step.append(jac * res / CHEB_THETA)
        first = pressure_ref[:, lanes] + step[c]
        base_ref[:, lanes] = first + RHO_NEXT * RHO_FIRST * step[c]
        res_ref[:, lanes] = res
    out = laplace(step, geom_ref, tab_f_ref, tab_b_ref, coef_ref)
    w = permute(perm_ref[...], out)
    for c in range(4):
        w_ref[:, 128 * c : 128 * c + 128] = w[c]
    send_values([assemble_local(w)], shi_ref, fhi_ref, slow_ref, flow_ref, msg_ref, up_ref, down_ref, 8)
    for peer in range(32):
        msg_ref[8 * peer + 2 : 8 * peer + 8, :] = msg_m_ref[6 * peer : 6 * peer + 6, :]
    up_ref[16:64, :] = up_m_ref[...]
    down_ref[16:64, :] = down_m_ref[...]


def last_kernel(
    msg_in_ref, low_ref, upp_ref, w_in_ref, w_m_ref, jacobi_ref, base_ref, res_ref, back_ref, shi_ref, fhi_ref, slo_ref,
    flo_ref,
    pressure_h, momentum_h,
    out_ref, slow_ref, flow_ref, sems,
):
    build_lows(slo_ref, flo_ref, slow_ref, flow_ref)
    sides, faces = take_values(4, shi_ref, fhi_ref, slow_ref, flow_ref, msg_in_ref, low_ref, upp_ref, 8)
    copies = []
    for f in range(4):
        held = w_in_ref[...] if f == 0 else w_m_ref[f - 1]
        w = add_back(chunks_of(held), sides[f], faces[f])
        applied = permute(back_ref[...], assemble_local(w))
        for c in range(4):
            lanes = slice(128 * c, 128 * c + 128)
            value = applied[c]
            if f == 0:
                value = base_ref[:, lanes] + 2.0 * RHO_NEXT / CHEB_DELTA * jacobi_ref[:, lanes] * (
                    res_ref[:, lanes] - value
                )
            out_ref[f, :, lanes] = value
        copy = pltpu.make_async_copy(out_ref.at[f], pressure_h if f == 0 else momentum_h.at[f - 1], sems.at[f])
        copy.start()
        copies.append(copy)
    for copy in copies:
        copy.wait()


def shape(*dims, dtype=F32):
    return jax.ShapeDtypeStruct(dims, dtype)


def in_vmem():
    return pl.BlockSpec(memory_space=pltpu.VMEM)


def in_hbm():
    return pl.BlockSpec(memory_space=pltpu.HBM)


def call(kernel, outs, args, scratch=(), name=None, args_hbm=False, outs_hbm=False):
    if args_hbm:
        args = [pltpu.with_memory_space_constraint(x, pltpu.HBM) for x in args]
    return pl.pallas_call(
        kernel,
        out_shape=outs,
        in_specs=[in_hbm() if args_hbm else in_vmem() for _ in args],
        out_specs=[in_hbm() if outs_hbm else in_vmem() for _ in outs],
        scratch_shapes=list(scratch),
        compiler_params=pltpu.CompilerParams(vmem_limit_bytes=VMEM_LIMIT),
        name=name,
    )(*args)


def lows():
    return [pltpu.VMEM((128, 8192), BF16), pltpu.VMEM((128, 4096), BF16)]


def like(x):
    return jax.ShapeDtypeStruct(x.shape, x.dtype)


def run_first(conn, peer, slot, node, counts, axial, pressure, geom, later):
    fwd, bwd, coef = [jnp.asarray(t) for t in const_tables()]
    held = [conn, peer, slot, node, counts, axial, fwd, bwd]
    outs = call(
        first_kernel,
        [shape(64, 128), shape(16, 128), shape(16, 128), shape(64, 512), shape(64, 128, dtype=I32),
         shape(32, 128, dtype=I32), shape(64, 128, dtype=I32), shape(32, 128, dtype=I32),
         shape(64, 192, dtype=BF16), shape(64, 192, dtype=BF16), shape(768, 256, dtype=BF16), shape(768, 128, dtype=BF16),
         like(coef), like(pressure), like(geom), *[like(x) for x in later]],
        [conn, peer, slot, node, counts, axial, pressure, geom, fwd, bwd, coef, *later],
        [*[pltpu.VMEM(x.shape, x.dtype) for x in held], pltpu.VMEM((32, 128), F32), *lows(),
         pltpu.SemaphoreType.DMA((11 + len(later),))],
        "first",
        args_hbm=True,
    )
    return outs[:4], outs[4:8], outs[8:10], outs[10:13], outs[13:15], outs[15:]


def run_momentum(velocity, force, mass, metric, geom, tables, perm, lists):
    return call(
        momentum_kernel,
        [shape(192, 128), shape(48, 128), shape(48, 128), shape(3, 64, 512)],
        [velocity, force, mass, metric, geom, *tables, perm, *lists],
        lows(),
        name="momentum",
    )


def run_second(msg, low, upp, w, pressure, rhs, jacobi, geom, tables, perm, back, lists, msg_m, up_m, down_m):
    return call(
        second_kernel,
        [shape(256, 128), shape(64, 128), shape(64, 128), shape(64, 512), shape(64, 512), shape(64, 512)],
        [msg, low, upp, w, pressure, rhs, jacobi, geom, *tables, perm, back, *lists, msg_m, up_m, down_m],
        lows(),
        name="second",
    )


def run_last(msg, low, upp, w, w_m, jacobi, base, res, back, lists):
    return call(
        last_kernel,
        [shape(64, 512), shape(3, 64, 512)],
        [msg, low, upp, w, w_m, jacobi, base, res, back, *lists],
        [pltpu.VMEM((4, 64, 512), F32), *lows(), pltpu.SemaphoreType.DMA((4,))],
        name="last",
        outs_hbm=True,
    )


def exchange(msg, up, down):
    rows = msg.shape[0] // 32
    arrived = lax.all_to_all(msg.reshape(32, rows, 128), ("gy", "gz"), split_axis=0, concat_axis=0, tiled=True)
    count = lax.axis_size("gx")
    from_low = lax.ppermute(up, "gx", [(i, (i + 1) % count) for i in range(count)])
    from_upp = lax.ppermute(down, "gx", [((i + 1) % count, i) for i in range(count)])
    return arrived.reshape(32 * rows, 128), from_low, from_upp


def on_device(
    pressure, rhs, jacobi, geom, velocity, force, mass, metric, conn, ent_peer, ent_slot, ent_node, counts, axial_nodes
):
    sent, lists, (perm, back), tables, (pressure, geom), later = run_first(
        conn, ent_peer, ent_slot, ent_node, counts, axial_nodes, pressure, geom,
        [velocity, force, mass, metric, rhs, jacobi],
    )
    velocity, force, mass, metric, rhs, jacobi = later
    msg, up, down, w = sent
    got = exchange(msg, up, down)
    msg_m, up_m, down_m, w_m = run_momentum(velocity, force, mass, metric, geom, tables, perm, lists)
    msg, up, down, w, base, res = run_second(
        *got, w, pressure, rhs, jacobi, geom, tables, perm, back, lists, msg_m, up_m, down_m
    )
    got = exchange(msg, up, down)
    return tuple(run_last(*got, w, w_m, jacobi, base, res, back, lists))


def solution(mesh):
    both = P(("gx", "gy", "gz"), None)
    three = P(None, ("gx", "gy", "gz"), None)
    return jax.shard_map(
        on_device,
        mesh=mesh,
        in_specs=(
            both, both, both, three, three, three, both, P(None, ("gx", "gy", "gz")), both, both, both, both, both,
            P(("gx", "gy", "gz"), None, None),
        ),
        out_specs=(both, three),
        check_vma=False,
    )
```

```python
import jax
import jax.numpy as jnp
import numpy as np
from jax import lax
from jax.experimental import pallas as pl
from jax.experimental.pallas import tpu as pltpu
from jax.sharding import PartitionSpec as P

F32 = jnp.float32
BF16 = jnp.bfloat16
I32 = jnp.int32

VISCOSITY = 0.2
CHEB_THETA = 1.1
CHEB_DELTA = 0.9
RHO_FIRST = 9.0 / 11.0
RHO_NEXT = 99.0 / 161.0

HI = 208
VMEM_LIMIT = 48 * 1024 * 1024


def deriv_table():
    points = np.array(
        [
            -1.0,
            -0.8717401485096066,
            -0.5917001814331423,
            -0.2092992179024789,
            0.2092992179024789,
            0.5917001814331423,
            0.8717401485096066,
            1.0,
        ]
    )
    before = np.ones(8)
    legendre = points.copy()
    for degree in range(1, 7):
        after = ((2 * degree + 1) * points * legendre - degree * before) / (degree + 1)
        before = legendre
        legendre = after
    spread = points[:, None] - points[None, :]
    safe = np.where(spread == 0.0, 1.0, spread)
    deriv = legendre[:, None] / (legendre[None, :] * safe)
    deriv = np.where(spread == 0.0, 0.0, deriv)
    deriv[0, 0] = -14.0
    deriv[7, 7] = 14.0
    return deriv


def const_tables():
    d32 = deriv_table().astype(np.float32)
    along_j = np.kron(np.eye(2), np.kron(d32, np.eye(8))).astype(np.float32)
    along_k = np.kron(np.eye(16), d32).astype(np.float32)
    fwd = np.concatenate([along_j.T, along_k.T], axis=1)
    bwd = np.concatenate([along_j, along_k], axis=0)
    coef = np.zeros((64, 128), np.float32)
    for way, mat in enumerate((d32, d32.T)):
        for to in range(4):
            for src in range(4):
                for half in range(2):
                    lanes = slice(64 * half, 64 * half + 64)
                    row = way * 32 + (to * 4 + src) * 2
                    coef[row, lanes] = mat[2 * to + half, 2 * src + half]
                    coef[row + 1, lanes] = mat[2 * to + half, 2 * src + 1 - half]
    return fwd, bwd, coef


def iota(shape, dim):
    return lax.broadcasted_iota(I32, shape, dim)


def split(x, count):
    parts = []
    for at in range(count):
        part = x.astype(BF16)
        parts.append(part)
        if at + 1 < count:
            x = x - part.astype(F32)
    return parts


def dot(a, b):
    return lax.dot_general(a, b, (((1,), (0,)), ((), ())), preferred_element_type=F32)


def dot_nt(a, b):
    return lax.dot_general(a, b, (((1,), (1,)), ((), ())), preferred_element_type=F32)


def repeat_row(row, count):
    pair = jnp.broadcast_to(row.astype(F32), (16, row.shape[1])).astype(BF16)
    return jnp.concatenate([pair] * (count // 16), axis=0)


def marks(row, count):
    base = iota((count, 128), 0).astype(F32).astype(BF16)
    return jnp.concatenate([base] * (row.shape[1] // 128), axis=1) == repeat_row(row, count)


def choose(mask, value):
    return jnp.where(mask, value, jnp.zeros(mask.shape, BF16))


def one_hot(row, count):
    return choose(marks(row, count), jnp.ones((count, row.shape[1]), BF16))


def chunks_of(x):
    return [x[:, 128 * c : 128 * c + 128] for c in range(4)]


def along_i(chunks, coef_ref, way):
    turned = [pltpu.roll(x, 64, 1) for x in chunks]
    out = []
    for to in range(4):
        total = None
        for src in range(4):
            row = way * 32 + (to * 4 + src) * 2
            term = coef_ref[row : row + 1, :] * chunks[src] + coef_ref[row + 1 : row + 2, :] * turned[src]
            total = term if total is None else total + term
        out.append(total)
    return out


def grads(chunks, tab_f_ref, coef_ref):
    rows = chunks[0].shape[0]
    g_i = along_i(chunks, coef_ref, 0)
    h, m, l = split(jnp.concatenate(chunks, axis=0), 3)
    hm = jnp.concatenate([h, m], axis=1)
    hl = jnp.concatenate([h, l], axis=1)
    g_jk = dot(hm, tab_f_ref[0:256, :]) + (dot(hm, tab_f_ref[256:512, :]) + dot(hl, tab_f_ref[512:768, :]))
    g_j = [g_jk[rows * c : rows * c + rows, 0:128] for c in range(4)]
    g_k = [g_jk[rows * c : rows * c + rows, 128:256] for c in range(4)]
    return g_i, g_j, g_k


def divergence(u_i, u_j, u_k, tab_b_ref, coef_ref):
    rows = u_i[0].shape[0]
    out_i = along_i(u_i, coef_ref, 1)
    u = jnp.concatenate([jnp.concatenate(u_j, axis=0), jnp.concatenate(u_k, axis=0)], axis=1)
    h, m, l = split(u, 3)
    b_h = tab_b_ref[0:256, :]
    b_m = tab_b_ref[256:512, :]
    b_l = tab_b_ref[512:768, :]
    wide = jnp.concatenate([b_h, b_m], axis=1)
    both = dot(h, wide) + dot(m, wide)
    small = dot(h, b_l) + dot(l, b_h)
    total = both[:, 0:128] + (both[:, 128:256] + small)
    return [out_i[c] + total[rows * c : rows * c + rows] for c in range(4)]


def tiled(x, times):
    return x if times == 1 else jnp.concatenate([x] * times, axis=0)


def laplace(chunks, geom_ref, tab_f_ref, tab_b_ref, coef_ref):
    g_i, g_j, g_k = grads(chunks, tab_f_ref, coef_ref)
    geom = [chunks_of(geom_ref[a]) for a in range(3)]
    return divergence(
        [geom[0][c] * g_i[c] for c in range(4)],
        [geom[1][c] * g_j[c] for c in range(4)],
        [geom[2][c] * g_k[c] for c in range(4)],
        tab_b_ref,
        coef_ref,
    )


def permute(perm, chunks):
    parts = split(jnp.concatenate(chunks, axis=1), 3)
    return chunks_of(dot(perm, jnp.concatenate(parts, axis=0)))


def assemble_local(w):
    lane = iota((64, 128), 1)
    row = iota((64, 128), 0)
    bx = row & 7
    jj = (lane >> 3) & 7
    w = list(w)
    low = pltpu.roll(pltpu.roll(w[0], 64, 1), 63, 0)
    high = pltpu.roll(pltpu.roll(w[3], 64, 1), 1, 0)
    w[3] = w[3] + jnp.where((lane >= 64) & (bx < 7), low, 0.0)
    w[0] = w[0] + jnp.where((lane < 64) & (bx > 0), high, 0.0)
    out = []
    zero = jnp.zeros((8, 128), F32)
    for x in w:
        nxt = jnp.concatenate([pltpu.roll(x[8:64], 56, 1), zero], axis=0)
        prv = jnp.concatenate([zero, pltpu.roll(x[0:56], 72, 1)], axis=0)
        out.append(x + jnp.where(jj == 7, nxt, 0.0) + jnp.where(jj == 0, prv, 0.0))
    return out


def pack_sides(w):
    lane1 = iota((1, 128), 1)
    rows = [
        jnp.where(lane1 < 64, w[0][8 * by : 8 * by + 1], w[3][8 * by + 7 : 8 * by + 8]) for by in range(8)
    ]
    x_side = jnp.concatenate(rows, axis=0)
    jj = (iota((8, 128), 1) >> 3) & 7
    y_side = jnp.zeros((8, 128), F32)
    for c in range(4):
        y_side = jnp.where(jj == 2 * c, pltpu.roll(w[c][0:8], 16 * c, 1), y_side)
        y_side = jnp.where(jj == 2 * c + 1, pltpu.roll(w[c][56:64], (16 * c - 48) % 128, 1), y_side)
    return jnp.concatenate([x_side, y_side], axis=0)


def pack_faces(w):
    kk = iota((32, 128), 1) & 7
    faces = []
    for k in (0, 7):
        face = jnp.zeros((32, 128), F32)
        for c in range(4):
            for h in range(2):
                face = jnp.where(
                    kk == 4 * h + c, pltpu.roll(w[c][32 * h : 32 * h + 32], (4 * h + c - k) % 128, 1), face
                )
        faces.append(face)
    return faces


def add_back(w, side, face):
    lane = iota((64, 128), 1)
    sub = iota((64, 128), 0) & 7
    kk = lane & 7
    jj = (iota((8, 128), 1) >> 3) & 7
    x_rows = jnp.concatenate(
        [jnp.broadcast_to(side[by : by + 1], (8, 128)) for by in range(8)], axis=0
    )
    y_side = side[8:16]
    out = []
    for c in range(4):
        x = w[c]
        if c == 0:
            x = x + jnp.where((sub == 0) & (lane < 64), x_rows, 0.0)
        if c == 3:
            x = x + jnp.where((sub == 7) & (lane >= 64), x_rows, 0.0)
        for k, part in zip((0, 7), face):
            spread = [pltpu.roll(part, (k - 4 * h - c) % 128, 1) for h in range(2)]
            x = x + jnp.where(kk == k, jnp.concatenate(spread, axis=0), 0.0)
        first = x[0:8] + jnp.where(jj == 0, pltpu.roll(y_side, (-16 * c) % 128, 1), 0.0)
        last = x[56:64] + jnp.where(jj == 7, pltpu.roll(y_side, (48 - 16 * c) % 128, 1), 0.0)
        out.append(jnp.concatenate([first, x[8:56], last], axis=0))
    return out


def block_row(block):
    return jnp.concatenate([block[t : t + 1] for t in range(8)], axis=1)


def gather_tables(tables, hi_block, lows, hi_count):
    parts = []
    for table in tables:
        parts += split(table, 2)
    got = dot(jnp.concatenate(parts, axis=0), lows)
    mask = iota((hi_count, 1024), 0) == block_row(hi_block)
    out = []
    for at in range(len(tables)):
        both = got[2 * at * hi_count : (2 * at + 1) * hi_count] + got[(2 * at + 1) * hi_count : (2 * at + 2) * hi_count]
        out.append(jnp.sum(jnp.where(mask, both, 0.0), axis=0, keepdims=True))
    return out


def scatter_tables(rows, hi_block, lows, hi_count):
    mask = marks(block_row(hi_block), hi_count)
    parts = []
    for values in rows:
        for part in split(values, 2):
            parts.append(choose(mask, repeat_row(part, hi_count)))
    return dot_nt(jnp.concatenate(parts, axis=0), lows)


def build_lows(slo_ref, flo_ref, slow_ref, flow_ref):
    for g in range(8):
        slow_ref[:, lanes_of(g)] = one_hot(block_row(slo_ref[rows_of(g), :]), 128)
    for g in range(4):
        flow_ref[:, lanes_of(g)] = one_hot(block_row(flo_ref[rows_of(g), :]), 128)


def lanes_of(g):
    return slice(1024 * g, 1024 * g + 1024)


def rows_of(g):
    return slice(8 * g, 8 * g + 8)


def send_values(local_fields, shi_ref, fhi_ref, slow_ref, flow_ref, msg_ref, up_ref, down_ref, stride):
    sides = [pack_sides(w) for w in local_fields]
    faces = [pack_faces(w) for w in local_fields]
    for g in range(8):
        got = gather_tables(sides, shi_ref[rows_of(g), :], slow_ref[:, lanes_of(g)], 16)
        for f, values in enumerate(got):
            for t in range(8):
                at = (8 * g + t) // 2 * stride + 2 * f + t % 2
                msg_ref[at : at + 1, :] = values[:, 128 * t : 128 * t + 128]
    for g in range(4):
        got = gather_tables([f[g // 2] for f in faces], fhi_ref[rows_of(g), :], flow_ref[:, lanes_of(g)], 32)
        out_ref = down_ref if g < 2 else up_ref
        for f, values in enumerate(got):
            for t in range(8):
                at = 16 * f + 8 * (g % 2) + t
                out_ref[at : at + 1, :] = values[:, 128 * t : 128 * t + 128]


def take_values(count, shi_ref, fhi_ref, slow_ref, flow_ref, msg_ref, low_ref, upp_ref, stride):
    side = None
    for g in range(8):
        rows = []
        for f in range(count):
            cells = []
            for t in range(8):
                at = (8 * g + t) // 2 * stride + 2 * f + t % 2
                cells.append(msg_ref[at : at + 1, :])
            rows.append(jnp.concatenate(cells, axis=1))
        part = scatter_tables(rows, shi_ref[rows_of(g), :], slow_ref[:, lanes_of(g)], 16)
        side = part if side is None else side + part
    face = [None, None]
    for g in range(4):
        ref = low_ref if g < 2 else upp_ref
        rows = [block_row(ref[16 * f + 8 * (g % 2) : 16 * f + 8 * (g % 2) + 8, :]) for f in range(count)]
        part = scatter_tables(rows, fhi_ref[rows_of(g), :], flow_ref[:, lanes_of(g)], 32)
        face[g // 2] = part if face[g // 2] is None else face[g // 2] + part
    sides = [side[32 * f : 32 * f + 16] + side[32 * f + 16 : 32 * f + 32] for f in range(count)]
    faces = [[x[64 * f : 64 * f + 32] + x[64 * f + 32 : 64 * f + 64] for x in face] for f in range(count)]
    return sides, faces


def chain_place(left):
    eye = (iota((64, 64), 0) == iota((64, 64), 1)).astype(F32)
    l1 = left.astype(BF16)
    l2 = dot(l1, l1)
    m1 = eye + left
    l2b = l2.astype(BF16)
    l4 = dot(l2b, l2b)
    m2 = m1 + dot(l2b, m1.astype(BF16))
    m4 = m2 + dot(l4.astype(BF16), m2.astype(BF16))
    return jnp.sum(m4, axis=1, keepdims=True) - 1.0


def brick_places(conn):
    same = iota((64, 64), 0) == iota((64, 64), 1)

    def as_row(col):
        return jnp.sum(jnp.where(same, col, 0), axis=0, keepdims=True)

    end_x = as_row(conn[:, 475:476])
    end_y = as_row(conn[:, 251:252])
    left_x = (conn[:, 27:28] == end_x).astype(F32)
    left_y = (conn[:, 195:196] == end_y).astype(F32)
    return (chain_place(left_y) * 8.0 + chain_place(left_x)).astype(I32)


def place_table(hi, lo, count):
    lane = 1.0 + iota((1, 128), 1).astype(F32) * (1.0 / 128.0)
    total = None
    for g in range(count // 8):
        top = one_hot(block_row(hi[rows_of(g)]), HI)
        low = []
        for t in range(8):
            hit = marks(lo[8 * g + t : 8 * g + t + 1], 128)
            low.append(choose(hit, repeat_row(lane * (2.0 ** (8 * g + t - count // 2)), 128)))
        part = dot_nt(jnp.concatenate(low, axis=1), top)
        total = part if total is None else total + part
    return total.astype(BF16)


def look_up(table, row):
    got = dot(table, one_hot(row >> 7, HI))
    mask = iota((128, row.shape[1]), 0) == (row & 127)
    return jnp.sum(jnp.where(mask, got, 0.0), axis=0, keepdims=True)


def decode(x, count):
    x = x * (2.0 ** (count // 2))
    row = jnp.zeros(x.shape, I32)
    jump = count // 2
    while jump:
        big = x >= 2.0**jump
        row = row + jnp.where(big, jump, 0)
        x = jnp.where(big, x * (2.0**-jump), x)
        jump //= 2
    return row, (x * 128.0).astype(I32) - 128


def put_rows(ref, at, values):
    for t in range(8):
        ref[at + t : at + t + 1, :] = values[:, 128 * t : 128 * t + 128]


def build_perm(conn, perm_ref, back_ref):
    place = brick_places(conn)
    lane3 = iota((64, 192), 1) & 63
    place_row = jnp.sum(jnp.where(lane3 == iota((64, 192), 0), place, 0), axis=0, keepdims=True)
    perm_ref[...] = (iota((64, 192), 0) == place_row).astype(F32).astype(BF16)
    back_ref[...] = (lane3 == place).astype(F32).astype(BF16)


def node_places(conn, perm):
    ids = jnp.concatenate([(conn >> 7).astype(F32), (conn & 127).astype(F32)], axis=1).astype(BF16)
    ids = dot(perm, ids)
    hi_c = chunks_of(ids[:, 0:512])
    lo_c = chunks_of(ids[:, 512:1024])
    lane8 = iota((16, 128), 1)
    row8 = iota((16, 128), 0)
    in_x = (((lane8 >> 3) & 7) < 7) | (row8 == 7)
    i_y = 2 * (((lane8 >> 3) & 7) >> 1) + (lane8 >> 6)
    in_y = (i_y < 7) & ((row8 > 8) | (i_y > 0))
    keep_s = ((row8 < 8) & in_x) | ((row8 >= 8) & in_y)
    lane = iota((32, 128), 1)
    row = iota((32, 128), 0) + 32 * ((lane >> 2) & 1)
    i_f = 2 * (lane & 3) + (lane >> 6)
    keep_f = ((i_f < 7) | ((row & 7) == 7)) & ((((lane >> 3) & 7) < 7) | ((row >> 3) == 7))
    table_s = place_table(
        jnp.where(keep_s, pack_sides(hi_c), -1.0).astype(I32), pack_sides(lo_c).astype(I32), 16
    )
    tables_f = [
        place_table(jnp.where(keep_f, hi, -1.0).astype(I32), lo.astype(I32), 32)
        for hi, lo in zip(pack_faces(hi_c), pack_faces(lo_c))
    ]
    return table_s, tables_f


def side_lists(table_s, peer_ref, slot_ref, node_ref, counts, shi_ref, slo_ref):
    total = None
    for g in range(8):
        at = lanes_of(g)
        slot = slot_ref[:, at]
        places = look_up(table_s, node_ref[:, at])
        hit = marks(peer_ref[:, at] * 2 + (slot >> 7), 64)
        part = dot_nt(choose(hit, repeat_row(places, 64)), one_hot(slot & 127, 128))
        total = part if total is None else total + part
    row, lane = decode(total, 16)
    limit = jnp.sum(jnp.where(iota((64, 32), 1) == (iota((64, 32), 0) >> 1), counts, 0), axis=1, keepdims=True)
    slots = (iota((64, 128), 0) & 1) * 128 + iota((64, 128), 1)
    shi_ref[...] = jnp.where(slots < limit, row, -1)
    slo_ref[...] = lane


def face_lists(tables_f, axial_ref, coded_ref, fhi_ref, flo_ref):
    for g in range(4):
        put_rows(coded_ref, 8 * g, look_up(tables_f[g // 2], axial_ref[0, g // 2 : g // 2 + 1, lanes_of(g % 2)]))
    row, lane = decode(coded_ref[...], 32)
    fhi_ref[...] = row
    flo_ref[...] = lane


def first_kernel(*refs):
    (conn_h, peer_h, slot_h, node_h, counts_h, axial_h, pressure_h, geom_h, fwd_h, bwd_h, coef_h) = refs[:11]
    later_h = refs[11:17]
    (msg_ref, up_ref, down_ref, w_ref, shi_ref, fhi_ref, slo_ref, flo_ref, perm_ref, back_ref) = refs[17:27]
    (tab_f_ref, tab_b_ref, coef_ref, pressure_ref, geom_ref) = refs[27:32]
    later = refs[32:38]
    (conn_ref, peer_ref, slot_ref, node_ref, counts_ref, axial_ref, fwd_ref, bwd_ref, coded_ref, slow_ref, flow_ref, sems) = (
        refs[38:]
    )
    pairs = [
        (conn_h, conn_ref), (pressure_h, pressure_ref), (fwd_h, fwd_ref), (bwd_h, bwd_ref), (coef_h, coef_ref),
        (geom_h, geom_ref), (node_h, node_ref), (peer_h, peer_ref), (slot_h, slot_ref), (counts_h, counts_ref),
        (axial_h, axial_ref), *zip(later_h, later),
    ]
    copies = [pltpu.make_async_copy(src, dst, sems.at[at]) for at, (src, dst) in enumerate(pairs)]
    for copy in copies:
        copy.start()
    copies[0].wait()
    conn = conn_ref[...]
    build_perm(conn, perm_ref, back_ref)
    for copy in copies[1:11]:
        copy.wait()
    fh, fm, fl = split(fwd_ref[...], 3)
    for at, part in enumerate([fh, fh, fm, fm, fl, fh]):
        tab_f_ref[128 * at : 128 * at + 128, :] = part
    for at, part in enumerate(split(bwd_ref[...], 3)):
        tab_b_ref[256 * at : 256 * at + 256, :] = part
    table_s, tables_f = node_places(conn, perm_ref[:, 0:64])
    out = laplace(chunks_of(pressure_ref[...]), geom_ref, tab_f_ref, tab_b_ref, coef_ref)
    w = permute(perm_ref[...], out)
    for c in range(4):
        w_ref[:, 128 * c : 128 * c + 128] = w[c]
    side_lists(table_s, peer_ref, slot_ref, node_ref, counts_ref[...], shi_ref, slo_ref)
    face_lists(tables_f, axial_ref, coded_ref, fhi_ref, flo_ref)
    build_lows(slo_ref, flo_ref, slow_ref, flow_ref)
    send_values([assemble_local(w)], shi_ref, fhi_ref, slow_ref, flow_ref, msg_ref, up_ref, down_ref, 2)
    for copy in copies[11:]:
        copy.wait()


def momentum_kernel(
    velocity_ref, force_ref, mass_ref, metric_ref, geom_ref, tab_f_ref, tab_b_ref, coef_ref, perm_ref, shi_ref, fhi_ref,
    slo_ref, flo_ref,
    msg_ref, up_ref, down_ref, w_ref,
    slow_ref, flow_ref,
):
    build_lows(slo_ref, flo_ref, slow_ref, flow_ref)
    parts = [chunks_of(velocity_ref[a]) for a in range(3)]
    stacked = [jnp.concatenate([parts[a][c] for a in range(3)], axis=0) for c in range(4)]
    grad = grads(stacked, tab_f_ref, coef_ref)
    same = iota((64, 64), 0) == iota((64, 64), 1)
    scale = [jnp.sum(jnp.where(same, metric_ref[a : a + 1, :], 0.0), axis=1, keepdims=True) for a in range(3)]
    convect = []
    flux = [[], [], []]
    for c in range(4):
        total = None
        for a in range(3):
            speed = tiled(scale[a] * parts[a][c], 3)
            term = speed * grad[a][c]
            total = term if total is None else total + term
            flux[a].append(tiled(geom_ref[a, :, 128 * c : 128 * c + 128], 3) * grad[a][c])
        convect.append(total)
    diffuse = divergence(flux[0], flux[1], flux[2], tab_b_ref, coef_ref)
    fields = []
    for f in range(3):
        rows = slice(64 * f, 64 * f + 64)
        out = []
        for c in range(4):
            lanes = slice(128 * c, 128 * c + 128)
            out.append(
                mass_ref[:, lanes] * (force_ref[f, :, lanes] - convect[c][rows]) - VISCOSITY * diffuse[c][rows]
            )
        w = permute(perm_ref[...], out)
        for c in range(4):
            w_ref[f, :, 128 * c : 128 * c + 128] = w[c]
        fields.append(assemble_local(w))
    send_values(fields, shi_ref, fhi_ref, slow_ref, flow_ref, msg_ref, up_ref, down_ref, 6)


def second_kernel(
    msg_in_ref, low_ref, upp_ref, w_in_ref, pressure_ref, rhs_ref, jacobi_ref, geom_ref, tab_f_ref, tab_b_ref, coef_ref,
    perm_ref, back_ref, shi_ref, fhi_ref, slo_ref, flo_ref, msg_m_ref, up_m_ref, down_m_ref,
    msg_ref, up_ref, down_ref, w_ref, base_ref, res_ref,
    slow_ref, flow_ref,
):
    build_lows(slo_ref, flo_ref, slow_ref, flow_ref)
    sides, faces = take_values(1, shi_ref, fhi_ref, slow_ref, flow_ref, msg_in_ref, low_ref, upp_ref, 2)
    w = add_back(chunks_of(w_in_ref[...]), sides[0], faces[0])
    applied = permute(back_ref[...], assemble_local(w))
    step = []
    for c in range(4):
        lanes = slice(128 * c, 128 * c + 128)
        jac = jacobi_ref[:, lanes]
        res = rhs_ref[:, lanes] - applied[c]
        step.append(jac * res / CHEB_THETA)
        first = pressure_ref[:, lanes] + step[c]
        base_ref[:, lanes] = first + RHO_NEXT * RHO_FIRST * step[c]
        res_ref[:, lanes] = res
    out = laplace(step, geom_ref, tab_f_ref, tab_b_ref, coef_ref)
    w = permute(perm_ref[...], out)
    for c in range(4):
        w_ref[:, 128 * c : 128 * c + 128] = w[c]
    send_values([assemble_local(w)], shi_ref, fhi_ref, slow_ref, flow_ref, msg_ref, up_ref, down_ref, 8)
    for peer in range(32):
        msg_ref[8 * peer + 2 : 8 * peer + 8, :] = msg_m_ref[6 * peer : 6 * peer + 6, :]
    up_ref[16:64, :] = up_m_ref[...]
    down_ref[16:64, :] = down_m_ref[...]


def last_kernel(
    msg_in_ref, low_ref, upp_ref, w_in_ref, w_m_ref, jacobi_ref, base_ref, res_ref, back_ref, shi_ref, fhi_ref, slo_ref,
    flo_ref,
    pressure_h, momentum_h,
    out_ref, slow_ref, flow_ref, sems,
):
    build_lows(slo_ref, flo_ref, slow_ref, flow_ref)
    sides, faces = take_values(4, shi_ref, fhi_ref, slow_ref, flow_ref, msg_in_ref, low_ref, upp_ref, 8)
    copies = []
    for f in range(4):
        held = w_in_ref[...] if f == 0 else w_m_ref[f - 1]
        w = add_back(chunks_of(held), sides[f], faces[f])
        applied = permute(back_ref[...], assemble_local(w))
        for c in range(4):
            lanes = slice(128 * c, 128 * c + 128)
            value = applied[c]
            if f == 0:
                value = base_ref[:, lanes] + 2.0 * RHO_NEXT / CHEB_DELTA * jacobi_ref[:, lanes] * (
                    res_ref[:, lanes] - value
                )
            out_ref[f, :, lanes] = value
        copy = pltpu.make_async_copy(out_ref.at[f], pressure_h if f == 0 else momentum_h.at[f - 1], sems.at[f])
        copy.start()
        copies.append(copy)
    for copy in copies:
        copy.wait()


def shape(*dims, dtype=F32):
    return jax.ShapeDtypeStruct(dims, dtype)


def in_vmem():
    return pl.BlockSpec(memory_space=pltpu.VMEM)


def in_hbm():
    return pl.BlockSpec(memory_space=pltpu.HBM)


def call(kernel, outs, args, scratch=(), name=None, args_hbm=False, outs_hbm=False):
    if args_hbm:
        args = [pltpu.with_memory_space_constraint(x, pltpu.HBM) for x in args]
    return pl.pallas_call(
        kernel,
        out_shape=outs,
        in_specs=[in_hbm() if args_hbm else in_vmem() for _ in args],
        out_specs=[in_hbm() if outs_hbm else in_vmem() for _ in outs],
        scratch_shapes=list(scratch),
        compiler_params=pltpu.CompilerParams(vmem_limit_bytes=VMEM_LIMIT),
        name=name,
    )(*args)


def lows():
    return [pltpu.VMEM((128, 8192), BF16), pltpu.VMEM((128, 4096), BF16)]


def like(x):
    return jax.ShapeDtypeStruct(x.shape, x.dtype)


def run_first(conn, peer, slot, node, counts, axial, pressure, geom, later):
    fwd, bwd, coef = [jnp.asarray(t) for t in const_tables()]
    held = [conn, peer, slot, node, counts, axial, fwd, bwd]
    outs = call(
        first_kernel,
        [shape(64, 128), shape(16, 128), shape(16, 128), shape(64, 512), shape(64, 128, dtype=I32),
         shape(32, 128, dtype=I32), shape(64, 128, dtype=I32), shape(32, 128, dtype=I32),
         shape(64, 192, dtype=BF16), shape(64, 192, dtype=BF16), shape(768, 256, dtype=BF16), shape(768, 128, dtype=BF16),
         like(coef), like(pressure), like(geom), *[like(x) for x in later]],
        [conn, peer, slot, node, counts, axial, pressure, geom, fwd, bwd, coef, *later],
        [*[pltpu.VMEM(x.shape, x.dtype) for x in held], pltpu.VMEM((32, 128), F32), *lows(),
         pltpu.SemaphoreType.DMA((11 + len(later),))],
        "first",
        args_hbm=True,
    )
    return outs[:4], outs[4:8], outs[8:10], outs[10:13], outs[13:15], outs[15:]


def run_momentum(velocity, force, mass, metric, geom, tables, perm, lists):
    return call(
        momentum_kernel,
        [shape(192, 128), shape(48, 128), shape(48, 128), shape(3, 64, 512)],
        [velocity, force, mass, metric, geom, *tables, perm, *lists],
        lows(),
        name="momentum",
    )


def run_second(msg, low, upp, w, pressure, rhs, jacobi, geom, tables, perm, back, lists, msg_m, up_m, down_m):
    return call(
        second_kernel,
        [shape(256, 128), shape(64, 128), shape(64, 128), shape(64, 512), shape(64, 512), shape(64, 512)],
        [msg, low, upp, w, pressure, rhs, jacobi, geom, *tables, perm, back, *lists, msg_m, up_m, down_m],
        lows(),
        name="second",
    )


def run_last(msg, low, upp, w, w_m, jacobi, base, res, back, lists):
    return call(
        last_kernel,
        [shape(64, 512), shape(3, 64, 512)],
        [msg, low, upp, w, w_m, jacobi, base, res, back, *lists],
        [pltpu.VMEM((4, 64, 512), F32), *lows(), pltpu.SemaphoreType.DMA((4,))],
        name="last",
        outs_hbm=True,
    )


def exchange(msg, up, down):
    rows = msg.shape[0] // 32
    arrived = lax.all_to_all(msg.reshape(32, rows, 128), ("gy", "gz"), split_axis=0, concat_axis=0, tiled=True)
    count = lax.axis_size("gx")
    from_low = lax.ppermute(up, "gx", [(i, (i + 1) % count) for i in range(count)])
    from_upp = lax.ppermute(down, "gx", [((i + 1) % count, i) for i in range(count)])
    return arrived.reshape(32 * rows, 128), from_low, from_upp


def on_device(
    pressure, rhs, jacobi, geom, velocity, force, mass, metric, conn, ent_peer, ent_slot, ent_node, counts, axial_nodes
):
    sent, lists, (perm, back), tables, (pressure, geom), later = run_first(
        conn, ent_peer, ent_slot, ent_node, counts, axial_nodes, pressure, geom,
        [velocity, force, mass, metric, rhs, jacobi],
    )
    velocity, force, mass, metric, rhs, jacobi = later
    msg, up, down, w = sent
    got = exchange(msg, up, down)
    msg_m, up_m, down_m, w_m = run_momentum(velocity, force, mass, metric, geom, tables, perm, lists)
    msg, up, down, w, base, res = run_second(
        *got, w, pressure, rhs, jacobi, geom, tables, perm, back, lists, msg_m, up_m, down_m
    )
    got = exchange(msg, up, down)
    return tuple(run_last(*got, w, w_m, jacobi, base, res, back, lists))


def solution(mesh):
    both = P(("gx", "gy", "gz"), None)
    three = P(None, ("gx", "gy", "gz"), None)
    return jax.shard_map(
        on_device,
        mesh=mesh,
        in_specs=(
            both, both, both, three, three, three, both, P(None, ("gx", "gy", "gz")), both, both, both, both, both,
            P(("gx", "gy", "gz"), None, None),
        ),
        out_specs=(both, three),
        check_vma=False,
    )
```

```python
import jax
import jax.numpy as jnp
import numpy as np
from jax import lax
from jax.experimental import pallas as pl
from jax.experimental.pallas import tpu as pltpu
from jax.sharding import PartitionSpec as P

F32 = jnp.float32
BF16 = jnp.bfloat16
I32 = jnp.int32

VISCOSITY = 0.2
CHEB_THETA = 1.1
CHEB_DELTA = 0.9
RHO_FIRST = 9.0 / 11.0
RHO_NEXT = 99.0 / 161.0

HI = 208
VMEM_LIMIT = 48 * 1024 * 1024


def deriv_table():
    points = np.array(
        [
            -1.0,
            -0.8717401485096066,
            -0.5917001814331423,
            -0.2092992179024789,
            0.2092992179024789,
            0.5917001814331423,
            0.8717401485096066,
            1.0,
        ]
    )
    before = np.ones(8)
    legendre = points.copy()
    for degree in range(1, 7):
        after = ((2 * degree + 1) * points * legendre - degree * before) / (degree + 1)
        before = legendre
        legendre = after
    spread = points[:, None] - points[None, :]
    safe = np.where(spread == 0.0, 1.0, spread)
    deriv = legendre[:, None] / (legendre[None, :] * safe)
    deriv = np.where(spread == 0.0, 0.0, deriv)
    deriv[0, 0] = -14.0
    deriv[7, 7] = 14.0
    return deriv


def const_tables():
    d32 = deriv_table().astype(np.float32)
    along_j = np.kron(np.eye(2), np.kron(d32, np.eye(8))).astype(np.float32)
    along_k = np.kron(np.eye(16), d32).astype(np.float32)
    fwd = np.concatenate([along_j.T, along_k.T], axis=1)
    bwd = np.concatenate([along_j, along_k], axis=0)
    coef = np.zeros((64, 128), np.float32)
    for way, mat in enumerate((d32, d32.T)):
        for to in range(4):
            for src in range(4):
                for half in range(2):
                    lanes = slice(64 * half, 64 * half + 64)
                    row = way * 32 + (to * 4 + src) * 2
                    coef[row, lanes] = mat[2 * to + half, 2 * src + half]
                    coef[row + 1, lanes] = mat[2 * to + half, 2 * src + 1 - half]
    return fwd, bwd, coef


def iota(shape, dim):
    return lax.broadcasted_iota(I32, shape, dim)


def split(x, count):
    parts = []
    for at in range(count):
        part = x.astype(BF16)
        parts.append(part)
        if at + 1 < count:
            x = x - part.astype(F32)
    return parts


def dot(a, b):
    return lax.dot_general(a, b, (((1,), (0,)), ((), ())), preferred_element_type=F32)


def dot_nt(a, b):
    return lax.dot_general(a, b, (((1,), (1,)), ((), ())), preferred_element_type=F32)


def repeat_row(row, count):
    pair = jnp.broadcast_to(row.astype(F32), (16, row.shape[1])).astype(BF16)
    return jnp.concatenate([pair] * (count // 16), axis=0)


def marks(row, count):
    base = iota((count, 128), 0).astype(F32).astype(BF16)
    return jnp.concatenate([base] * (row.shape[1] // 128), axis=1) == repeat_row(row, count)


def choose(mask, value):
    return jnp.where(mask, value, jnp.zeros(mask.shape, BF16))


def one_hot(row, count):
    return choose(marks(row, count), jnp.ones((count, row.shape[1]), BF16))


def chunks_of(x):
    return [x[:, 128 * c : 128 * c + 128] for c in range(4)]


def along_i(chunks, coef_ref, way):
    turned = [pltpu.roll(x, 64, 1) for x in chunks]
    out = []
    for to in range(4):
        total = None
        for src in range(4):
            row = way * 32 + (to * 4 + src) * 2
            term = coef_ref[row : row + 1, :] * chunks[src] + coef_ref[row + 1 : row + 2, :] * turned[src]
            total = term if total is None else total + term
        out.append(total)
    return out


def grads(chunks, tab_f_ref, coef_ref):
    rows = chunks[0].shape[0]
    g_i = along_i(chunks, coef_ref, 0)
    h, m, l = split(jnp.concatenate(chunks, axis=0), 3)
    hm = jnp.concatenate([h, m], axis=1)
    hl = jnp.concatenate([h, l], axis=1)
    g_jk = dot(hm, tab_f_ref[0:256, :]) + (dot(hm, tab_f_ref[256:512, :]) + dot(hl, tab_f_ref[512:768, :]))
    g_j = [g_jk[rows * c : rows * c + rows, 0:128] for c in range(4)]
    g_k = [g_jk[rows * c : rows * c + rows, 128:256] for c in range(4)]
    return g_i, g_j, g_k


def divergence(u_i, u_j, u_k, tab_b_ref, coef_ref):
    rows = u_i[0].shape[0]
    out_i = along_i(u_i, coef_ref, 1)
    u = jnp.concatenate([jnp.concatenate(u_j, axis=0), jnp.concatenate(u_k, axis=0)], axis=1)
    h, m, l = split(u, 3)
    b_h = tab_b_ref[0:256, :]
    b_m = tab_b_ref[256:512, :]
    b_l = tab_b_ref[512:768, :]
    wide = jnp.concatenate([b_h, b_m], axis=1)
    both = dot(h, wide) + dot(m, wide)
    small = dot(h, b_l) + dot(l, b_h)
    total = both[:, 0:128] + (both[:, 128:256] + small)
    return [out_i[c] + total[rows * c : rows * c + rows] for c in range(4)]


def tiled(x, times):
    return x if times == 1 else jnp.concatenate([x] * times, axis=0)


def laplace(chunks, geom_ref, tab_f_ref, tab_b_ref, coef_ref):
    g_i, g_j, g_k = grads(chunks, tab_f_ref, coef_ref)
    geom = [chunks_of(geom_ref[a]) for a in range(3)]
    return divergence(
        [geom[0][c] * g_i[c] for c in range(4)],
        [geom[1][c] * g_j[c] for c in range(4)],
        [geom[2][c] * g_k[c] for c in range(4)],
        tab_b_ref,
        coef_ref,
    )


def permute(perm, chunks):
    parts = split(jnp.concatenate(chunks, axis=1), 3)
    return chunks_of(dot(perm, jnp.concatenate(parts, axis=0)))


def assemble_local(w):
    lane = iota((64, 128), 1)
    row = iota((64, 128), 0)
    bx = row & 7
    jj = (lane >> 3) & 7
    w = list(w)
    low = pltpu.roll(pltpu.roll(w[0], 64, 1), 63, 0)
    high = pltpu.roll(pltpu.roll(w[3], 64, 1), 1, 0)
    w[3] = w[3] + jnp.where((lane >= 64) & (bx < 7), low, 0.0)
    w[0] = w[0] + jnp.where((lane < 64) & (bx > 0), high, 0.0)
    out = []
    zero = jnp.zeros((8, 128), F32)
    for x in w:
        nxt = jnp.concatenate([pltpu.roll(x[8:64], 56, 1), zero], axis=0)
        prv = jnp.concatenate([zero, pltpu.roll(x[0:56], 72, 1)], axis=0)
        out.append(x + jnp.where(jj == 7, nxt, 0.0) + jnp.where(jj == 0, prv, 0.0))
    return out


def pack_sides(w):
    lane1 = iota((1, 128), 1)
    rows = [
        jnp.where(lane1 < 64, w[0][8 * by : 8 * by + 1], w[3][8 * by + 7 : 8 * by + 8]) for by in range(8)
    ]
    x_side = jnp.concatenate(rows, axis=0)
    jj = (iota((8, 128), 1) >> 3) & 7
    y_side = jnp.zeros((8, 128), F32)
    for c in range(4):
        y_side = jnp.where(jj == 2 * c, pltpu.roll(w[c][0:8], 16 * c, 1), y_side)
        y_side = jnp.where(jj == 2 * c + 1, pltpu.roll(w[c][56:64], (16 * c - 48) % 128, 1), y_side)
    return jnp.concatenate([x_side, y_side], axis=0)


def pack_faces(w):
    kk = iota((32, 128), 1) & 7
    faces = []
    for k in (0, 7):
        face = jnp.zeros((32, 128), F32)
        for c in range(4):
            for h in range(2):
                face = jnp.where(
                    kk == 4 * h + c, pltpu.roll(w[c][32 * h : 32 * h + 32], (4 * h + c - k) % 128, 1), face
                )
        faces.append(face)
    return faces


def add_faces(w, face):
    kk = iota((64, 128), 1) & 7
    out = []
    for c in range(4):
        x = w[c]
        for k, part in zip((0, 7), face):
            spread = [pltpu.roll(part, (k - 4 * h - c) % 128, 1) for h in range(2)]
            x = x + jnp.where(kk == k, jnp.concatenate(spread, axis=0), 0.0)
        out.append(x)
    return out


def add_sides(w, side):
    lane = iota((64, 128), 1)
    sub = iota((64, 128), 0) & 7
    jj = (iota((8, 128), 1) >> 3) & 7
    x_rows = jnp.concatenate(
        [jnp.broadcast_to(side[by : by + 1], (8, 128)) for by in range(8)], axis=0
    )
    y_side = side[8:16]
    out = []
    for c in range(4):
        x = w[c]
        if c == 0:
            x = x + jnp.where((sub == 0) & (lane < 64), x_rows, 0.0)
        if c == 3:
            x = x + jnp.where((sub == 7) & (lane >= 64), x_rows, 0.0)
        first = x[0:8] + jnp.where(jj == 0, pltpu.roll(y_side, (-16 * c) % 128, 1), 0.0)
        last = x[56:64] + jnp.where(jj == 7, pltpu.roll(y_side, (48 - 16 * c) % 128, 1), 0.0)
        out.append(jnp.concatenate([first, x[8:56], last], axis=0))
    return out


def on_all_copies(side):
    lane = iota((8, 128), 1)
    row = iota((8, 128), 0)
    x_side, y_side = side[0:8], side[8:16]
    x_next = pltpu.roll(pltpu.roll(x_side, 56, 1), 7, 0)
    y_next = pltpu.roll(pltpu.roll(y_side, 112, 1), 7, 0)
    x_side = jnp.where((((lane >> 3) & 7) == 7) & (row < 7), x_next, x_side)
    y_side = jnp.where((lane >= 112) & (row < 7), y_next, y_side)
    return jnp.concatenate([x_side, y_side], axis=0)


def block_row(block):
    return jnp.concatenate([block[t : t + 1] for t in range(8)], axis=1)


def gather_tables(tables, hi_block, lows, hi_count):
    parts = []
    for table in tables:
        parts += split(table, 2)
    got = dot(jnp.concatenate(parts, axis=0), lows)
    mask = iota((hi_count, 1024), 0) == block_row(hi_block)
    out = []
    for at in range(len(tables)):
        both = got[2 * at * hi_count : (2 * at + 1) * hi_count] + got[(2 * at + 1) * hi_count : (2 * at + 2) * hi_count]
        out.append(jnp.sum(jnp.where(mask, both, 0.0), axis=0, keepdims=True))
    return out


def scatter_tables(rows, hi_block, lows, hi_count):
    mask = marks(block_row(hi_block), hi_count)
    parts = []
    for values in rows:
        for part in split(values, 2):
            parts.append(choose(mask, repeat_row(part, hi_count)))
    return dot_nt(jnp.concatenate(parts, axis=0), lows)


def build_low(lo_ref, low_ref):
    for g in range(lo_ref.shape[0] // 8):
        low_ref[:, lanes_of(g)] = one_hot(block_row(lo_ref[rows_of(g), :]), 128)


def build_lows(slo_ref, flo_ref, slow_ref, flow_ref):
    build_low(slo_ref, slow_ref)
    build_low(flo_ref, flow_ref)


def lanes_of(g):
    return slice(1024 * g, 1024 * g + 1024)


def rows_of(g):
    return slice(8 * g, 8 * g + 8)


def send_values(local_fields, shi_ref, fhi_ref, slow_ref, flow_ref, msg_ref, up_ref, down_ref, stride):
    sides = [pack_sides(w) for w in local_fields]
    faces = [pack_faces(w) for w in local_fields]
    for g in range(8):
        got = gather_tables(sides, shi_ref[rows_of(g), :], slow_ref[:, lanes_of(g)], 16)
        for f, values in enumerate(got):
            for t in range(8):
                at = (8 * g + t) // 2 * stride + 2 * f + t % 2
                msg_ref[at : at + 1, :] = values[:, 128 * t : 128 * t + 128]
    for g in range(4):
        got = gather_tables([f[g // 2] for f in faces], fhi_ref[rows_of(g), :], flow_ref[:, lanes_of(g)], 32)
        out_ref = down_ref if g < 2 else up_ref
        for f, values in enumerate(got):
            for t in range(8):
                at = 16 * f + 8 * (g % 2) + t
                out_ref[at : at + 1, :] = values[:, 128 * t : 128 * t + 128]


def take_sides(count, shi_ref, slow_ref, msg_ref, stride):
    side = None
    for g in range(8):
        rows = []
        for f in range(count):
            cells = []
            for t in range(8):
                at = (8 * g + t) // 2 * stride + 2 * f + t % 2
                cells.append(msg_ref[at : at + 1, :])
            rows.append(jnp.concatenate(cells, axis=1))
        part = scatter_tables(rows, shi_ref[rows_of(g), :], slow_ref[:, lanes_of(g)], 16)
        side = part if side is None else side + part
    return [side[32 * f : 32 * f + 16] + side[32 * f + 16 : 32 * f + 32] for f in range(count)]


def take_faces(count, fhi_ref, flow_ref, low_ref, upp_ref):
    face = [None, None]
    for g in range(4):
        ref = low_ref if g < 2 else upp_ref
        rows = [block_row(ref[16 * f + 8 * (g % 2) : 16 * f + 8 * (g % 2) + 8, :]) for f in range(count)]
        part = scatter_tables(rows, fhi_ref[rows_of(g), :], flow_ref[:, lanes_of(g)], 32)
        face[g // 2] = part if face[g // 2] is None else face[g // 2] + part
    return [[x[64 * f : 64 * f + 32] + x[64 * f + 32 : 64 * f + 64] for x in face] for f in range(count)]


def chain_place(left):
    eye = (iota((64, 64), 0) == iota((64, 64), 1)).astype(F32)
    l1 = left.astype(BF16)
    l2 = dot(l1, l1)
    m1 = eye + left
    l2b = l2.astype(BF16)
    l4 = dot(l2b, l2b)
    m2 = m1 + dot(l2b, m1.astype(BF16))
    m4 = m2 + dot(l4.astype(BF16), m2.astype(BF16))
    return jnp.sum(m4, axis=1, keepdims=True) - 1.0


def brick_places(conn):
    same = iota((64, 64), 0) == iota((64, 64), 1)

    def as_row(col):
        return jnp.sum(jnp.where(same, col, 0), axis=0, keepdims=True)

    end_x = as_row(conn[:, 475:476])
    end_y = as_row(conn[:, 251:252])
    left_x = (conn[:, 27:28] == end_x).astype(F32)
    left_y = (conn[:, 195:196] == end_y).astype(F32)
    return (chain_place(left_y) * 8.0 + chain_place(left_x)).astype(I32)


def place_table(hi, lo, count):
    lane = 1.0 + iota((1, 128), 1).astype(F32) * (1.0 / 128.0)
    total = None
    for g in range(count // 8):
        top = one_hot(block_row(hi[rows_of(g)]), HI)
        low = []
        for t in range(8):
            hit = marks(lo[8 * g + t : 8 * g + t + 1], 128)
            low.append(choose(hit, repeat_row(lane * (2.0 ** (8 * g + t - count // 2)), 128)))
        part = dot_nt(jnp.concatenate(low, axis=1), top)
        total = part if total is None else total + part
    return total.astype(BF16)


def look_up(table, row):
    got = choose(marks(row & 127, 128), dot(table, one_hot(row >> 7, HI)).astype(BF16))
    total = got[0:16]
    for at in range(1, 8):
        total = total + got[16 * at : 16 * at + 16]
    return jnp.sum(total.astype(F32), axis=0, keepdims=True)


def decode(x, count):
    x = x * (2.0 ** (count // 2))
    row = jnp.zeros(x.shape, I32)
    jump = count // 2
    while jump:
        big = x >= 2.0**jump
        row = row + jnp.where(big, jump, 0)
        x = jnp.where(big, x * (2.0**-jump), x)
        jump //= 2
    return row, (x * 128.0).astype(I32) - 128


def put_rows(ref, at, values):
    for t in range(8):
        ref[at + t : at + t + 1, :] = values[:, 128 * t : 128 * t + 128]


def build_perm(conn, perm_ref, back_ref):
    place = brick_places(conn)
    lane3 = iota((64, 192), 1) & 63
    place_row = jnp.sum(jnp.where(lane3 == iota((64, 192), 0), place, 0), axis=0, keepdims=True)
    perm_ref[...] = (iota((64, 192), 0) == place_row).astype(F32).astype(BF16)
    back_ref[...] = (lane3 == place).astype(F32).astype(BF16)


def node_places(conn, perm):
    ids = jnp.concatenate([(conn >> 7).astype(F32), (conn & 127).astype(F32)], axis=1).astype(BF16)
    ids = dot(perm, ids)
    hi_c = chunks_of(ids[:, 0:512])
    lo_c = chunks_of(ids[:, 512:1024])
    lane8 = iota((16, 128), 1)
    row8 = iota((16, 128), 0)
    in_x = (((lane8 >> 3) & 7) < 7) | (row8 == 7)
    i_y = 2 * (((lane8 >> 3) & 7) >> 1) + (lane8 >> 6)
    in_y = (i_y < 7) & ((row8 > 8) | (i_y > 0))
    keep_s = ((row8 < 8) & in_x) | ((row8 >= 8) & in_y)
    lane = iota((32, 128), 1)
    row = iota((32, 128), 0) + 32 * ((lane >> 2) & 1)
    i_f = 2 * (lane & 3) + (lane >> 6)
    keep_f = ((i_f < 7) | ((row & 7) == 7)) & ((((lane >> 3) & 7) < 7) | ((row >> 3) == 7))
    table_s = place_table(
        jnp.where(keep_s, pack_sides(hi_c), -1.0).astype(I32), pack_sides(lo_c).astype(I32), 16
    )
    tables_f = [
        place_table(jnp.where(keep_f, hi, -1.0).astype(I32), lo.astype(I32), 32)
        for hi, lo in zip(pack_faces(hi_c), pack_faces(lo_c))
    ]
    return table_s, tables_f


def side_lists(table_s, peer_ref, slot_ref, node_ref, counts, shi_ref, slo_ref):
    total = None
    for g in range(8):
        at = lanes_of(g)
        slot = slot_ref[:, at]
        places = look_up(table_s, node_ref[:, at])
        hit = marks(peer_ref[:, at] * 2 + (slot >> 7), 64)
        part = dot_nt(choose(hit, repeat_row(places, 64)), one_hot(slot & 127, 128))
        total = part if total is None else total + part
    row, lane = decode(total, 16)
    limit = jnp.sum(jnp.where(iota((64, 32), 1) == (iota((64, 32), 0) >> 1), counts, 0), axis=1, keepdims=True)
    slots = (iota((64, 128), 0) & 1) * 128 + iota((64, 128), 1)
    shi_ref[...] = jnp.where(slots < limit, row, -1)
    slo_ref[...] = lane


def face_lists(tables_f, axial_ref, coded_ref, fhi_ref, flo_ref):
    for g in range(4):
        put_rows(coded_ref, 8 * g, look_up(tables_f[g // 2], axial_ref[0, g // 2 : g // 2 + 1, lanes_of(g % 2)]))
    row, lane = decode(coded_ref[...], 32)
    fhi_ref[...] = row
    flo_ref[...] = lane


def first_kernel(*refs):
    (conn_h, peer_h, slot_h, node_h, counts_h, axial_h, pressure_h, geom_h, fwd_h, bwd_h, coef_h) = refs[:11]
    later_h = refs[11:17]
    (msg_ref, up_ref, down_ref, w_ref, shi_ref, fhi_ref, slo_ref, flo_ref, perm_ref, back_ref) = refs[17:27]
    (tab_f_ref, tab_b_ref, coef_ref, pressure_ref, geom_ref) = refs[27:32]
    later = refs[32:38]
    (conn_ref, peer_ref, slot_ref, node_ref, counts_ref, axial_ref, fwd_ref, bwd_ref, coded_ref, slow_ref, flow_ref, sems) = (
        refs[38:]
    )
    pairs = [
        (conn_h, conn_ref), (pressure_h, pressure_ref), (fwd_h, fwd_ref), (bwd_h, bwd_ref), (coef_h, coef_ref),
        (geom_h, geom_ref), (node_h, node_ref), (peer_h, peer_ref), (slot_h, slot_ref), (counts_h, counts_ref),
        (axial_h, axial_ref), *zip(later_h, later),
    ]
    copies = [pltpu.make_async_copy(src, dst, sems.at[at]) for at, (src, dst) in enumerate(pairs)]
    for copy in copies[:11]:
        copy.start()
    copies[0].wait()
    for copy in copies[11:]:
        copy.start()
    conn = conn_ref[...]
    build_perm(conn, perm_ref, back_ref)
    for copy in copies[1:11]:
        copy.wait()
    fh, fm, fl = split(fwd_ref[...], 3)
    for at, part in enumerate([fh, fh, fm, fm, fl, fh]):
        tab_f_ref[128 * at : 128 * at + 128, :] = part
    for at, part in enumerate(split(bwd_ref[...], 3)):
        tab_b_ref[256 * at : 256 * at + 256, :] = part
    table_s, tables_f = node_places(conn, perm_ref[:, 0:64])
    out = laplace(chunks_of(pressure_ref[...]), geom_ref, tab_f_ref, tab_b_ref, coef_ref)
    w = permute(perm_ref[...], out)
    for c in range(4):
        w_ref[:, 128 * c : 128 * c + 128] = w[c]
    side_lists(table_s, peer_ref, slot_ref, node_ref, counts_ref[...], shi_ref, slo_ref)
    face_lists(tables_f, axial_ref, coded_ref, fhi_ref, flo_ref)
    build_lows(slo_ref, flo_ref, slow_ref, flow_ref)
    send_values([assemble_local(w)], shi_ref, fhi_ref, slow_ref, flow_ref, msg_ref, up_ref, down_ref, 2)
    for copy in copies[11:]:
        copy.wait()


def momentum_kernel(
    velocity_ref, force_ref, mass_ref, metric_ref, geom_ref, tab_f_ref, tab_b_ref, coef_ref, perm_ref, shi_ref, fhi_ref,
    slo_ref, flo_ref,
    msg_ref, up_ref, down_ref, w_ref,
    slow_ref, flow_ref,
):
    build_lows(slo_ref, flo_ref, slow_ref, flow_ref)
    parts = [chunks_of(velocity_ref[a]) for a in range(3)]
    stacked = [jnp.concatenate([parts[a][c] for a in range(3)], axis=0) for c in range(4)]
    grad = grads(stacked, tab_f_ref, coef_ref)
    same = iota((64, 64), 0) == iota((64, 64), 1)
    scale = [jnp.sum(jnp.where(same, metric_ref[a : a + 1, :], 0.0), axis=1, keepdims=True) for a in range(3)]
    convect = []
    flux = [[], [], []]
    for c in range(4):
        total = None
        for a in range(3):
            speed = tiled(scale[a] * parts[a][c], 3)
            term = speed * grad[a][c]
            total = term if total is None else total + term
            flux[a].append(tiled(geom_ref[a, :, 128 * c : 128 * c + 128], 3) * grad[a][c])
        convect.append(total)
    diffuse = divergence(flux[0], flux[1], flux[2], tab_b_ref, coef_ref)
    fields = []
    for f in range(3):
        rows = slice(64 * f, 64 * f + 64)
        out = []
        for c in range(4):
            lanes = slice(128 * c, 128 * c + 128)
            out.append(
                mass_ref[:, lanes] * (force_ref[f, :, lanes] - convect[c][rows]) - VISCOSITY * diffuse[c][rows]
            )
        w = permute(perm_ref[...], out)
        for c in range(4):
            w_ref[f, :, 128 * c : 128 * c + 128] = w[c]
        fields.append(assemble_local(w))
    send_values(fields, shi_ref, fhi_ref, slow_ref, flow_ref, msg_ref, up_ref, down_ref, 6)


def second_kernel(
    msg_in_ref, low_ref, upp_ref, w_in_ref, pressure_ref, rhs_ref, jacobi_ref, geom_ref, tab_f_ref, tab_b_ref, coef_ref,
    perm_ref, back_ref, shi_ref, fhi_ref, slo_ref, flo_ref, msg_m_ref, up_m_ref, down_m_ref,
    msg_ref, up_ref, down_ref, w_ref, base_ref, res_ref,
    slow_ref, flow_ref,
):
    build_lows(slo_ref, flo_ref, slow_ref, flow_ref)
    sides = take_sides(1, shi_ref, slow_ref, msg_in_ref, 2)
    faces = take_faces(1, fhi_ref, flow_ref, low_ref, upp_ref)
    w = add_sides(add_faces(chunks_of(w_in_ref[...]), faces[0]), sides[0])
    applied = permute(back_ref[...], assemble_local(w))
    step = []
    for c in range(4):
        lanes = slice(128 * c, 128 * c + 128)
        jac = jacobi_ref[:, lanes]
        res = rhs_ref[:, lanes] - applied[c]
        step.append(jac * res / CHEB_THETA)
        first = pressure_ref[:, lanes] + step[c]
        base_ref[:, lanes] = first + RHO_NEXT * RHO_FIRST * step[c]
        res_ref[:, lanes] = res
    out = laplace(step, geom_ref, tab_f_ref, tab_b_ref, coef_ref)
    w = permute(perm_ref[...], out)
    for c in range(4):
        w_ref[:, 128 * c : 128 * c + 128] = w[c]
    send_values([assemble_local(w)], shi_ref, fhi_ref, slow_ref, flow_ref, msg_ref, up_ref, down_ref, 8)
    for peer in range(32):
        msg_ref[8 * peer + 2 : 8 * peer + 8, :] = msg_m_ref[6 * peer : 6 * peer + 6, :]
    up_ref[16:64, :] = up_m_ref[...]
    down_ref[16:64, :] = down_m_ref[...]


def faces_kernel(low_ref, upp_ref, w_in_ref, w_m_ref, fhi_ref, flo_ref, held_ref, flow_ref):
    build_low(flo_ref, flow_ref)
    faces = take_faces(4, fhi_ref, flow_ref, low_ref, upp_ref)
    for f in range(4):
        w = w_in_ref[...] if f == 0 else w_m_ref[f - 1]
        w = assemble_local(add_faces(chunks_of(w), faces[f]))
        for c in range(4):
            held_ref[f, :, 128 * c : 128 * c + 128] = w[c]


def last_kernel(
    msg_in_ref, held_ref, jacobi_ref, base_ref, res_ref, back_ref, shi_ref, slo_ref,
    pressure_h, momentum_h,
    out_ref, slow_ref, sems,
):
    build_low(slo_ref, slow_ref)
    sides = take_sides(4, shi_ref, slow_ref, msg_in_ref, 8)
    copies = []
    for f in range(4):
        applied = permute(back_ref[...], add_sides(chunks_of(held_ref[f]), on_all_copies(sides[f])))
        for c in range(4):
            lanes = slice(128 * c, 128 * c + 128)
            value = applied[c]
            if f == 0:
                value = base_ref[:, lanes] + 2.0 * RHO_NEXT / CHEB_DELTA * jacobi_ref[:, lanes] * (
                    res_ref[:, lanes] - value
                )
            out_ref[f, :, lanes] = value
        copy = pltpu.make_async_copy(out_ref.at[f], pressure_h if f == 0 else momentum_h.at[f - 1], sems.at[f])
        copy.start()
        copies.append(copy)
    for copy in copies:
        copy.wait()


def shape(*dims, dtype=F32):
    return jax.ShapeDtypeStruct(dims, dtype)


def in_vmem():
    return pl.BlockSpec(memory_space=pltpu.VMEM)


def in_hbm():
    return pl.BlockSpec(memory_space=pltpu.HBM)


def call(kernel, outs, args, scratch=(), name=None, args_hbm=False, outs_hbm=False):
    if args_hbm:
        args = [pltpu.with_memory_space_constraint(x, pltpu.HBM) for x in args]
    return pl.pallas_call(
        kernel,
        out_shape=outs,
        in_specs=[in_hbm() if args_hbm else in_vmem() for _ in args],
        out_specs=[in_hbm() if outs_hbm else in_vmem() for _ in outs],
        scratch_shapes=list(scratch),
        compiler_params=pltpu.CompilerParams(vmem_limit_bytes=VMEM_LIMIT),
        name=name,
    )(*args)


def lows():
    return [pltpu.VMEM((128, 8192), BF16), pltpu.VMEM((128, 4096), BF16)]


def like(x):
    return jax.ShapeDtypeStruct(x.shape, x.dtype)


def run_first(conn, peer, slot, node, counts, axial, pressure, geom, later):
    fwd, bwd, coef = [jnp.asarray(t) for t in const_tables()]
    held = [conn, peer, slot, node, counts, axial, fwd, bwd]
    outs = call(
        first_kernel,
        [shape(64, 128), shape(16, 128), shape(16, 128), shape(64, 512), shape(64, 128, dtype=I32),
         shape(32, 128, dtype=I32), shape(64, 128, dtype=I32), shape(32, 128, dtype=I32),
         shape(64, 192, dtype=BF16), shape(64, 192, dtype=BF16), shape(768, 256, dtype=BF16), shape(768, 128, dtype=BF16),
         like(coef), like(pressure), like(geom), *[like(x) for x in later]],
        [conn, peer, slot, node, counts, axial, pressure, geom, fwd, bwd, coef, *later],
        [*[pltpu.VMEM(x.shape, x.dtype) for x in held], pltpu.VMEM((32, 128), F32), *lows(),
         pltpu.SemaphoreType.DMA((11 + len(later),))],
        "first",
        args_hbm=True,
    )
    return outs[:4], outs[4:8], outs[8:10], outs[10:13], outs[13:15], outs[15:]


def run_momentum(velocity, force, mass, metric, geom, tables, perm, lists):
    return call(
        momentum_kernel,
        [shape(192, 128), shape(48, 128), shape(48, 128), shape(3, 64, 512)],
        [velocity, force, mass, metric, geom, *tables, perm, *lists],
        lows(),
        name="momentum",
    )


def run_second(msg, low, upp, w, pressure, rhs, jacobi, geom, tables, perm, back, lists, msg_m, up_m, down_m):
    return call(
        second_kernel,
        [shape(256, 128), shape(64, 128), shape(64, 128), shape(64, 512), shape(64, 512), shape(64, 512)],
        [msg, low, upp, w, pressure, rhs, jacobi, geom, *tables, perm, back, *lists, msg_m, up_m, down_m],
        lows(),
        name="second",
    )


def run_faces(low, upp, w, w_m, lists):
    (held,) = call(
        faces_kernel,
        [shape(4, 64, 512)],
        [low, upp, w, w_m, lists[1], lists[3]],
        [pltpu.VMEM((128, 4096), BF16)],
        name="faces",
    )
    return held


def run_last(msg, held, jacobi, base, res, back, lists):
    return call(
        last_kernel,
        [shape(64, 512), shape(3, 64, 512)],
        [msg, held, jacobi, base, res, back, lists[0], lists[2]],
        [pltpu.VMEM((4, 64, 512), F32), pltpu.VMEM((128, 8192), BF16), pltpu.SemaphoreType.DMA((4,))],
        name="last",
        outs_hbm=True,
    )


def exchange(msg, up, down):
    rows = msg.shape[0] // 32
    arrived = lax.all_to_all(msg.reshape(32, rows, 128), ("gy", "gz"), split_axis=0, concat_axis=0, tiled=True)
    count = lax.axis_size("gx")
    from_low = lax.ppermute(up, "gx", [(i, (i + 1) % count) for i in range(count)])
    from_upp = lax.ppermute(down, "gx", [((i + 1) % count, i) for i in range(count)])
    return arrived.reshape(32 * rows, 128), from_low, from_upp


def on_device(
    pressure, rhs, jacobi, geom, velocity, force, mass, metric, conn, ent_peer, ent_slot, ent_node, counts, axial_nodes
):
    sent, lists, (perm, back), tables, (pressure, geom), later = run_first(
        conn, ent_peer, ent_slot, ent_node, counts, axial_nodes, pressure, geom,
        [velocity, force, mass, metric, rhs, jacobi],
    )
    velocity, force, mass, metric, rhs, jacobi = later
    msg, up, down, w = sent
    got = exchange(msg, up, down)
    msg_m, up_m, down_m, w_m = run_momentum(velocity, force, mass, metric, geom, tables, perm, lists)
    msg, up, down, w, base, res = run_second(
        *got, w, pressure, rhs, jacobi, geom, tables, perm, back, lists, msg_m, up_m, down_m
    )
    msg, low, upp = exchange(msg, up, down)
    held = run_faces(low, upp, w, w_m, lists)
    return tuple(run_last(msg, held, jacobi, base, res, back, lists))


def solution(mesh):
    both = P(("gx", "gy", "gz"), None)
    three = P(None, ("gx", "gy", "gz"), None)
    return jax.shard_map(
        on_device,
        mesh=mesh,
        in_specs=(
            both, both, both, three, three, three, both, P(None, ("gx", "gy", "gz")), both, both, both, both, both,
            P(("gx", "gy", "gz"), None, None),
        ),
        out_specs=(both, three),
        check_vma=False,
    )
```

```python
import jax
import jax.numpy as jnp
import numpy as np
from jax import lax
from jax.experimental import pallas as pl
from jax.experimental.pallas import tpu as pltpu
from jax.sharding import PartitionSpec as P

F32 = jnp.float32
BF16 = jnp.bfloat16
I32 = jnp.int32

VISCOSITY = 0.2
CHEB_THETA = 1.1
CHEB_DELTA = 0.9
RHO_FIRST = 9.0 / 11.0
RHO_NEXT = 99.0 / 161.0

HI = 208
VMEM_LIMIT = 48 * 1024 * 1024


def deriv_table():
    points = np.array(
        [
            -1.0,
            -0.8717401485096066,
            -0.5917001814331423,
            -0.2092992179024789,
            0.2092992179024789,
            0.5917001814331423,
            0.8717401485096066,
            1.0,
        ]
    )
    before = np.ones(8)
    legendre = points.copy()
    for degree in range(1, 7):
        after = ((2 * degree + 1) * points * legendre - degree * before) / (degree + 1)
        before = legendre
        legendre = after
    spread = points[:, None] - points[None, :]
    safe = np.where(spread == 0.0, 1.0, spread)
    deriv = legendre[:, None] / (legendre[None, :] * safe)
    deriv = np.where(spread == 0.0, 0.0, deriv)
    deriv[0, 0] = -14.0
    deriv[7, 7] = 14.0
    return deriv


def const_tables():
    d32 = deriv_table().astype(np.float32)
    along_j = np.kron(np.eye(2), np.kron(d32, np.eye(8))).astype(np.float32)
    along_k = np.kron(np.eye(16), d32).astype(np.float32)
    fwd = np.concatenate([along_j.T, along_k.T], axis=1)
    bwd = np.concatenate([along_j, along_k], axis=0)
    coef = np.zeros((64, 128), np.float32)
    for way, mat in enumerate((d32, d32.T)):
        for to in range(4):
            for src in range(4):
                for half in range(2):
                    lanes = slice(64 * half, 64 * half + 64)
                    row = way * 32 + (to * 4 + src) * 2
                    coef[row, lanes] = mat[2 * to + half, 2 * src + half]
                    coef[row + 1, lanes] = mat[2 * to + half, 2 * src + 1 - half]
    return fwd, bwd, coef


def iota(shape, dim):
    return lax.broadcasted_iota(I32, shape, dim)


def split(x, count):
    parts = []
    for at in range(count):
        part = x.astype(BF16)
        parts.append(part)
        if at + 1 < count:
            x = x - part.astype(F32)
    return parts


def dot(a, b):
    return lax.dot_general(a, b, (((1,), (0,)), ((), ())), preferred_element_type=F32)


def dot_nt(a, b):
    return lax.dot_general(a, b, (((1,), (1,)), ((), ())), preferred_element_type=F32)


def repeat_row(row, count):
    pair = jnp.broadcast_to(row.astype(F32), (16, row.shape[1])).astype(BF16)
    return jnp.concatenate([pair] * (count // 16), axis=0)


def marks(row, count):
    base = iota((count, 128), 0).astype(F32).astype(BF16)
    return jnp.concatenate([base] * (row.shape[1] // 128), axis=1) == repeat_row(row, count)


def choose(mask, value):
    return jnp.where(mask, value, jnp.zeros(mask.shape, BF16))


def one_hot(row, count):
    return choose(marks(row, count), jnp.ones((count, row.shape[1]), BF16))


def chunks_of(x):
    return [x[:, 128 * c : 128 * c + 128] for c in range(4)]


def along_i(chunks, coef_ref, way):
    turned = [pltpu.roll(x, 64, 1) for x in chunks]
    out = []
    for to in range(4):
        total = None
        for src in range(4):
            row = way * 32 + (to * 4 + src) * 2
            term = coef_ref[row : row + 1, :] * chunks[src] + coef_ref[row + 1 : row + 2, :] * turned[src]
            total = term if total is None else total + term
        out.append(total)
    return out


def grads(chunks, tab_f_ref, coef_ref):
    rows = chunks[0].shape[0]
    g_i = along_i(chunks, coef_ref, 0)
    h, m, l = split(jnp.concatenate(chunks, axis=0), 3)
    hm = jnp.concatenate([h, m], axis=1)
    hl = jnp.concatenate([h, l], axis=1)
    g_jk = dot(hm, tab_f_ref[0:256, :]) + (dot(hm, tab_f_ref[256:512, :]) + dot(hl, tab_f_ref[512:768, :]))
    g_j = [g_jk[rows * c : rows * c + rows, 0:128] for c in range(4)]
    g_k = [g_jk[rows * c : rows * c + rows, 128:256] for c in range(4)]
    return g_i, g_j, g_k


def divergence(u_i, u_j, u_k, tab_b_ref, coef_ref):
    rows = u_i[0].shape[0]
    out_i = along_i(u_i, coef_ref, 1)
    u = jnp.concatenate([jnp.concatenate(u_j, axis=0), jnp.concatenate(u_k, axis=0)], axis=1)
    h, m, l = split(u, 3)
    b_h = tab_b_ref[0:256, :]
    b_m = tab_b_ref[256:512, :]
    b_l = tab_b_ref[512:768, :]
    wide = jnp.concatenate([b_h, b_m], axis=1)
    both = dot(h, wide) + dot(m, wide)
    small = dot(h, b_l) + dot(l, b_h)
    total = both[:, 0:128] + (both[:, 128:256] + small)
    return [out_i[c] + total[rows * c : rows * c + rows] for c in range(4)]


def tiled(x, times):
    return x if times == 1 else jnp.concatenate([x] * times, axis=0)


def laplace(chunks, geom_ref, tab_f_ref, tab_b_ref, coef_ref):
    g_i, g_j, g_k = grads(chunks, tab_f_ref, coef_ref)
    geom = [chunks_of(geom_ref[a]) for a in range(3)]
    return divergence(
        [geom[0][c] * g_i[c] for c in range(4)],
        [geom[1][c] * g_j[c] for c in range(4)],
        [geom[2][c] * g_k[c] for c in range(4)],
        tab_b_ref,
        coef_ref,
    )


def permute(perm, chunks):
    parts = split(jnp.concatenate(chunks, axis=1), 3)
    return chunks_of(dot(perm, jnp.concatenate(parts, axis=0)))


def assemble_local(w):
    lane = iota((64, 128), 1)
    row = iota((64, 128), 0)
    bx = row & 7
    jj = (lane >> 3) & 7
    w = list(w)
    low = pltpu.roll(pltpu.roll(w[0], 64, 1), 63, 0)
    high = pltpu.roll(pltpu.roll(w[3], 64, 1), 1, 0)
    w[3] = w[3] + jnp.where((lane >= 64) & (bx < 7), low, 0.0)
    w[0] = w[0] + jnp.where((lane < 64) & (bx > 0), high, 0.0)
    out = []
    zero = jnp.zeros((8, 128), F32)
    for x in w:
        nxt = jnp.concatenate([pltpu.roll(x[8:64], 56, 1), zero], axis=0)
        prv = jnp.concatenate([zero, pltpu.roll(x[0:56], 72, 1)], axis=0)
        out.append(x + jnp.where(jj == 7, nxt, 0.0) + jnp.where(jj == 0, prv, 0.0))
    return out


def pack_sides(w):
    lane1 = iota((1, 128), 1)
    rows = [
        jnp.where(lane1 < 64, w[0][8 * by : 8 * by + 1], w[3][8 * by + 7 : 8 * by + 8]) for by in range(8)
    ]
    x_side = jnp.concatenate(rows, axis=0)
    jj = (iota((8, 128), 1) >> 3) & 7
    y_side = jnp.zeros((8, 128), F32)
    for c in range(4):
        y_side = jnp.where(jj == 2 * c, pltpu.roll(w[c][0:8], 16 * c, 1), y_side)
        y_side = jnp.where(jj == 2 * c + 1, pltpu.roll(w[c][56:64], (16 * c - 48) % 128, 1), y_side)
    return jnp.concatenate([x_side, y_side], axis=0)


def pack_faces(w):
    kk = iota((32, 128), 1) & 7
    faces = []
    for k in (0, 7):
        face = jnp.zeros((32, 128), F32)
        for c in range(4):
            for h in range(2):
                face = jnp.where(
                    kk == 4 * h + c, pltpu.roll(w[c][32 * h : 32 * h + 32], (4 * h + c - k) % 128, 1), face
                )
        faces.append(face)
    return faces


def add_faces(w, face):
    kk = iota((64, 128), 1) & 7
    out = []
    for c in range(4):
        x = w[c]
        for k, part in zip((0, 7), face):
            spread = [pltpu.roll(part, (k - 4 * h - c) % 128, 1) for h in range(2)]
            x = x + jnp.where(kk == k, jnp.concatenate(spread, axis=0), 0.0)
        out.append(x)
    return out


def add_sides(w, side):
    lane = iota((64, 128), 1)
    sub = iota((64, 128), 0) & 7
    jj = (iota((8, 128), 1) >> 3) & 7
    x_rows = jnp.concatenate(
        [jnp.broadcast_to(side[by : by + 1], (8, 128)) for by in range(8)], axis=0
    )
    y_side = side[8:16]
    out = []
    for c in range(4):
        x = w[c]
        if c == 0:
            x = x + jnp.where((sub == 0) & (lane < 64), x_rows, 0.0)
        if c == 3:
            x = x + jnp.where((sub == 7) & (lane >= 64), x_rows, 0.0)
        first = x[0:8] + jnp.where(jj == 0, pltpu.roll(y_side, (-16 * c) % 128, 1), 0.0)
        last = x[56:64] + jnp.where(jj == 7, pltpu.roll(y_side, (48 - 16 * c) % 128, 1), 0.0)
        out.append(jnp.concatenate([first, x[8:56], last], axis=0))
    return out


def on_all_copies(side):
    lane = iota((8, 128), 1)
    row = iota((8, 128), 0)
    x_side, y_side = side[0:8], side[8:16]
    x_next = pltpu.roll(pltpu.roll(x_side, 56, 1), 7, 0)
    y_next = pltpu.roll(pltpu.roll(y_side, 112, 1), 7, 0)
    x_side = jnp.where((((lane >> 3) & 7) == 7) & (row < 7), x_next, x_side)
    y_side = jnp.where((lane >= 112) & (row < 7), y_next, y_side)
    return jnp.concatenate([x_side, y_side], axis=0)


def block_row(block):
    return jnp.concatenate([block[t : t + 1] for t in range(8)], axis=1)


def gather_tables(tables, hi_block, lows, hi_count):
    parts = []
    for table in tables:
        parts += split(table, 2)
    got = dot(jnp.concatenate(parts, axis=0), lows)
    mask = iota((hi_count, 1024), 0) == block_row(hi_block)
    out = []
    for at in range(len(tables)):
        both = got[2 * at * hi_count : (2 * at + 1) * hi_count] + got[(2 * at + 1) * hi_count : (2 * at + 2) * hi_count]
        out.append(jnp.sum(jnp.where(mask, both, 0.0), axis=0, keepdims=True))
    return out


def scatter_tables(rows, hi_block, lows, hi_count):
    mask = marks(block_row(hi_block), hi_count)
    parts = []
    for values in rows:
        for part in split(values, 2):
            parts.append(choose(mask, repeat_row(part, hi_count)))
    parts = jnp.concatenate(parts, axis=0)
    return dot_nt(lows, parts) if hi_count == 16 else dot_nt(parts, lows)


def build_low(lo_ref, low_ref):
    for g in range(lo_ref.shape[0] // 8):
        low_ref[:, lanes_of(g)] = one_hot(block_row(lo_ref[rows_of(g), :]), 128)


def build_lows(slo_ref, flo_ref, slow_ref, flow_ref):
    build_low(slo_ref, slow_ref)
    build_low(flo_ref, flow_ref)


def lanes_of(g):
    return slice(1024 * g, 1024 * g + 1024)


def rows_of(g):
    return slice(8 * g, 8 * g + 8)


def send_values(local_fields, shi_ref, fhi_ref, slow_ref, flow_ref, msg_ref, up_ref, down_ref, stride):
    sides = [pack_sides(w) for w in local_fields]
    faces = [pack_faces(w) for w in local_fields]
    for g in range(8):
        got = gather_tables(sides, shi_ref[rows_of(g), :], slow_ref[:, lanes_of(g)], 16)
        for f, values in enumerate(got):
            for t in range(8):
                at = (8 * g + t) // 2 * stride + 2 * f + t % 2
                msg_ref[at : at + 1, :] = values[:, 128 * t : 128 * t + 128]
    for g in range(4):
        got = gather_tables([f[g // 2] for f in faces], fhi_ref[rows_of(g), :], flow_ref[:, lanes_of(g)], 32)
        out_ref = down_ref if g < 2 else up_ref
        for f, values in enumerate(got):
            for t in range(8):
                at = 16 * f + 8 * (g % 2) + t
                out_ref[at : at + 1, :] = values[:, 128 * t : 128 * t + 128]


def take_sides(count, shi_ref, slow_ref, msg_ref, stride):
    side = None
    for g in range(8):
        rows = []
        for f in range(count):
            cells = []
            for t in range(8):
                at = (8 * g + t) // 2 * stride + 2 * f + t % 2
                cells.append(msg_ref[at : at + 1, :])
            rows.append(jnp.concatenate(cells, axis=1))
        part = scatter_tables(rows, shi_ref[rows_of(g), :], slow_ref[:, lanes_of(g)], 16)
        side = part if side is None else side + part
    side = side.T
    return [side[32 * f : 32 * f + 16] + side[32 * f + 16 : 32 * f + 32] for f in range(count)]


def take_faces(count, fhi_ref, flow_ref, low_ref, upp_ref):
    face = [None, None]
    for g in range(4):
        ref = low_ref if g < 2 else upp_ref
        rows = [block_row(ref[16 * f + 8 * (g % 2) : 16 * f + 8 * (g % 2) + 8, :]) for f in range(count)]
        part = scatter_tables(rows, fhi_ref[rows_of(g), :], flow_ref[:, lanes_of(g)], 32)
        face[g // 2] = part if face[g // 2] is None else face[g // 2] + part
    return [[x[64 * f : 64 * f + 32] + x[64 * f + 32 : 64 * f + 64] for x in face] for f in range(count)]


def chain_place(left):
    eye = (iota((64, 64), 0) == iota((64, 64), 1)).astype(F32)
    l1 = left.astype(BF16)
    l2 = dot(l1, l1)
    m1 = eye + left
    l2b = l2.astype(BF16)
    l4 = dot(l2b, l2b)
    m2 = m1 + dot(l2b, m1.astype(BF16))
    m4 = m2 + dot(l4.astype(BF16), m2.astype(BF16))
    return jnp.sum(m4, axis=1, keepdims=True) - 1.0


def brick_places(conn):
    same = iota((64, 64), 0) == iota((64, 64), 1)

    def as_row(col):
        return jnp.sum(jnp.where(same, col, 0), axis=0, keepdims=True)

    end_x = as_row(conn[:, 475:476])
    end_y = as_row(conn[:, 251:252])
    left_x = (conn[:, 27:28] == end_x).astype(F32)
    left_y = (conn[:, 195:196] == end_y).astype(F32)
    return (chain_place(left_y) * 8.0 + chain_place(left_x)).astype(I32)


def place_table(hi, lo, count):
    lane = 1.0 + iota((1, 128), 1).astype(F32) * (1.0 / 128.0)
    total = None
    for g in range(count // 8):
        top = one_hot(block_row(hi[rows_of(g)]), HI)
        low = []
        for t in range(8):
            hit = marks(lo[8 * g + t : 8 * g + t + 1], 128)
            low.append(choose(hit, repeat_row(lane * (2.0 ** (8 * g + t - count // 2)), 128)))
        part = dot_nt(jnp.concatenate(low, axis=1), top)
        total = part if total is None else total + part
    return total.astype(BF16)


def look_up(table, row):
    got = choose(marks(row & 127, 128), dot(table, one_hot(row >> 7, HI)).astype(BF16))
    total = got[0:16]
    for at in range(1, 8):
        total = total + got[16 * at : 16 * at + 16]
    return jnp.sum(total.astype(F32), axis=0, keepdims=True)


def decode(x, count):
    x = x * (2.0 ** (count // 2))
    row = jnp.zeros(x.shape, I32)
    jump = count // 2
    while jump:
        big = x >= 2.0**jump
        row = row + jnp.where(big, jump, 0)
        x = jnp.where(big, x * (2.0**-jump), x)
        jump //= 2
    return row, (x * 128.0).astype(I32) - 128


def put_rows(ref, at, values):
    for t in range(8):
        ref[at + t : at + t + 1, :] = values[:, 128 * t : 128 * t + 128]


def build_perm(conn, perm_ref, back_ref):
    place = brick_places(conn)
    lane3 = iota((64, 192), 1) & 63
    place_row = jnp.sum(jnp.where(lane3 == iota((64, 192), 0), place, 0), axis=0, keepdims=True)
    perm_ref[...] = (iota((64, 192), 0) == place_row).astype(F32).astype(BF16)
    back_ref[...] = (lane3 == place).astype(F32).astype(BF16)


def node_places(conn, perm):
    ids = jnp.concatenate([(conn >> 7).astype(F32), (conn & 127).astype(F32)], axis=1).astype(BF16)
    ids = dot(perm, ids)
    hi_c = chunks_of(ids[:, 0:512])
    lo_c = chunks_of(ids[:, 512:1024])
    lane8 = iota((16, 128), 1)
    row8 = iota((16, 128), 0)
    in_x = (((lane8 >> 3) & 7) < 7) | (row8 == 7)
    i_y = 2 * (((lane8 >> 3) & 7) >> 1) + (lane8 >> 6)
    in_y = (i_y < 7) & ((row8 > 8) | (i_y > 0))
    keep_s = ((row8 < 8) & in_x) | ((row8 >= 8) & in_y)
    lane = iota((32, 128), 1)
    row = iota((32, 128), 0) + 32 * ((lane >> 2) & 1)
    i_f = 2 * (lane & 3) + (lane >> 6)
    keep_f = ((i_f < 7) | ((row & 7) == 7)) & ((((lane >> 3) & 7) < 7) | ((row >> 3) == 7))
    table_s = place_table(
        jnp.where(keep_s, pack_sides(hi_c), -1.0).astype(I32), pack_sides(lo_c).astype(I32), 16
    )
    tables_f = [
        place_table(jnp.where(keep_f, hi, -1.0).astype(I32), lo.astype(I32), 32)
        for hi, lo in zip(pack_faces(hi_c), pack_faces(lo_c))
    ]
    return table_s, tables_f


def side_lists(table_s, peer_ref, slot_ref, node_ref, counts, shi_ref, slo_ref):
    total = None
    for g in range(8):
        at = lanes_of(g)
        slot = slot_ref[:, at]
        places = look_up(table_s, node_ref[:, at])
        hit = marks(peer_ref[:, at] * 2 + (slot >> 7), 64)
        part = dot_nt(one_hot(slot & 127, 128), choose(hit, repeat_row(places, 64)))
        total = part if total is None else total + part
    row, lane = decode(total.T, 16)
    limit = jnp.sum(jnp.where(iota((64, 32), 1) == (iota((64, 32), 0) >> 1), counts, 0), axis=1, keepdims=True)
    slots = (iota((64, 128), 0) & 1) * 128 + iota((64, 128), 1)
    shi_ref[...] = jnp.where(slots < limit, row, -1)
    slo_ref[...] = lane


def face_lists(tables_f, axial_ref, coded_ref, fhi_ref, flo_ref):
    for g in range(4):
        put_rows(coded_ref, 8 * g, look_up(tables_f[g // 2], axial_ref[0, g // 2 : g // 2 + 1, lanes_of(g % 2)]))
    row, lane = decode(coded_ref[...], 32)
    fhi_ref[...] = row
    flo_ref[...] = lane


def first_kernel(*refs):
    (conn_h, peer_h, slot_h, node_h, counts_h, axial_h, pressure_h, geom_h, fwd_h, bwd_h, coef_h) = refs[:11]
    later_h = refs[11:17]
    (msg_ref, up_ref, down_ref, w_ref, shi_ref, fhi_ref, slo_ref, flo_ref, perm_ref, back_ref) = refs[17:27]
    (tab_f_ref, tab_b_ref, coef_ref, pressure_ref, geom_ref) = refs[27:32]
    later = refs[32:38]
    (conn_ref, peer_ref, slot_ref, node_ref, counts_ref, axial_ref, fwd_ref, bwd_ref, coded_ref, slow_ref, flow_ref, sems) = (
        refs[38:]
    )
    pairs = [
        (conn_h, conn_ref), (pressure_h, pressure_ref), (fwd_h, fwd_ref), (bwd_h, bwd_ref), (coef_h, coef_ref),
        (geom_h, geom_ref), (node_h, node_ref), (peer_h, peer_ref), (slot_h, slot_ref), (counts_h, counts_ref),
        (axial_h, axial_ref), *zip(later_h, later),
    ]
    copies = [pltpu.make_async_copy(src, dst, sems.at[at]) for at, (src, dst) in enumerate(pairs)]
    for copy in copies[:11]:
        copy.start()
    copies[0].wait()
    for copy in copies[11:]:
        copy.start()
    conn = conn_ref[...]
    build_perm(conn, perm_ref, back_ref)
    for copy in copies[1:11]:
        copy.wait()
    fh, fm, fl = split(fwd_ref[...], 3)
    for at, part in enumerate([fh, fh, fm, fm, fl, fh]):
        tab_f_ref[128 * at : 128 * at + 128, :] = part
    for at, part in enumerate(split(bwd_ref[...], 3)):
        tab_b_ref[256 * at : 256 * at + 256, :] = part
    table_s, tables_f = node_places(conn, perm_ref[:, 0:64])
    out = laplace(chunks_of(pressure_ref[...]), geom_ref, tab_f_ref, tab_b_ref, coef_ref)
    w = permute(perm_ref[...], out)
    for c in range(4):
        w_ref[:, 128 * c : 128 * c + 128] = w[c]
    side_lists(table_s, peer_ref, slot_ref, node_ref, counts_ref[...], shi_ref, slo_ref)
    face_lists(tables_f, axial_ref, coded_ref, fhi_ref, flo_ref)
    build_lows(slo_ref, flo_ref, slow_ref, flow_ref)
    send_values([assemble_local(w)], shi_ref, fhi_ref, slow_ref, flow_ref, msg_ref, up_ref, down_ref, 2)
    for copy in copies[11:]:
        copy.wait()


def momentum_kernel(
    velocity_ref, force_ref, mass_ref, metric_ref, geom_ref, tab_f_ref, tab_b_ref, coef_ref, perm_ref, shi_ref, fhi_ref,
    slo_ref, flo_ref,
    msg_ref, up_ref, down_ref, w_ref,
    slow_ref, flow_ref,
):
    build_lows(slo_ref, flo_ref, slow_ref, flow_ref)
    parts = [chunks_of(velocity_ref[a]) for a in range(3)]
    stacked = [jnp.concatenate([parts[a][c] for a in range(3)], axis=0) for c in range(4)]
    grad = grads(stacked, tab_f_ref, coef_ref)
    same = iota((64, 64), 0) == iota((64, 64), 1)
    scale = [jnp.sum(jnp.where(same, metric_ref[a : a + 1, :], 0.0), axis=1, keepdims=True) for a in range(3)]
    convect = []
    flux = [[], [], []]
    for c in range(4):
        total = None
        for a in range(3):
            speed = tiled(scale[a] * parts[a][c], 3)
            term = speed * grad[a][c]
            total = term if total is None else total + term
            flux[a].append(tiled(geom_ref[a, :, 128 * c : 128 * c + 128], 3) * grad[a][c])
        convect.append(total)
    diffuse = divergence(flux[0], flux[1], flux[2], tab_b_ref, coef_ref)
    fields = []
    for f in range(3):
        rows = slice(64 * f, 64 * f + 64)
        out = []
        for c in range(4):
            lanes = slice(128 * c, 128 * c + 128)
            out.append(
                mass_ref[:, lanes] * (force_ref[f, :, lanes] - convect[c][rows]) - VISCOSITY * diffuse[c][rows]
            )
        w = permute(perm_ref[...], out)
        for c in range(4):
            w_ref[f, :, 128 * c : 128 * c + 128] = w[c]
        fields.append(assemble_local(w))
    send_values(fields, shi_ref, fhi_ref, slow_ref, flow_ref, msg_ref, up_ref, down_ref, 6)


def second_kernel(
    msg_in_ref, low_ref, upp_ref, w_in_ref, pressure_ref, rhs_ref, jacobi_ref, geom_ref, tab_f_ref, tab_b_ref, coef_ref,
    perm_ref, back_ref, shi_ref, fhi_ref, slo_ref, flo_ref, msg_m_ref, up_m_ref, down_m_ref,
    msg_ref, up_ref, down_ref, w_ref, base_ref, res_ref,
    slow_ref, flow_ref,
):
    build_lows(slo_ref, flo_ref, slow_ref, flow_ref)
    sides = take_sides(1, shi_ref, slow_ref, msg_in_ref, 2)
    faces = take_faces(1, fhi_ref, flow_ref, low_ref, upp_ref)
    w = add_sides(add_faces(chunks_of(w_in_ref[...]), faces[0]), sides[0])
    applied = permute(back_ref[...], assemble_local(w))
    step = []
    for c in range(4):
        lanes = slice(128 * c, 128 * c + 128)
        jac = jacobi_ref[:, lanes]
        res = rhs_ref[:, lanes] - applied[c]
        step.append(jac * res / CHEB_THETA)
        first = pressure_ref[:, lanes] + step[c]
        base_ref[:, lanes] = first + RHO_NEXT * RHO_FIRST * step[c]
        res_ref[:, lanes] = res
    out = laplace(step, geom_ref, tab_f_ref, tab_b_ref, coef_ref)
    w = permute(perm_ref[...], out)
    for c in range(4):
        w_ref[:, 128 * c : 128 * c + 128] = w[c]
    send_values([assemble_local(w)], shi_ref, fhi_ref, slow_ref, flow_ref, msg_ref, up_ref, down_ref, 8)
    for peer in range(32):
        msg_ref[8 * peer + 2 : 8 * peer + 8, :] = msg_m_ref[6 * peer : 6 * peer + 6, :]
    up_ref[16:64, :] = up_m_ref[...]
    down_ref[16:64, :] = down_m_ref[...]


def faces_kernel(low_ref, upp_ref, w_in_ref, w_m_ref, fhi_ref, flo_ref, held_ref, flow_ref):
    build_low(flo_ref, flow_ref)
    faces = take_faces(4, fhi_ref, flow_ref, low_ref, upp_ref)
    for f in range(4):
        w = w_in_ref[...] if f == 0 else w_m_ref[f - 1]
        w = assemble_local(add_faces(chunks_of(w), faces[f]))
        for c in range(4):
            held_ref[f, :, 128 * c : 128 * c + 128] = w[c]


def last_kernel(
    msg_in_ref, held_ref, jacobi_ref, base_ref, res_ref, back_ref, shi_ref, slo_ref,
    pressure_h, momentum_h,
    out_ref, slow_ref, sems,
):
    build_low(slo_ref, slow_ref)
    sides = take_sides(4, shi_ref, slow_ref, msg_in_ref, 8)
    copies = []
    for f in range(4):
        applied = permute(back_ref[...], add_sides(chunks_of(held_ref[f]), on_all_copies(sides[f])))
        for c in range(4):
            lanes = slice(128 * c, 128 * c + 128)
            value = applied[c]
            if f == 0:
                value = base_ref[:, lanes] + 2.0 * RHO_NEXT / CHEB_DELTA * jacobi_ref[:, lanes] * (
                    res_ref[:, lanes] - value
                )
            out_ref[f, :, lanes] = value
        copy = pltpu.make_async_copy(out_ref.at[f], pressure_h if f == 0 else momentum_h.at[f - 1], sems.at[f])
        copy.start()
        copies.append(copy)
    for copy in copies:
        copy.wait()


def shape(*dims, dtype=F32):
    return jax.ShapeDtypeStruct(dims, dtype)


def in_vmem():
    return pl.BlockSpec(memory_space=pltpu.VMEM)


def in_hbm():
    return pl.BlockSpec(memory_space=pltpu.HBM)


def call(kernel, outs, args, scratch=(), name=None, args_hbm=False, outs_hbm=False):
    if args_hbm:
        args = [pltpu.with_memory_space_constraint(x, pltpu.HBM) for x in args]
    return pl.pallas_call(
        kernel,
        out_shape=outs,
        in_specs=[in_hbm() if args_hbm else in_vmem() for _ in args],
        out_specs=[in_hbm() if outs_hbm else in_vmem() for _ in outs],
        scratch_shapes=list(scratch),
        compiler_params=pltpu.CompilerParams(vmem_limit_bytes=VMEM_LIMIT),
        name=name,
    )(*args)


def lows():
    return [pltpu.VMEM((128, 8192), BF16), pltpu.VMEM((128, 4096), BF16)]


def like(x):
    return jax.ShapeDtypeStruct(x.shape, x.dtype)


def run_first(conn, peer, slot, node, counts, axial, pressure, geom, later):
    fwd, bwd, coef = [jnp.asarray(t) for t in const_tables()]
    held = [conn, peer, slot, node, counts, axial, fwd, bwd]
    outs = call(
        first_kernel,
        [shape(64, 128), shape(16, 128), shape(16, 128), shape(64, 512), shape(64, 128, dtype=I32),
         shape(32, 128, dtype=I32), shape(64, 128, dtype=I32), shape(32, 128, dtype=I32),
         shape(64, 192, dtype=BF16), shape(64, 192, dtype=BF16), shape(768, 256, dtype=BF16), shape(768, 128, dtype=BF16),
         like(coef), like(pressure), like(geom), *[like(x) for x in later]],
        [conn, peer, slot, node, counts, axial, pressure, geom, fwd, bwd, coef, *later],
        [*[pltpu.VMEM(x.shape, x.dtype) for x in held], pltpu.VMEM((32, 128), F32), *lows(),
         pltpu.SemaphoreType.DMA((11 + len(later),))],
        "first",
        args_hbm=True,
    )
    return outs[:4], outs[4:8], outs[8:10], outs[10:13], outs[13:15], outs[15:]


def run_momentum(velocity, force, mass, metric, geom, tables, perm, lists):
    return call(
        momentum_kernel,
        [shape(192, 128), shape(48, 128), shape(48, 128), shape(3, 64, 512)],
        [velocity, force, mass, metric, geom, *tables, perm, *lists],
        lows(),
        name="momentum",
    )


def run_second(msg, low, upp, w, pressure, rhs, jacobi, geom, tables, perm, back, lists, msg_m, up_m, down_m):
    return call(
        second_kernel,
        [shape(256, 128), shape(64, 128), shape(64, 128), shape(64, 512), shape(64, 512), shape(64, 512)],
        [msg, low, upp, w, pressure, rhs, jacobi, geom, *tables, perm, back, *lists, msg_m, up_m, down_m],
        lows(),
        name="second",
    )


def run_faces(low, upp, w, w_m, lists):
    (held,) = call(
        faces_kernel,
        [shape(4, 64, 512)],
        [low, upp, w, w_m, lists[1], lists[3]],
        [pltpu.VMEM((128, 4096), BF16)],
        name="faces",
    )
    return held


def run_last(msg, held, jacobi, base, res, back, lists):
    return call(
        last_kernel,
        [shape(64, 512), shape(3, 64, 512)],
        [msg, held, jacobi, base, res, back, lists[0], lists[2]],
        [pltpu.VMEM((4, 64, 512), F32), pltpu.VMEM((128, 8192), BF16), pltpu.SemaphoreType.DMA((4,))],
        name="last",
        outs_hbm=True,
    )


def exchange(msg, up, down):
    rows = msg.shape[0] // 32
    arrived = lax.all_to_all(msg.reshape(32, rows, 128), ("gy", "gz"), split_axis=0, concat_axis=0, tiled=True)
    count = lax.axis_size("gx")
    from_low = lax.ppermute(up, "gx", [(i, (i + 1) % count) for i in range(count)])
    from_upp = lax.ppermute(down, "gx", [((i + 1) % count, i) for i in range(count)])
    return arrived.reshape(32 * rows, 128), from_low, from_upp


def on_device(
    pressure, rhs, jacobi, geom, velocity, force, mass, metric, conn, ent_peer, ent_slot, ent_node, counts, axial_nodes
):
    sent, lists, (perm, back), tables, (pressure, geom), later = run_first(
        conn, ent_peer, ent_slot, ent_node, counts, axial_nodes, pressure, geom,
        [velocity, force, mass, metric, rhs, jacobi],
    )
    velocity, force, mass, metric, rhs, jacobi = later
    msg, up, down, w = sent
    got = exchange(msg, up, down)
    msg_m, up_m, down_m, w_m = run_momentum(velocity, force, mass, metric, geom, tables, perm, lists)
    msg, up, down, w, base, res = run_second(
        *got, w, pressure, rhs, jacobi, geom, tables, perm, back, lists, msg_m, up_m, down_m
    )
    msg, low, upp = exchange(msg, up, down)
    held = run_faces(low, upp, w, w_m, lists)
    return tuple(run_last(msg, held, jacobi, base, res, back, lists))


def solution(mesh):
    both = P(("gx", "gy", "gz"), None)
    three = P(None, ("gx", "gy", "gz"), None)
    return jax.shard_map(
        on_device,
        mesh=mesh,
        in_specs=(
            both, both, both, three, three, three, both, P(None, ("gx", "gy", "gz")), both, both, both, both, both,
            P(("gx", "gy", "gz"), None, None),
        ),
        out_specs=(both, three),
        check_vma=False,
    )
```
